32 devices in a mesh: wide: 8 (over z, x), narrow: 4 (over y, core).
Axes of the slice: x: 2, y: 2, z: 4, core: 2. Of those that a mesh axis runs over, the one named last changes fastest.
Arguments:
- tokens: bfloat16 [49152, 512], P(('wide', 'narrow')), may hold values from -6 to 6
- window_lengths: int32 [32, 6], P(('wide', 'narrow')), may hold values from 0 to 1024, as said below
- conv_weight: bfloat16 [9, 512, 512], P(None, 'wide', 'narrow'), may hold values from -0.09375 to 0.09375
- feedforward_input_weight: bfloat16 [512, 2048], P('wide', 'narrow'), may hold values from -0.25 to 0.25
- ffn_out: bfloat16 [2048, 512], P('wide', 'narrow'), may hold values from -0.125 to 0.125
- small_params: bfloat16 [5120], P(('wide', 'narrow')), may hold values from -1.25 to 1.625
- cotangent: bfloat16 [49152, 512], P(('wide', 'narrow')), may hold values from -6 to 6
Outputs:
- block_out: bfloat16 [49152, 512], P(('wide', 'narrow'))
- grad_tokens: float32 [49152, 512], P(('wide', 'narrow'))
- convolution_weight_gradient: float32 [9, 512, 512], P(None, 'wide', 'narrow')
- grad_ffn_in: float32 [512, 2048], P('wide', 'narrow')
- grad_ffn_out: float32 [2048, 512], P('wide', 'narrow')
- grad_small: float32 [5120], P(('wide', 'narrow'))
The draws below stay inside these ranges and needn't reach their ends.
Inputs may be any that keep to these rules, and one draw needn't show every extreme that they name: `window_lengths`: each row lists its device's window lengths in order, each 256, 512 or 1024, then zeros; the first is 1024 and their sum is at most 1536.
All inputs are finite; a program needn't handle non-finite values.
Results may differ from the reference program's by a relative error of at most 0.0064.
Values may be sent and summed in bfloat16 or wider, within the bound.
A program may use at most 192 MiB of HBM per device.

```python
import jax
import jax.numpy as jnp
from jax import lax

D = 512
FF = 2048
KERNEL_TAPS = 9
DILATION_STEP = 8
WIN_MIN = 256
TOK_DEV = 1536
SLOTS = 6
TOKENS = 49152
N_WIDE = 8
N_NARROW = 4


def draw_window_lengths(key, part):
    key = jax.random.fold_in(key, 5)
    first_key, second_key = jax.random.split(key)
    device_rows = N_WIDE * N_NARROW
    picks = jax.random.randint(first_key, (device_rows, SLOTS), 0, 3)
    lengths = jnp.where(picks == 0, WIN_MIN, jnp.where(picks == 1, 2 * WIN_MIN, 4 * WIN_MIN)).astype(jnp.int32)
    lengths = lengths.at[:, 0].set(4 * WIN_MIN)
    target = jax.random.randint(second_key, (device_rows, 1), TOK_DEV // 2, TOK_DEV + 1)
    target = jnp.maximum(target, 4 * WIN_MIN)
    running = jnp.cumsum(lengths, axis=1)
    return (lengths * (running <= target).astype(jnp.int32)).astype(jnp.int32)


def draw_small_params(key, part):
    key = jax.random.fold_in(key, 7)
    total = 6 * D + FF
    noise = jax.random.normal(key, (total,), jnp.float32)
    noise = jnp.clip(noise, -2.5, 2.5)
    places = jnp.arange(total)
    gain_selected = (places >= D) & (places < 2 * D) | (places >= 4 * D + FF) & (places < 5 * D + FF)
    is_shift = (places >= 2 * D) & (places < 3 * D) | (places >= 5 * D + FF)
    values = jnp.where(gain_selected, 1.0 + 0.25 * noise, jnp.where(is_shift, 0.3 * noise, 0.5 * noise))
    return values.astype(jnp.bfloat16)


def level_of(stream_key, extent, cuts, smallest, high):
    def one(dim, parts):
        steps = jax.random.uniform(jax.random.fold_in(jax.random.fold_in(stream_key, 6), dim), (parts,), jnp.float32, smallest / len(cuts), high / len(cuts))
        return jnp.repeat(jnp.exp(steps), extent[dim] // parts).reshape((-1,) + (1,) * (len(extent) - dim - 1))

    level = one(*cuts[0])
    for cut in cuts[1:]:
        level = level * one(*cut)
    return level


def bell_draw(key, shape, scale, bound, cuts=(), held_as=jnp.bfloat16):
    entries = jax.random.normal(key, shape, jnp.float32) * scale
    if len(cuts) > 0:
        entries = level_of(key, shape, cuts, -0.22, 0.18) * entries
    return jnp.clip(entries, min=-bound, max=bound).astype(held_as)


def setup_inputs(seed: int = 0) -> dict:
    arg_keys = jax.random.split(jax.random.key(seed), 8)
    return {
        "tokens": bell_draw(arg_keys[0], (TOKENS, D), 1.0, 6.0, ((0, 32),)),
        "window_lengths": draw_window_lengths(jax.random.fold_in(arg_keys[7], 71), 0),
        "conv_weight": bell_draw(arg_keys[2], (KERNEL_TAPS, D, D), (KERNEL_TAPS * D) ** -0.5, 0.09375, ((1, 8), (2, 4))),
        "feedforward_input_weight": bell_draw(arg_keys[3], (D, FF), D ** -0.5, 0.25, ((0, 8), (1, 4))),
        "ffn_out": bell_draw(arg_keys[4], (FF, D), FF ** -0.5, 0.125, ((0, 8), (1, 4))),
        "small_params": draw_small_params(jax.random.fold_in(arg_keys[7], 71), 0),
        "cotangent": bell_draw(arg_keys[6], (TOKENS, D), 1.0, 6.0, ((0, 32),)),
    }


@jax.custom_vjp
def low(v):
    return lax.optimization_barrier(v.astype(jnp.bfloat16)).astype(jnp.float32)

@jax.custom_vjp
def low_back(v):
    return v

def low_keep(v):
    return (low(v), None)

def low_pass(kept, grad):
    return (grad,)

def back_keep(v):
    return (v, None)

def back_low(kept, grad):
    return (low(grad),)
low.defvjp(low_keep, low_pass)
low_back.defvjp(back_keep, back_low)
EPSILON = 1e-05

def layer_norm(values, norm_gain, norm_shift):
    centre = values - lax.optimization_barrier(jnp.mean(values, axis=-1, keepdims=True))
    spread = lax.optimization_barrier(jnp.mean(centre * centre, axis=-1, keepdims=True))
    return centre * lax.rsqrt(spread + EPSILON) * norm_gain + norm_shift

def window_masks(lengths, row_count):
    bounds = jnp.cumsum(lengths.astype(jnp.int32)).astype(jnp.int32)
    places = jnp.arange(row_count, dtype=jnp.int32)
    segment_ids = lax.optimization_barrier(jnp.sum((places[:, None] >= bounds[None, :]).astype(jnp.int32), axis=1)).astype(jnp.int32)
    live_rows = (places < bounds[-1]).astype(jnp.float32)
    tap_valid = []
    for index_of_tap in range(KERNEL_TAPS):
        tap_displacement = (index_of_tap - KERNEL_TAPS // 2) * DILATION_STEP
        source = places + tap_displacement
        inside = (source >= 0) & (source < row_count)
        same_window = jnp.roll(segment_ids, -tap_displacement) == segment_ids
        tap_valid.append((inside & same_window).astype(jnp.float32))
    return (live_rows, tap_valid)

def split_params(flat_params):
    return (flat_params[0:D], flat_params[D:2 * D], flat_params[2 * D:3 * D], flat_params[3 * D:3 * D + FF], flat_params[3 * D + FF:4 * D + FF], flat_params[4 * D + FF:5 * D + FF], flat_params[5 * D + FF:6 * D + FF])

def dense(left, right):
    return jnp.dot(left, right, precision=lax.Precision.HIGHEST, preferred_element_type=jnp.float32)

def block_forward(inputs, lengths, conv_weight, feedforward_input_weight, ffn_out, small_params):
    row_count = inputs.shape[0]
    live_rows, tap_valid = window_masks(lengths, row_count)
    conv_bias, gain_one, shift_one, inner_bias, outer_bias, gain_two, shift_two = split_params(small_params)
    start_rows = inputs * live_rows[:, None]
    conv_sum = jnp.zeros((row_count, D), jnp.float32)
    for index_of_tap in range(KERNEL_TAPS):
        tap_displacement = (index_of_tap - KERNEL_TAPS // 2) * DILATION_STEP
        shifted = jnp.roll(start_rows, -tap_displacement, axis=0) * tap_valid[index_of_tap][:, None]
        conv_sum = conv_sum + dense(shifted, conv_weight[index_of_tap])
    conv_out = low_back(conv_sum) + conv_bias
    residual_one = start_rows + layer_norm(jax.nn.gelu(conv_out), gain_one, shift_one)
    inner_sum = low_back(dense(low(residual_one), feedforward_input_weight)) + inner_bias
    active = low(jax.nn.gelu(inner_sum))
    outer_sum = low_back(dense(active, ffn_out)) + outer_bias
    return live_rows[:, None] * (residual_one + layer_norm(outer_sum, gain_two, shift_two))

def reference(tokens, window_lengths, conv_weight, feedforward_input_weight, ffn_out, small_params, cotangent):
    groups = N_WIDE * N_NARROW
    inputs = tokens.astype(jnp.float32).reshape(groups, TOK_DEV, D)
    per_block = jax.checkpoint(block_forward)

    def whole_layer(inputs, conv_full, inner_full, outer_full, flat_params):
        return lax.map(lambda packed: per_block(packed[0], packed[1], conv_full, inner_full, outer_full, flat_params), (inputs, window_lengths))
    result, pull_back = jax.vjp(whole_layer, inputs, conv_weight.astype(jnp.float32), feedforward_input_weight.astype(jnp.float32), ffn_out.astype(jnp.float32), small_params.astype(jnp.float32))
    gradients = pull_back(cotangent.astype(jnp.float32).reshape(groups, TOK_DEV, D))
    return (result.reshape(TOKENS, D).astype(jnp.bfloat16), gradients[0].reshape(TOKENS, D), gradients[1], gradients[2], gradients[3], gradients[4])
```

```python
import functools

import jax
import jax.numpy as jnp
from jax import lax
from jax.experimental import pallas as pl
from jax.experimental.pallas import tpu as pltpu
from jax.sharding import PartitionSpec as P

D = 512
FF = 2048
KERNEL_TAPS = 9
DILATION_STEP = 8
EPSILON = 1e-05

def layer_norm(values, norm_gain, norm_shift):
    centre = values - jnp.mean(values, axis=-1, keepdims=True)
    spread = jnp.mean(centre * centre, axis=-1, keepdims=True)
    return centre * lax.rsqrt(spread + EPSILON) * norm_gain + norm_shift


def window_masks(lengths, row_count):
    bounds = jnp.cumsum(lengths)
    places = jnp.arange(row_count, dtype=jnp.int32)
    segment_ids = jnp.sum((places[:, None] >= bounds[None, :]).astype(jnp.int32), axis=1)
    live_rows = (places < bounds[-1]).astype(jnp.float32)
    tap_valid = []
    for index_of_tap in range(KERNEL_TAPS):
        tap_displacement = (index_of_tap - KERNEL_TAPS // 2) * DILATION_STEP
        source = places + tap_displacement
        inside = (source >= 0) & (source < row_count)
        same_window = jnp.roll(segment_ids, -tap_displacement) == segment_ids
        tap_valid.append((inside & same_window).astype(jnp.float32))
    return (live_rows, tap_valid)


def split_params(flat_params):
    return (
        flat_params[0:D],
        flat_params[D : 2 * D],
        flat_params[2 * D : 3 * D],
        flat_params[3 * D : 3 * D + FF],
        flat_params[3 * D + FF : 4 * D + FF],
        flat_params[4 * D + FF : 5 * D + FF],
        flat_params[5 * D + FF : 6 * D + FF],
    )


def branch_one(conv_sum, conv_bias, gain_one, shift_one):
    return layer_norm(jax.nn.gelu(conv_sum + conv_bias), gain_one, shift_one)


def branch_two(outer_sum, outer_bias, gain_two, shift_two):
    return layer_norm(outer_sum + outer_bias, gain_two, shift_two)


def fetch_forward(conv_weight, feedforward_input_weight, ffn_out, small_params):
    narrow_set = (
        lax.all_gather(conv_weight, "narrow", axis=2, tiled=True),
        lax.all_gather(feedforward_input_weight, "narrow", axis=1, tiled=True),
        lax.all_gather(ffn_out, "narrow", axis=1, tiled=True),
        lax.all_gather(small_params, "narrow", axis=0, tiled=True),
    )
    return (
        lax.all_gather(narrow_set[0], "wide", axis=1, tiled=True),
        lax.all_gather(narrow_set[1], "wide", axis=0, tiled=True),
        lax.all_gather(narrow_set[2], "wide", axis=0, tiled=True),
        lax.all_gather(narrow_set[3], "wide", axis=0, tiled=True),
    )


def shards(
    tokens, window_lengths, conv_weight, feedforward_input_weight, ffn_out, small_params, cotangent
):
    row_count = tokens.shape[0]
    block_size = min(512, row_count)
    live_rows, tap_valid = window_masks(window_lengths[0], row_count)
    weights = fetch_forward(conv_weight, feedforward_input_weight, ffn_out, small_params)
    conv_full, inner_full, outer_full = (weights[0], weights[1], weights[2])
    pieces = split_params(weights[3].astype(jnp.float32))
    start_rows = tokens * live_rows[:, None].astype(jnp.bfloat16)
    conv_sum = jnp.zeros((row_count, D), jnp.float32)
    for index_of_tap in range(KERNEL_TAPS):
        tap_displacement = (index_of_tap - KERNEL_TAPS // 2) * DILATION_STEP
        shifted = jnp.roll(start_rows, -tap_displacement, axis=0) * tap_valid[index_of_tap][
            :, None
        ].astype(jnp.bfloat16)
        conv_sum = conv_sum + jnp.dot(
            shifted, conv_full[index_of_tap], preferred_element_type=jnp.float32
        )
    branch_out, pull_one = jax.vjp(branch_one, conv_sum, pieces[0], pieces[1], pieces[2])
    residual_one = start_rows.astype(jnp.float32) + branch_out
    residual_low = residual_one.astype(jnp.bfloat16)
    outer_parts = []
    for first_row in range(0, row_count, block_size):
        inner_sum = (
            jnp.dot(
                residual_low[first_row : first_row + block_size],
                inner_full,
                preferred_element_type=jnp.float32,
            )
            + pieces[3]
        )
        active = jax.nn.gelu(inner_sum).astype(jnp.bfloat16)
        outer_parts.append(jnp.dot(active, outer_full, preferred_element_type=jnp.float32))
    outer_sum = jnp.concatenate(outer_parts, axis=0)
    normed, pull_two = jax.vjp(branch_two, outer_sum, pieces[4], pieces[5], pieces[6])
    block_out = (live_rows[:, None] * (residual_one + normed)).astype(jnp.bfloat16)
    upstream = cotangent.astype(jnp.float32) * live_rows[:, None]
    d_outer, d_outer_bias, d_gain_two, d_shift_two = pull_two(upstream)
    outer_low = d_outer.astype(jnp.bfloat16)
    grad_in = jnp.zeros((D, FF), jnp.float32)
    grad_out = jnp.zeros((FF, D), jnp.float32)
    inner_bias_grad = jnp.zeros((FF,), jnp.float32)
    resid_parts = []
    for first_row in range(0, row_count, block_size):
        rows_low = residual_low[first_row : first_row + block_size]
        outer_rows = outer_low[first_row : first_row + block_size]
        inner_sum = jnp.dot(rows_low, inner_full, preferred_element_type=jnp.float32) + pieces[3]
        active_full, pull_gelu = jax.vjp(jax.nn.gelu, inner_sum)
        active = active_full.astype(jnp.bfloat16)
        d_active = jnp.einsum(
            "rd,fd->rf", outer_rows, outer_full, preferred_element_type=jnp.float32
        )
        d_inner = pull_gelu(d_active)[0]
        inner_bias_grad = inner_bias_grad + jnp.sum(d_inner, axis=0)
        inner_low = d_inner.astype(jnp.bfloat16)
        grad_in = grad_in + jnp.einsum(
            "rd,rf->df", rows_low, inner_low, preferred_element_type=jnp.float32
        )
        grad_out = grad_out + jnp.einsum(
            "rf,rd->fd", active, outer_rows, preferred_element_type=jnp.float32
        )
        resid_parts.append(
            jnp.einsum("rf,df->rd", inner_low, inner_full, preferred_element_type=jnp.float32)
        )
    d_resid = upstream + jnp.concatenate(resid_parts, axis=0)
    d_conv, d_conv_bias, d_gain_one, d_shift_one = pull_one(d_resid)
    convolution_reduced = d_conv.astype(jnp.bfloat16)
    conv_grads = []
    d_start = d_resid
    for index_of_tap in range(KERNEL_TAPS):
        tap_displacement = (index_of_tap - KERNEL_TAPS // 2) * DILATION_STEP
        tap_mask = tap_valid[index_of_tap][:, None]
        shifted = jnp.roll(start_rows, -tap_displacement, axis=0) * tap_mask.astype(jnp.bfloat16)
        conv_grads.append(
            jnp.einsum(
                "ri,ro->io", shifted, convolution_reduced, preferred_element_type=jnp.float32
            )
        )
        back_rows = jnp.einsum(
            "ro,io->ri",
            convolution_reduced,
            conv_full[index_of_tap],
            preferred_element_type=jnp.float32,
        )
        d_start = d_start + jnp.roll(back_rows * tap_mask, tap_displacement, axis=0)
    grad_tokens = d_start * live_rows[:, None]
    convolution_weight_gradient = jnp.stack(conv_grads, axis=0)
    grad_flat = jnp.concatenate(
        [
            d_conv_bias,
            d_gain_one,
            d_shift_one,
            inner_bias_grad,
            d_outer_bias,
            d_gain_two,
            d_shift_two,
        ],
        axis=0,
    )
    wide_sums = (
        lax.psum_scatter(convolution_weight_gradient, "wide", scatter_dimension=1, tiled=True),
        lax.psum_scatter(grad_in, "wide", scatter_dimension=0, tiled=True),
        lax.psum_scatter(grad_out, "wide", scatter_dimension=0, tiled=True),
        lax.psum_scatter(grad_flat, "wide", scatter_dimension=0, tiled=True),
    )
    owned = (
        lax.psum_scatter(wide_sums[0], "narrow", scatter_dimension=2, tiled=True),
        lax.psum_scatter(wide_sums[1], "narrow", scatter_dimension=1, tiled=True),
        lax.psum_scatter(wide_sums[2], "narrow", scatter_dimension=1, tiled=True),
        lax.psum_scatter(wide_sums[3], "narrow", scatter_dimension=0, tiled=True),
    )
    owned_flat = owned[3]
    return (block_out, grad_tokens, owned[0], owned[1], owned[2], owned_flat)

MESH = pl.DeviceIdType.MESH
BF = jnp.bfloat16
F32 = jnp.float32
BLOCK = 256
REACH = KERNEL_TAPS // 2 * DILATION_STEP
STEP_ROWS = 512
PARAM_ROWS = 48
GRAD_ROWS = 40
VMEM_LIMIT = 63 << 20
GELU_A = 0.7978845608028654
GELU_B = 0.044715
TAP_PIECES = ((0, 1), (1, 3), (3, 6), (6, 9))
GRAD_TAP_PIECES = ((0, 3), (3, 6), (6, 9))


class Links:
    def __init__(self, sizes, send_sems, recv_sems):
        self.Z, self.X, self.Y = sizes
        wide, narrow = lax.axis_index("wide"), lax.axis_index("narrow")
        self.z, self.x = wide // self.X, wide % self.X
        self.y, self.c = narrow // 2, narrow % 2
        self.send_sems, self.recv_sems = send_sems, recv_sems
        self.used = 0
        self.copies = []

    def device(self, axis, step):
        z, x, y, c = self.z, self.x, self.y, self.c
        if axis == "z":
            z = lax.rem(z + step, self.Z)
        elif axis == "x":
            x = lax.rem(x + step, self.X)
        elif axis == "y":
            y = lax.rem(y + step, self.Y)
        else:
            c = 1 - c
        return (z * self.X + x, y * 2 + c)

    def steps(self, axis):
        return range(1, {"z": self.Z, "x": self.X, "y": self.Y, "c": 2}[axis])

    def send(self, source, target, axis, step=1):
        index = self.used
        self.used += 1
        copy = pltpu.make_async_remote_copy(
            src_ref=source,
            dst_ref=target,
            send_sem=self.send_sems.at[index],
            recv_sem=self.recv_sems.at[index],
            device_id=self.device(axis, step),
            device_id_type=MESH,
        )
        copy.start()
        self.copies.append(copy)
        return copy

    def barrier(self):
        semaphore = pltpu.get_barrier_semaphore()
        partners = [self.device(axis, s) for axis in "zxyc" for s in self.steps(axis)]
        for partner in partners:
            pl.semaphore_signal(semaphore, inc=1, device_id=partner, device_id_type=MESH)
        pl.semaphore_wait(semaphore, len(partners))

    def finish(self):
        for copy in self.copies:
            copy.wait_send()


class Gather:
    def __init__(self, links, shard, whole, first, last):
        self.links, self.shard, self.whole = links, shard, whole
        self.taps = pl.ds(first, last - first)
        half = whole.shape[5] // 2
        self.low, self.high = pl.ds(0, half), pl.ds(half, half)

    def along_z(self):
        k = self.links
        target = self.whole.at[self.taps, k.y, k.c, k.z, k.x]
        self.waits = [k.send(self.shard.at[self.taps], target, "z", s) for s in k.steps("z")]

    def first(self, own=None):
        k = self.links
        for copy in self.waits:
            copy.wait_recv()
        if own is not None:
            own.wait()
        low = self.whole.at[self.taps, k.y, k.c, :, k.x, self.low]
        high = self.whole.at[self.taps, k.y, k.c, :, k.x, self.high]
        self.lows = [k.send(low, low, "x", s) for s in k.steps("x")]
        self.highs = [k.send(high, high, "y", s) for s in k.steps("y")]

    def second(self):
        k = self.links
        for copy in self.lows:
            copy.wait_recv()
        low = self.whole.at[self.taps, k.y, k.c, :, :, self.low]
        self.waits = [k.send(low, low, "y", s) for s in k.steps("y")]
        for copy in self.highs:
            copy.wait_recv()
        high = self.whole.at[self.taps, :, k.c, :, k.x, self.high]
        self.waits += [k.send(high, high, "x", s) for s in k.steps("x")]

    def to_core(self):
        k = self.links
        for copy in self.waits:
            copy.wait_recv()
        own = self.whole.at[self.taps, :, k.c]
        self.last = k.send(own, own, "c")

    def arrive(self):
        self.last.wait_recv()


class Scatter:
    def __init__(self, links, buffers, half, first, last, finish):
        self.links, self.half, self.finish = links, half, finish
        self.taps = pl.ds(first, last - first)
        self.partial, self.pair, self.one, self.two, self.three = buffers

    def to_core(self):
        k, h, t = self.links, self.half, self.taps
        self.wait = [k.send(self.partial.at[1 - k.c, h, t], self.pair.at[h, t], "c")]

    def first(self):
        k, h, t, pair = self.links, self.half, self.taps, self.pair
        for copy in self.wait:
            copy.wait_recv()
        pair[h, t] = pair[h, t] + self.partial[k.c, h, t]
        if h == 0:
            self.wait = [
                k.send(pair.at[h, t, lax.rem(k.y + s, k.Y)], self.one[h].at[s - 1, t], "y", s)
                for s in k.steps("y")
            ]
        else:
            self.wait = [
                k.send(pair.at[h, t, :, :, lax.rem(k.x + s, k.X)], self.one[h].at[s - 1, t], "x", s)
                for s in k.steps("x")
            ]

    def second(self):
        k, h, t, pair, one = self.links, self.half, self.taps, self.pair, self.one[self.half]
        for copy in self.wait:
            copy.wait_recv()
        if h == 0:
            for s in k.steps("y"):
                pair[h, t, k.y] = pair[h, t, k.y] + one[s - 1, t]
            self.wait = [
                k.send(pair.at[h, t, k.y, :, lax.rem(k.x + s, k.X)], self.two[h].at[s - 1, t], "x", s)
                for s in k.steps("x")
            ]
        else:
            for s in k.steps("x"):
                pair[h, t, :, :, k.x] = pair[h, t, :, :, k.x] + one[s - 1, t]
            self.wait = [
                k.send(pair.at[h, t, lax.rem(k.y + s, k.Y), :, k.x], self.two[h].at[s - 1, t], "y", s)
                for s in k.steps("y")
            ]

    def along_z(self):
        k, h, t, pair, two = self.links, self.half, self.taps, self.pair, self.two[self.half]
        for copy in self.wait:
            copy.wait_recv()
        for s in k.steps("x" if h == 0 else "y"):
            pair[h, t, k.y, :, k.x] = pair[h, t, k.y, :, k.x] + two[s - 1, t]
        self.wait = [
            k.send(pair.at[h, t, k.y, lax.rem(k.z + s, k.Z), k.x], self.three.at[s - 1, h, t], "z", s)
            for s in k.steps("z")
        ]

    def arrive(self):
        k, h, t = self.links, self.half, self.taps
        for copy in self.wait:
            copy.wait_recv()
        total = self.pair[h, t, k.y, k.z, k.x].astype(F32)
        for s in k.steps("z"):
            total = total + self.three[s - 1, h, t].astype(F32)
        self.finish(total, h, t)


def gelu_pair(value):
    square = value * value
    bend = jnp.tanh(value * (GELU_A + (GELU_A * GELU_B) * square))
    share = 0.5 + 0.5 * bend
    slope = share + (0.5 * value) * ((1.0 - bend * bend) * (GELU_A + (3 * GELU_A * GELU_B) * square))
    return value * share, slope


def normalize(value):
    centre = value - jnp.mean(value, axis=-1, keepdims=True)
    factor = lax.rsqrt(jnp.mean(centre * centre, axis=-1, keepdims=True) + EPSILON)
    return centre * factor, factor


def normalize_back(grad, hat, factor):
    return factor * (
        grad
        - jnp.mean(grad, axis=-1, keepdims=True)
        - hat * jnp.mean(grad * hat, axis=-1, keepdims=True)
    )


def side_by_side(whole, tap):
    lanes = whole.shape[-1]
    return jnp.concatenate(
        [whole[tap, y, c].reshape(-1, lanes) for y in range(whole.shape[1]) for c in range(2)], axis=1
    )


def dot(left, right, over=((1,), (0,))):
    return lax.dot_general(left, right, (over, ((), ())), preferred_element_type=F32)


OVER_ROWS = ((0,), (0,))
OVER_LANES = ((1,), (1,))


def kernel(
    sizes, lengths, params_in, tokens, cotangent, conv_in, inner_in, outer_in,
    block_out, grad_tokens, conv_out, inner_out, outer_out, params_out,
    conv_w, inner_w, outer_w, params_got, params_sum,
    rows_buf, cot_buf, padded, padded_by8, padded_back, stage, conv_sum, resid, resid_low, active, slope, outer_low,
    conv_partial, inner_partial, outer_partial,
    conv_pair, inner_pair, outer_pair,
    conv_one_a, conv_one_b, inner_one_a, inner_one_b, outer_one_a, outer_one_b,
    conv_two_a, conv_two_b, inner_two_a, inner_two_b, outer_two_a, outer_two_b,
    conv_three, inner_three, outer_three,
    grads, grads_got,
    send_sems, recv_sems, local_sems,
):
    k = Links(sizes, send_sems, recv_sems)
    Z, X, Y = sizes
    row_count = tokens.shape[0]
    blocks = row_count // BLOCK
    steps = row_count // STEP_ROWS
    per_step = STEP_ROWS // BLOCK
    mine = k.y, k.c, k.z, k.x

    def local(index, source, target):
        copy = pltpu.make_async_copy(source, target, local_sems.at[index])
        copy.start()
        return copy

    rows_in = local(0, tokens, rows_buf)
    own = [
        local(1 + i, shard, whole.at[:, k.y, k.c, k.z, k.x])
        for i, (shard, whole) in enumerate(((conv_in, conv_w), (inner_in, inner_w), (outer_in, outer_w)))
    ]
    cot_in = local(4, cotangent, cot_buf)
    k.barrier()

    pieces = [Gather(k, conv_in, conv_w, first, last) for first, last in TAP_PIECES]
    pieces += [Gather(k, inner_in, inner_w, 0, 1), Gather(k, outer_in, outer_w, 0, 1)]
    own_of = {0: own[0], len(TAP_PIECES): own[1], len(TAP_PIECES) + 1: own[2]}
    count = len(pieces)

    bounds = []
    total = 0
    for slot in range(lengths.shape[1]):
        total = total + lengths[0, slot]
        bounds.append(total)

    def window(block):
        number = 0
        for bound in bounds:
            number = number + jnp.where(block * BLOCK >= bound, 1, 0)
        return number

    def live(block):
        return jnp.where(block * BLOCK < total, 1.0, 0.0).astype(F32)

    def joined(block):
        return jnp.where(window(block) == window(block + 1), 1.0, 0.0).astype(F32) * live(block)

    def pad(source, target, target_by8):
        for b in range(blocks):
            at = b * BLOCK
            if b > 0:
                stage[0:REACH] = source[at - REACH : at].astype(F32) * joined(b - 1)
            else:
                stage[0:REACH] = jnp.zeros((REACH, D), F32)
            stage[REACH : REACH + BLOCK] = source[at : at + BLOCK].astype(F32) * live(b)
            if b < blocks - 1:
                stage[REACH + BLOCK :] = source[at + BLOCK : at + BLOCK + REACH].astype(F32) * joined(b)
            else:
                stage[REACH + BLOCK :] = jnp.zeros((REACH, D), F32)
            target[b] = stage[...].astype(BF)
            target_by8[b] = stage[8 : BLOCK + 2 * REACH - 8].astype(BF)

    def window_rows(source, source_by8, block, place):
        if place % 2 == 0:
            return source[block, pl.ds(8 * place, BLOCK), :]
        return source_by8[block, pl.ds(8 * (place - 1), BLOCK), :]

    def step_rows(source, source_by8, step, place):
        return jnp.concatenate(
            [window_rows(source, source_by8, step * per_step + j, place) for j in range(per_step)], axis=0
        )

    def all_rows(source, source_by8, place):
        return jnp.concatenate([window_rows(source, source_by8, b, place) for b in range(blocks)], axis=0)

    def at_step(step):
        return pl.ds(pl.multiple_of(step * STEP_ROWS, STEP_ROWS), STEP_ROWS)

    def live_rows(value, step):
        return jnp.concatenate(
            [value[j * BLOCK : (j + 1) * BLOCK] * live(step * per_step + j) for j in range(per_step)], axis=0
        )

    def param(first, width):
        return jnp.concatenate(
            [params_sum[4, pl.ds((first + i) // 128, 1), :].astype(F32) for i in range(0, width, 128)], axis=1
        )

    def add_grad(first, value):
        summed = jnp.sum(value, axis=0, keepdims=True)
        for i in range(0, summed.shape[1], 128):
            row = (first + i) // 128
            grads[0, row : row + 1, :] = grads[0, row : row + 1, :] + summed[:, i : i + 128]

    CONV_BIAS, GAIN_ONE, SHIFT_ONE, INNER_BIAS = 0, D, 2 * D, 3 * D
    OUTER_BIAS, GAIN_TWO, SHIFT_TWO = 3 * D + FF, 4 * D + FF, 5 * D + FF

    slot_at = {"z": 0, "x": Z - 1, "y": Z + X - 2, "c": Z + X + Y - 3}

    def share(source, got, axis):
        return [k.send(source, got.at[slot_at[axis] + s - 1], axis, s) for s in k.steps(axis)]

    def take(copies, source, got, axis):
        for copy in copies:
            copy.wait_recv()
        value = source[...]
        for s in k.steps(axis):
            value = value + got[slot_at[axis] + s - 1]
        return value

    def sum_on(copies, held, got, axes, stage_index):
        held[stage_index + 1] = take(copies, held.at[stage_index], got, axes[stage_index])
        if stage_index + 1 < len(axes):
            return share(held.at[stage_index + 1], got, axes[stage_index + 1])
        return []

    def conv_piece(piece):
        first, last = TAP_PIECES[piece]

        @pl.loop(0, steps)
        def _(step):
            value = None
            for tap in range(first, last):
                term = dot(step_rows(padded, padded_by8, step, tap), side_by_side(conv_w, tap))
                value = term if value is None else value + term
            if piece > 0:
                value = value + conv_sum[at_step(step), :]
            if piece == len(TAP_PIECES) - 1:
                value = value + param(CONV_BIAS, D)
            conv_sum[at_step(step), :] = value
            if piece == len(TAP_PIECES) - 1:
                start = step_rows(padded, padded_by8, step, REACH // 8).astype(F32)
                hat, _ = normalize(gelu_pair(value)[0])
                value = start + hat * param(GAIN_ONE, D) + param(SHIFT_ONE, D)
                resid[at_step(step), :] = value
                resid_low[at_step(step), :] = value.astype(BF)

    width = inner_w.shape[-1]

    def inner_step(step):
        low = resid_low[at_step(step), :]
        for y in range(Y):
            for c in range(2):
                first = (y * 2 + c) * width
                value = dot(low, inner_w[0, y, c].reshape(D, width)) + param(INNER_BIAS + first, width)
                bent, tilt = gelu_pair(value)
                active[at_step(step), first : first + width] = bent.astype(BF)
                slope[at_step(step), first : first + width] = tilt.astype(BF)

    def outer_step(step):
        value = dot(active[at_step(step), :], side_by_side(outer_w, 0)) + param(OUTER_BIAS, D)
        hat, factor = normalize(value)
        gain = param(GAIN_TWO, D)
        result = resid[at_step(step), :] + hat * gain + param(SHIFT_TWO, D)
        rows_buf[at_step(step), :] = live_rows(result, step).astype(BF)
        upstream = live_rows(cot_buf[at_step(step), :].astype(F32), step)
        back = normalize_back(upstream * gain, hat, factor)
        outer_low[at_step(step), :] = back.astype(BF)
        add_grad(OUTER_BIAS, back)
        add_grad(GAIN_TWO, upstream * hat)
        add_grad(SHIFT_TWO, upstream)

    outer_rows = outer_w.shape[5]

    def outer_grad(half):
        size = outer_rows // 2
        left = jnp.concatenate(
            [active[:, i * outer_rows + half * size : i * outer_rows + (half + 1) * size] for i in range(Z * X)],
            axis=1,
        )
        value = dot(left, outer_low[...], OVER_ROWS).astype(BF)
        for y in range(Y):
            for c in range(2):
                first = (y * 2 + c) * 128
                outer_partial[c, half, 0, y] = value[:, first : first + 128].reshape(Z, X, size, 128)

    def hidden_step(step):
        low = outer_low[at_step(step), :]
        for group in range(Y * 2):
            first = group * width
            right = jnp.concatenate(
                [outer_w[0, y, c, group].reshape(width, 128) for y in range(Y) for c in range(2)], axis=1
            )
            value = dot(low, right, OVER_LANES)
            value = value * slope[at_step(step), first : first + width].astype(F32)
            add_grad(INNER_BIAS + first, value)
            slope[at_step(step), first : first + width] = value.astype(BF)

    def inner_grad(half):
        size = width // 2
        right = jnp.concatenate(
            [slope[:, g * width + half * size : g * width + (half + 1) * size] for g in range(Y * 2)], axis=1
        )
        value = dot(resid_low[...], right, OVER_ROWS).astype(BF)
        for y in range(Y):
            for c in range(2):
                first = (y * 2 + c) * size
                inner_partial[c, half, 0, y] = value[:, first : first + size].reshape(Z, X, D // (Z * X), size)

    def resid_step(step):
        value = live_rows(cot_buf[at_step(step), :].astype(F32), step)
        for y in range(Y):
            for c in range(2):
                first = (y * 2 + c) * width
                value = value + dot(
                    slope[at_step(step), first : first + width], inner_w[0, y, c].reshape(D, width), OVER_LANES
                )
        resid[at_step(step), :] = value
        bent, tilt = gelu_pair(conv_sum[at_step(step), :])
        hat, factor = normalize(bent)
        add_grad(GAIN_ONE, value * hat)
        add_grad(SHIFT_ONE, value)
        back = normalize_back(value * param(GAIN_ONE, D), hat, factor) * tilt
        add_grad(CONV_BIAS, back)
        conv_sum[at_step(step), :] = back

    conv_rows = conv_w.shape[5]

    def conv_grad(first, last):
        left = all_rows(padded, None, REACH // 8)
        for tap in range(first, last):
            right = all_rows(padded_back, padded_by8, KERNEL_TAPS - 1 - tap)
            value = dot(left, right, OVER_ROWS).astype(BF)
            for y in range(Y):
                for c in range(2):
                    at = (y * 2 + c) * 128
                    part = value[:, at : at + 128].reshape(Z, X, conv_rows, 128)
                    for half in range(2):
                        size = conv_rows // 2
                        conv_partial[c, half, tap, y] = part[:, :, half * size : (half + 1) * size]

    def token_step(step):
        value = resid[at_step(step), :]
        for tap in range(KERNEL_TAPS):
            value = value + dot(
                step_rows(padded_back, padded_by8, step, KERNEL_TAPS - 1 - tap),
                side_by_side(conv_w, tap),
                OVER_LANES,
            )
        resid[at_step(step), :] = live_rows(value, step)

    def conv_finish(value, half, taps):
        size = conv_rows // 2
        conv_out[taps, pl.ds(half * size, size), :] = value

    def inner_finish(value, half, taps):
        size = width // 2
        inner_out[:, half * size : (half + 1) * size] = value[0]

    def outer_finish(value, half, taps):
        size = outer_rows // 2
        outer_out[half * size : (half + 1) * size, :] = value[0]

    params_sum[0] = params_in[...]
    sharing = share(params_in, params_got, "z")
    pieces[0].along_z()
    pieces[1].along_z()
    rows_in.wait()
    grads[0] = jnp.zeros((GRAD_ROWS, 128), F32)
    pad(rows_buf, padded, padded_by8)
    turn = ["z", "x", "y", "c"]
    for i in range(count + 3):
        if 0 < i and i + 1 < count:
            pieces[i + 1].along_z()
        if i < count:
            pieces[i].first(own_of.get(i))
        if 0 <= i - 1 < count:
            pieces[i - 1].second()
        if i < 4:
            sharing = sum_on(sharing, params_sum, params_got, turn, i)
        if 0 <= i - 2 < count:
            pieces[i - 2].to_core()
        if 0 <= i - 3 < len(TAP_PIECES):
            pieces[i - 3].arrive()
            conv_piece(i - 3)
    pieces[count - 2].arrive()
    pl.loop(0, steps)(inner_step)
    pieces[count - 1].arrive()
    cot_in.wait()
    pl.loop(0, steps)(outer_step)
    block_copy = local(0, rows_buf, block_out)

    outer_buffers = (outer_partial, outer_pair, (outer_one_a, outer_one_b), (outer_two_a, outer_two_b), outer_three)
    inner_buffers = (inner_partial, inner_pair, (inner_one_a, inner_one_b), (inner_two_a, inner_two_b), inner_three)
    conv_buffers = (conv_partial, conv_pair, (conv_one_a, conv_one_b), (conv_two_a, conv_two_b), conv_three)
    outers = [Scatter(k, outer_buffers, half, 0, 1, outer_finish) for half in range(2)]
    inners = [Scatter(k, inner_buffers, half, 0, 1, inner_finish) for half in range(2)]
    convs = [
        Scatter(k, conv_buffers, half, first, last, conv_finish)
        for first, last in GRAD_TAP_PIECES
        for half in range(2)
    ]
    outer_grad(0)
    outers[0].to_core()
    outer_grad(1)
    outers[1].to_core()
    outers[0].first()
    hidden_step(0)
    outers[1].first()
    hidden_step(1)
    outers[0].second()
    hidden_step(2)
    outers[1].second()
    inner_grad(0)
    inners[0].to_core()
    outers[0].along_z()
    inner_grad(1)
    inners[1].to_core()
    inners[0].first()
    outers[1].along_z()
    resid_step(0)
    inners[1].first()
    resid_step(1)
    inners[0].second()
    outers[0].arrive()
    resid_step(2)
    inners[1].second()
    outers[1].arrive()
    back_turn = ["c", "x", "y", "z"]
    sharing = share(grads.at[0], grads_got, "c")
    pad(conv_sum, padded_back, padded_by8)
    conv_grad(0, 3)
    convs[0].to_core()
    convs[1].to_core()
    inners[0].along_z()
    inners[1].along_z()
    sharing = sum_on(sharing, grads, grads_got, back_turn, 0)
    conv_grad(3, 6)
    sharing = sum_on(sharing, grads, grads_got, back_turn, 1)
    convs[0].first()
    convs[1].first()
    convs[2].to_core()
    convs[3].to_core()
    conv_grad(6, 9)
    sharing = sum_on(sharing, grads, grads_got, back_turn, 2)
    convs[2].first()
    convs[3].first()
    convs[4].to_core()
    convs[5].to_core()
    convs[0].second()
    convs[1].second()
    inners[0].arrive()
    inners[1].arrive()
    token_step(0)
    params_out[...] = take(sharing, grads.at[3], grads_got, "z")
    convs[4].first()
    convs[5].first()
    convs[2].second()
    convs[3].second()
    convs[0].along_z()
    convs[1].along_z()
    token_step(1)
    convs[4].second()
    convs[5].second()
    convs[2].along_z()
    convs[3].along_z()
    token_step(2)
    token_copy = local(1, resid, grad_tokens)
    convs[4].along_z()
    convs[5].along_z()
    for i in range(4):
        convs[i].arrive()
    convs[4].arrive()
    convs[5].arrive()
    block_copy.wait()
    token_copy.wait()
    k.finish()


def run_kernel(sizes, lengths, params, tokens, cotangent, conv_shard, inner_shard, outer_shard):
    Z, X, Y = sizes
    taps, conv_rows, lanes = conv_shard.shape
    inner_rows, width = inner_shard.shape
    outer_rows = outer_shard.shape[0]
    rows = tokens.shape[0]
    blocks = rows // BLOCK
    inner_shard, outer_shard = inner_shard[None], outer_shard[None]

    def whole(shard):
        return pltpu.VMEM((shard.shape[0], Y, 2, Z, X) + shard.shape[1:], BF)

    def scatter_buffers(count, r, lane):
        return (
            pltpu.VMEM((2, 2, count, Y, Z, X, r, lane), BF),
            pltpu.VMEM((2, count, Y, Z, X, r, lane), BF),
            pltpu.VMEM((Y - 1, count, Z, X, r, lane), BF),
            pltpu.VMEM((X - 1, count, Y, Z, r, lane), BF),
            pltpu.VMEM((X - 1, count, Z, r, lane), BF),
            pltpu.VMEM((Y - 1, count, Z, r, lane), BF),
            pltpu.VMEM((Z - 1, 2, count, r, lane), BF),
        )

    conv_b = scatter_buffers(taps, conv_rows // 2, lanes)
    inner_b = scatter_buffers(1, inner_rows, width // 2)
    outer_b = scatter_buffers(1, outer_rows // 2, lanes)
    partners = Z - 1 + X - 1 + Y - 1 + 1
    copies = 16 * (partners + 4)
    padded = BLOCK + 2 * REACH
    scratch = [whole(conv_shard), whole(inner_shard), whole(outer_shard)]
    scratch += [pltpu.VMEM((partners, PARAM_ROWS, 128), BF), pltpu.VMEM((5, PARAM_ROWS, 128), BF)]
    scratch += [
        pltpu.VMEM((rows, D), BF),
        pltpu.VMEM((rows, D), BF),
        pltpu.VMEM((blocks, padded, D), BF),
        pltpu.VMEM((blocks, padded - 16, D), BF),
        pltpu.VMEM((blocks, padded, D), BF),
        pltpu.VMEM((padded, D), F32),
        pltpu.VMEM((rows, D), F32),
        pltpu.VMEM((rows, D), F32),
        pltpu.VMEM((rows, D), BF),
        pltpu.VMEM((rows, FF), BF),
        pltpu.VMEM((rows, FF), BF),
        pltpu.VMEM((rows, D), BF),
    ]
    scratch += [b[0] for b in (conv_b, inner_b, outer_b)]
    scratch += [b[1] for b in (conv_b, inner_b, outer_b)]
    scratch += [b[i] for b in (conv_b, inner_b, outer_b) for i in (2, 3)]
    scratch += [b[i] for b in (conv_b, inner_b, outer_b) for i in (4, 5)]
    scratch += [b[6] for b in (conv_b, inner_b, outer_b)]
    scratch += [pltpu.VMEM((5, GRAD_ROWS, 128), F32), pltpu.VMEM((partners, GRAD_ROWS, 128), F32)]
    scratch += [pltpu.SemaphoreType.DMA((copies,)), pltpu.SemaphoreType.DMA((copies,)), pltpu.SemaphoreType.DMA((8,))]
    far = pl.BlockSpec(memory_space=pl.ANY)
    near = pl.BlockSpec(memory_space=pltpu.VMEM)
    return pl.pallas_call(
        functools.partial(kernel, sizes),
        out_shape=[
            jax.ShapeDtypeStruct((rows, D), BF),
            jax.ShapeDtypeStruct((rows, D), F32),
            jax.ShapeDtypeStruct(conv_shard.shape, F32),
            jax.ShapeDtypeStruct(inner_shard.shape[1:], F32),
            jax.ShapeDtypeStruct(outer_shard.shape[1:], F32),
            jax.ShapeDtypeStruct((GRAD_ROWS, 128), F32),
        ],
        in_specs=[pl.BlockSpec(memory_space=pltpu.SMEM), near] + [far] * 5,
        out_specs=[far, far, near, near, near, near],
        scratch_shapes=scratch,
        compiler_params=pltpu.CompilerParams(
            collective_id=0, has_side_effects=True, vmem_limit_bytes=VMEM_LIMIT
        ),
    )(lengths, params, tokens, cotangent, conv_shard, inner_shard, outer_shard)


def fused(
    sizes, tokens, window_lengths, conv_weight, feedforward_input_weight, ffn_out, small_params, cotangent
):
    share = small_params.shape[0]
    whole = 6 * D + FF
    device = lax.axis_index("wide") * (sizes[2] * 2) + lax.axis_index("narrow")
    places = jnp.arange(PARAM_ROWS * 128, dtype=jnp.int32)
    params = jnp.where(
        places // share == device, jnp.tile(small_params, PARAM_ROWS * 128 // share + 1)[: PARAM_ROWS * 128], 0
    ).reshape(PARAM_ROWS, 128)
    block_out, grad_tokens, conv_grad, inner_grad, outer_grad, params_grad = run_kernel(
        sizes, window_lengths, params, tokens, cotangent, conv_weight, feedforward_input_weight, ffn_out
    )
    own = lax.dynamic_slice(params_grad.reshape(whole), (device * share,), (share,))
    return (block_out, grad_tokens, conv_grad, inner_grad, outer_grad, own)


def solution(mesh):
    wide, narrow = mesh.shape["wide"], mesh.shape["narrow"]
    Y = X = narrow // 2
    sizes = (wide // X, X, Y)

    def step(*arrays):
        rows = arrays[0].shape[0]
        inner, outer = arrays[3].shape, arrays[4].shape
        whole_lanes = all(a.shape[-1] % 256 == 0 or a.shape[-1] == 128 for a in arrays[2:5])
        fits = rows % STEP_ROWS == 0 and inner[1] == X * outer[0] and whole_lanes
        if fits and wide % X == 0 and narrow % 2 == 0:
            return fused(sizes, *arrays)
        return shards(*arrays)

    return jax.shard_map(
        step,
        mesh=mesh,
        in_specs=(
            P(("wide", "narrow"), None),
            P(("wide", "narrow"), None),
            P(None, "wide", "narrow"),
            P("wide", "narrow"),
            P("wide", "narrow"),
            P(("wide", "narrow")),
            P(("wide", "narrow"), None),
        ),
        out_specs=(
            P(("wide", "narrow"), None),
            P(("wide", "narrow"), None),
            P(None, "wide", "narrow"),
            P("wide", "narrow"),
            P("wide", "narrow"),
            P(("wide", "narrow")),
        ),
        check_vma=False,
    )
```

```python
import functools

import jax
import jax.numpy as jnp
from jax import lax
from jax.experimental import pallas as pl
from jax.experimental.pallas import tpu as pltpu
from jax.sharding import PartitionSpec as P

D = 512
FF = 2048
KERNEL_TAPS = 9
DILATION_STEP = 8
EPSILON = 1e-05

def layer_norm(values, norm_gain, norm_shift):
    centre = values - jnp.mean(values, axis=-1, keepdims=True)
    spread = jnp.mean(centre * centre, axis=-1, keepdims=True)
    return centre * lax.rsqrt(spread + EPSILON) * norm_gain + norm_shift


def window_masks(lengths, row_count):
    bounds = jnp.cumsum(lengths)
    places = jnp.arange(row_count, dtype=jnp.int32)
    segment_ids = jnp.sum((places[:, None] >= bounds[None, :]).astype(jnp.int32), axis=1)
    live_rows = (places < bounds[-1]).astype(jnp.float32)
    tap_valid = []
    for index_of_tap in range(KERNEL_TAPS):
        tap_displacement = (index_of_tap - KERNEL_TAPS // 2) * DILATION_STEP
        source = places + tap_displacement
        inside = (source >= 0) & (source < row_count)
        same_window = jnp.roll(segment_ids, -tap_displacement) == segment_ids
        tap_valid.append((inside & same_window).astype(jnp.float32))
    return (live_rows, tap_valid)


def split_params(flat_params):
    return (
        flat_params[0:D],
        flat_params[D : 2 * D],
        flat_params[2 * D : 3 * D],
        flat_params[3 * D : 3 * D + FF],
        flat_params[3 * D + FF : 4 * D + FF],
        flat_params[4 * D + FF : 5 * D + FF],
        flat_params[5 * D + FF : 6 * D + FF],
    )


def branch_one(conv_sum, conv_bias, gain_one, shift_one):
    return layer_norm(jax.nn.gelu(conv_sum + conv_bias), gain_one, shift_one)


def branch_two(outer_sum, outer_bias, gain_two, shift_two):
    return layer_norm(outer_sum + outer_bias, gain_two, shift_two)


def fetch_forward(conv_weight, feedforward_input_weight, ffn_out, small_params):
    narrow_set = (
        lax.all_gather(conv_weight, "narrow", axis=2, tiled=True),
        lax.all_gather(feedforward_input_weight, "narrow", axis=1, tiled=True),
        lax.all_gather(ffn_out, "narrow", axis=1, tiled=True),
        lax.all_gather(small_params, "narrow", axis=0, tiled=True),
    )
    return (
        lax.all_gather(narrow_set[0], "wide", axis=1, tiled=True),
        lax.all_gather(narrow_set[1], "wide", axis=0, tiled=True),
        lax.all_gather(narrow_set[2], "wide", axis=0, tiled=True),
        lax.all_gather(narrow_set[3], "wide", axis=0, tiled=True),
    )


def shards(
    tokens, window_lengths, conv_weight, feedforward_input_weight, ffn_out, small_params, cotangent
):
    row_count = tokens.shape[0]
    block_size = min(512, row_count)
    live_rows, tap_valid = window_masks(window_lengths[0], row_count)
    weights = fetch_forward(conv_weight, feedforward_input_weight, ffn_out, small_params)
    conv_full, inner_full, outer_full = (weights[0], weights[1], weights[2])
    pieces = split_params(weights[3].astype(jnp.float32))
    start_rows = tokens * live_rows[:, None].astype(jnp.bfloat16)
    conv_sum = jnp.zeros((row_count, D), jnp.float32)
    for index_of_tap in range(KERNEL_TAPS):
        tap_displacement = (index_of_tap - KERNEL_TAPS // 2) * DILATION_STEP
        shifted = jnp.roll(start_rows, -tap_displacement, axis=0) * tap_valid[index_of_tap][
            :, None
        ].astype(jnp.bfloat16)
        conv_sum = conv_sum + jnp.dot(
            shifted, conv_full[index_of_tap], preferred_element_type=jnp.float32
        )
    branch_out, pull_one = jax.vjp(branch_one, conv_sum, pieces[0], pieces[1], pieces[2])
    residual_one = start_rows.astype(jnp.float32) + branch_out
    residual_low = residual_one.astype(jnp.bfloat16)
    outer_parts = []
    for first_row in range(0, row_count, block_size):
        inner_sum = (
            jnp.dot(
                residual_low[first_row : first_row + block_size],
                inner_full,
                preferred_element_type=jnp.float32,
            )
            + pieces[3]
        )
        active = jax.nn.gelu(inner_sum).astype(jnp.bfloat16)
        outer_parts.append(jnp.dot(active, outer_full, preferred_element_type=jnp.float32))
    outer_sum = jnp.concatenate(outer_parts, axis=0)
    normed, pull_two = jax.vjp(branch_two, outer_sum, pieces[4], pieces[5], pieces[6])
    block_out = (live_rows[:, None] * (residual_one + normed)).astype(jnp.bfloat16)
    upstream = cotangent.astype(jnp.float32) * live_rows[:, None]
    d_outer, d_outer_bias, d_gain_two, d_shift_two = pull_two(upstream)
    outer_low = d_outer.astype(jnp.bfloat16)
    grad_in = jnp.zeros((D, FF), jnp.float32)
    grad_out = jnp.zeros((FF, D), jnp.float32)
    inner_bias_grad = jnp.zeros((FF,), jnp.float32)
    resid_parts = []
    for first_row in range(0, row_count, block_size):
        rows_low = residual_low[first_row : first_row + block_size]
        outer_rows = outer_low[first_row : first_row + block_size]
        inner_sum = jnp.dot(rows_low, inner_full, preferred_element_type=jnp.float32) + pieces[3]
        active_full, pull_gelu = jax.vjp(jax.nn.gelu, inner_sum)
        active = active_full.astype(jnp.bfloat16)
        d_active = jnp.einsum(
            "rd,fd->rf", outer_rows, outer_full, preferred_element_type=jnp.float32
        )
        d_inner = pull_gelu(d_active)[0]
        inner_bias_grad = inner_bias_grad + jnp.sum(d_inner, axis=0)
        inner_low = d_inner.astype(jnp.bfloat16)
        grad_in = grad_in + jnp.einsum(
            "rd,rf->df", rows_low, inner_low, preferred_element_type=jnp.float32
        )
        grad_out = grad_out + jnp.einsum(
            "rf,rd->fd", active, outer_rows, preferred_element_type=jnp.float32
        )
        resid_parts.append(
            jnp.einsum("rf,df->rd", inner_low, inner_full, preferred_element_type=jnp.float32)
        )
    d_resid = upstream + jnp.concatenate(resid_parts, axis=0)
    d_conv, d_conv_bias, d_gain_one, d_shift_one = pull_one(d_resid)
    convolution_reduced = d_conv.astype(jnp.bfloat16)
    conv_grads = []
    d_start = d_resid
    for index_of_tap in range(KERNEL_TAPS):
        tap_displacement = (index_of_tap - KERNEL_TAPS // 2) * DILATION_STEP
        tap_mask = tap_valid[index_of_tap][:, None]
        shifted = jnp.roll(start_rows, -tap_displacement, axis=0) * tap_mask.astype(jnp.bfloat16)
        conv_grads.append(
            jnp.einsum(
                "ri,ro->io", shifted, convolution_reduced, preferred_element_type=jnp.float32
            )
        )
        back_rows = jnp.einsum(
            "ro,io->ri",
            convolution_reduced,
            conv_full[index_of_tap],
            preferred_element_type=jnp.float32,
        )
        d_start = d_start + jnp.roll(back_rows * tap_mask, tap_displacement, axis=0)
    grad_tokens = d_start * live_rows[:, None]
    convolution_weight_gradient = jnp.stack(conv_grads, axis=0)
    grad_flat = jnp.concatenate(
        [
            d_conv_bias,
            d_gain_one,
            d_shift_one,
            inner_bias_grad,
            d_outer_bias,
            d_gain_two,
            d_shift_two,
        ],
        axis=0,
    )
    wide_sums = (
        lax.psum_scatter(convolution_weight_gradient, "wide", scatter_dimension=1, tiled=True),
        lax.psum_scatter(grad_in, "wide", scatter_dimension=0, tiled=True),
        lax.psum_scatter(grad_out, "wide", scatter_dimension=0, tiled=True),
        lax.psum_scatter(grad_flat, "wide", scatter_dimension=0, tiled=True),
    )
    owned = (
        lax.psum_scatter(wide_sums[0], "narrow", scatter_dimension=2, tiled=True),
        lax.psum_scatter(wide_sums[1], "narrow", scatter_dimension=1, tiled=True),
        lax.psum_scatter(wide_sums[2], "narrow", scatter_dimension=1, tiled=True),
        lax.psum_scatter(wide_sums[3], "narrow", scatter_dimension=0, tiled=True),
    )
    owned_flat = owned[3]
    return (block_out, grad_tokens, owned[0], owned[1], owned[2], owned_flat)

MESH = pl.DeviceIdType.MESH
BF = jnp.bfloat16
F32 = jnp.float32
BLOCK = 256
REACH = KERNEL_TAPS // 2 * DILATION_STEP
STEP_ROWS = 512
GRAD_ROWS = 40
VMEM_LIMIT = 63 << 20
GELU_A = 0.7978845608028654
GELU_B = 0.044715
CONV_GATHER = (
    (0, 1, ('zxy', 'zyx')),
    (1, 4, ('zxy', 'zyx')),
    (4, 6, ('zxy', 'zyx')),
    (6, 9, ('xzy', 'yzx')),
)
INNER_GATHER = (('xzy', 'yzx'), ('zxy', 'zyx'))
OUTER_GATHER = (('zxy', 'zyx'), ('zxy', 'zyx'))
SCATTER = (
    ('FO0', 0, 1, 'yxz'),
    ('FO1', 1, 2, 'xzy'),
    ('FI0', 0, 2, 'yxz'),
    ('FI1', 2, 4, 'xzy'),
    ('C0a', 0, 2, 'yxz'),
    ('C0b', 9, 11, 'xyz'),
    ('C2a', 2, 4, 'yzx'),
    ('C2b', 11, 13, 'xzy'),
    ('C4a', 4, 5, 'yxz'),
    ('C4b', 13, 14, 'xyz'),
    ('C5a', 5, 7, 'yxz'),
    ('C5b', 14, 16, 'xyz'),
    ('C7a', 7, 9, 'yxz'),
    ('C7b', 16, 18, 'xyz'),
)
TAP_ORDER = (0,)
ORDER = (
    "c0a.0", "c0b.0", "c1a.0", "c1b.0", "c4a.0", "c4b.0", "c6a.0", "c6b.0", "fi0a.0", "fi0b.0", "pad",
    "fi1a.0", "fi1b.0", "P.0", "c6a.1", "c0a.1", "c0b.1", "P.1", "c1a.1", "c0a.2", "c0b.2", "c6b.1", "P.2",
    "c1b.1", "P.3", "c4a.1", "c0a.3", "c1a.2", "c0a.4", "c0b.3", "fi0a.1", "c1b.2", "c4b.1", "c0b.4", "conv0",
    "c4a.2", "fi0b.1", "fi1a.1", "c1a.3", "fi1b.1", "fo0a.0", "c4b.2", "c1a.4", "c6a.2", "fo0b.0", "c1b.3",
    "fo1a.0", "c1b.4", "conv1", "c4a.3", "c4b.3", "c6b.2", "fi1a.2", "fo1b.0", "c4a.4", "c4b.4", "conv4",
    "c6a.3", "fi0a.2", "fi1b.2", "c6a.4", "fi0b.2", "fi1a.3", "c6b.3", "fi1a.4", "fo0a.1", "fo0b.1", "c6b.4",
    "conv6", "fi0a.3", "fi1b.3", "fo1a.1", "fo1b.1", "epi0", "epi1", "fi0b.3", "fo0b.2", "fi0a.4", "fi1b.4",
    "epi2", "epi3", "epi4", "fi0b.4", "fo0a.2", "epi5", "inner0", "fo1a.2", "fo1b.2", "inner1", "inner2",
    "inner3", "inner4", "fo0b.3", "inner5", "fo0a.3", "inner6", "fo0b.4", "inner7", "fo0a.4", "fo1b.3",
    "inner8", "fo1a.3", "inner9", "fo1b.4", "inner10", "fo1a.4", "inner11", "outer0", "outer1", "outer2",
    "outer3", "outer4", "outer5", "og0", "og1", "FO0.0", "og2", "og3", "FO0.1", "FO1.0", "hid0", "hid1",
    "hid2", "FO1.1", "hid3", "hid4", "hid5", "hid6", "hid7", "hid8", "hid9", "hid10", "hid11", "ig0", "FO0.2",
    "ig1", "FI0.0", "ig2", "FO1.2", "ig3", "FI0.1", "FI1.0", "res0", "res1", "FO0.3", "FI1.1", "res2", "res3",
    "res4", "res5", "padb", "cg0", "FO1.3", "FI0.2", "cg1", "C0a.0", "C0b.0", "G.0", "cg2", "FI1.2", "C0a.1",
    "C0b.1", "cg3", "C2a.0", "C2b.0", "cg4", "C4a.0", "C4b.0", "C2a.1", "FI0.3", "C2b.1", "cg5", "C4a.1",
    "cg6", "C0a.2", "C5a.0", "C5b.0", "G.1", "cg7", "C0b.2", "C4b.1", "C5a.1", "C5b.1", "cg8", "C2a.2",
    "C7a.0", "C2b.2", "C7b.0", "tok0", "FI1.3", "C0a.3", "C4a.2", "C7a.1", "C7b.1", "G.2", "tok1", "C0b.3",
    "tok2", "tok3", "C4b.2", "C5a.2", "C5b.2", "tok4", "C2a.3", "C4a.3", "tok5", "tok6", "C2b.3", "C7a.2",
    "C7b.2", "C4b.3", "tok7", "C5a.3", "tok8", "C5b.3", "FO0.4", "G.3", "FO1.4", "FI0.4", "FI1.4", "C0a.4",
    "C2a.4", "C7a.3", "C7b.3", "C2b.4", "C0b.4", "C4a.4", "C4b.4", "C5a.4", "C5b.4", "C7a.4", "C7b.4",
)


def inbox_shapes(sizes, count, rows, axes):
    left = dict(zip("zxy", sizes))
    shapes = []
    for axis in axes:
        senders = left.pop(axis) - 1
        rest = tuple(left[name] for name in "yzx" if name in left)
        shapes.append((senders, count) + rest + (rows, 128))
    return shapes


class Links:
    def __init__(self, sizes, send_sems, recv_sems):
        self.Z, self.X, self.Y = sizes
        wide, narrow = lax.axis_index("wide"), lax.axis_index("narrow")
        self.z, self.x = wide // self.X, wide % self.X
        self.y, self.c = narrow // 2, narrow % 2
        self.send_sems, self.recv_sems = send_sems, recv_sems
        self.used = 0
        self.copies = []

    def device(self, axis, step):
        z, x, y, c = self.z, self.x, self.y, self.c
        if axis == "z":
            z = lax.rem(z + step, self.Z)
        elif axis == "x":
            x = lax.rem(x + step, self.X)
        elif axis == "y":
            y = lax.rem(y + step, self.Y)
        else:
            c = 1 - c
        return (z * self.X + x, y * 2 + c)

    def steps(self, axis):
        return range(1, {"z": self.Z, "x": self.X, "y": self.Y, "c": 2}[axis])

    def send(self, source, target, axis, step=1):
        index = self.used
        self.used += 1
        copy = pltpu.make_async_remote_copy(
            src_ref=source,
            dst_ref=target,
            send_sem=self.send_sems.at[index],
            recv_sem=self.recv_sems.at[index],
            device_id=self.device(axis, step),
            device_id_type=MESH,
        )
        copy.start()
        self.copies.append(copy)
        return copy

    def barrier(self):
        semaphore = pltpu.get_barrier_semaphore()
        partners = [self.device(axis, s) for axis in "zxyc" for s in self.steps(axis)]
        for partner in partners:
            pl.semaphore_signal(semaphore, inc=1, device_id=partner, device_id_type=MESH)
        pl.semaphore_wait(semaphore, len(partners))

    def finish(self):
        for copy in self.copies:
            copy.wait_send()


class Once:
    def __init__(self, copy):
        self.copy = copy

    def wait(self):
        if self.copy is not None:
            self.copy.wait()
        self.copy = None


class Gather:
    def __init__(self, links, shard, whole, own, taps, rows, axes):
        self.links, self.shard, self.whole, self.own = links, shard, whole, own
        self.taps, self.rows = pl.ds(taps[0], taps[1] - taps[0]), pl.ds(rows[0], rows[1] - rows[0])
        self.axes = axes + "c"
        self.stage = 0
        self.waits = []

    def region(self):
        k, done = self.links, self.axes[: self.stage]
        every = slice(None)
        y, z, x = (every if axis in done else at for axis, at in (("y", k.y), ("z", k.z), ("x", k.x)))
        return self.whole.at[self.taps, y, k.c, z, x, self.rows]

    def step(self):
        k = self.links
        for copy in self.waits:
            copy.wait_recv()
        if self.stage == len(self.axes):
            return
        target = self.region()
        source = target
        if self.stage == 0:
            source = self.shard.at[self.taps, self.rows]
        else:
            self.own.wait()
        axis = self.axes[self.stage]
        self.waits = [k.send(source, target, axis, s) for s in k.steps(axis)]
        self.stage += 1


class Scatter:
    def __init__(self, links, partial, pair, inboxes, parts, axes, finish):
        self.links, self.partial, self.pair, self.inboxes = links, partial, pair, inboxes
        self.parts = pl.ds(parts[0], parts[1] - parts[0])
        self.first, self.axes, self.finish = parts[0], axes, finish
        self.stage = 0

    def region(self, done, axis=None, at=None):
        k = self.links
        places = []
        for name, own in (("y", k.y), ("z", k.z), ("x", k.x)):
            places.append(at if name == axis else own if name in done else slice(None))
        return (self.parts, *places)

    def step(self):
        k, stage, pair = self.links, self.stage, self.pair
        self.stage += 1
        if stage == 0:
            self.waits = [k.send(self.partial.at[1 - k.c, self.parts], pair.at[self.parts], "c")]
            return
        for copy in self.waits:
            copy.wait_recv()
        held = self.region(self.axes[: stage - 1])
        if stage == 1:
            came = [self.partial[k.c, self.parts]]
        else:
            inbox = self.inboxes[stage - 2]
            came = [inbox[i] for i in range(inbox.shape[0])]
        if stage > len(self.axes):
            total = pair[held].astype(F32)
            for part in came:
                total = total + part.astype(F32)
            self.finish(total, self.first)
            return
        value = pair[held]
        for part in came:
            value = value + part
        pair[held] = value
        axis = self.axes[stage - 1]
        done = self.axes[: stage - 1]
        at, count = {"y": (k.y, k.Y), "z": (k.z, k.Z), "x": (k.x, k.X)}[axis]
        self.waits = [
            k.send(
                pair.at[self.region(done, axis, lax.rem(at + s, count))], self.inboxes[stage - 1].at[s - 1], axis, s
            )
            for s in k.steps(axis)
        ]


class Sharing:
    def __init__(self, share, take, held, got, axes):
        self.share, self.take, self.held, self.got, self.axes = share, take, held, got, axes
        self.stage = 0

    def send(self):
        self.copies = self.share(self.held.at[self.stage], self.got, self.axes[self.stage])

    def step(self):
        value = self.take(self.copies, self.held.at[self.stage], self.got, self.axes[self.stage])
        self.stage += 1
        self.held[self.stage] = value
        if self.stage < len(self.axes):
            self.send()


def gelu_pair(value):
    square = value * value
    bend = jnp.tanh(value * (GELU_A + (GELU_A * GELU_B) * square))
    share = 0.5 + 0.5 * bend
    slope = share + (0.5 * value) * ((1.0 - bend * bend) * (GELU_A + (3 * GELU_A * GELU_B) * square))
    return value * share, slope


def normalize(value):
    centre = value - jnp.mean(value, axis=-1, keepdims=True)
    factor = lax.rsqrt(jnp.mean(centre * centre, axis=-1, keepdims=True) + EPSILON)
    return centre * factor, factor


def normalize_back(grad, hat, factor):
    return factor * (
        grad
        - jnp.mean(grad, axis=-1, keepdims=True)
        - hat * jnp.mean(grad * hat, axis=-1, keepdims=True)
    )


def side_by_side(whole, tap):
    lanes = whole.shape[-1]
    return jnp.concatenate(
        [whole[tap, y, c].reshape(-1, lanes) for y in range(whole.shape[1]) for c in range(2)], axis=1
    )


def dot(left, right, over=((1,), (0,))):
    return lax.dot_general(left, right, (over, ((), ())), preferred_element_type=F32)


OVER_ROWS = ((0,), (0,))
OVER_LANES = ((1,), (1,))


def kernel(
    sizes, lengths, small_in, tokens, cotangent, conv_in, inner_in, outer_in,
    block_out, grad_tokens, conv_out, inner_out, outer_out, params_out,
    conv_w, inner_w, outer_w, params_got, params_sum,
    rows_buf, cot_buf, padded, padded_by8, padded_back, stage, conv_sum, resid, resid_low, active, slope, outer_low,
    conv_partial, inner_partial, outer_partial, conv_pair, inner_pair, outer_pair,
    grads, grads_got, send_sems, recv_sems, local_sems, *inboxes,
):
    k = Links(sizes, send_sems, recv_sems)
    Z, X, Y = sizes
    row_count = tokens.shape[0]
    blocks = row_count // BLOCK
    steps = row_count // STEP_ROWS
    per_step = STEP_ROWS // BLOCK

    def local(index, source, target):
        copy = pltpu.make_async_copy(source, target, local_sems.at[index])
        copy.start()
        return copy

    rows_in = local(0, tokens, rows_buf)
    own = [
        Once(local(1 + i, shard, whole.at[:, k.y, k.c, k.z, k.x]))
        for i, (shard, whole) in enumerate(((conv_in, conv_w), (inner_in, inner_w), (outer_in, outer_w)))
    ]
    cot_in = local(4, cotangent, cot_buf)
    k.barrier()

    bounds = []
    total = 0
    for slot in range(lengths.shape[1]):
        total = total + lengths[0, slot]
        bounds.append(total)

    def window(block):
        number = 0
        for bound in bounds:
            number = number + jnp.where(block * BLOCK >= bound, 1, 0)
        return number

    def live(block):
        return jnp.where(block * BLOCK < total, 1.0, 0.0).astype(F32)

    def joined(block):
        return jnp.where(window(block) == window(block + 1), 1.0, 0.0).astype(F32) * live(block)

    def pad(source, target, target_by8):
        for b in range(blocks):
            at = b * BLOCK
            if b > 0:
                stage[0:REACH] = source[at - REACH : at].astype(F32) * joined(b - 1)
            else:
                stage[0:REACH] = jnp.zeros((REACH, D), F32)
            stage[REACH : REACH + BLOCK] = source[at : at + BLOCK].astype(F32) * live(b)
            if b < blocks - 1:
                stage[REACH + BLOCK :] = source[at + BLOCK : at + BLOCK + REACH].astype(F32) * joined(b)
            else:
                stage[REACH + BLOCK :] = jnp.zeros((REACH, D), F32)
            target[b] = stage[...].astype(BF)
            target_by8[b] = stage[8 : BLOCK + 2 * REACH - 8].astype(BF)

    def window_rows(source, source_by8, block, place):
        if place % 2 == 0:
            return source[block, pl.ds(8 * place, BLOCK), :]
        return source_by8[block, pl.ds(8 * (place - 1), BLOCK), :]

    def step_rows(source, source_by8, step, place):
        return jnp.concatenate(
            [window_rows(source, source_by8, step * per_step + j, place) for j in range(per_step)], axis=0
        )

    def all_rows(source, source_by8, place):
        return jnp.concatenate([window_rows(source, source_by8, b, place) for b in range(blocks)], axis=0)

    def at_step(step):
        return pl.ds(pl.multiple_of(step * STEP_ROWS, STEP_ROWS), STEP_ROWS)

    def live_rows(value, step):
        return jnp.concatenate(
            [value[j * BLOCK : (j + 1) * BLOCK] * live(step * per_step + j) for j in range(per_step)], axis=0
        )

    def param(first, width):
        return jnp.concatenate(
            [params_sum[4, pl.ds((first + i) // 128, 1), :] for i in range(0, width, 128)], axis=1
        )

    def add_grad(first, value):
        summed = jnp.sum(value, axis=0, keepdims=True)
        for i in range(0, summed.shape[1], 128):
            row = (first + i) // 128
            grads[0, row : row + 1, :] = grads[0, row : row + 1, :] + summed[:, i : i + 128]

    CONV_BIAS, GAIN_ONE, SHIFT_ONE, INNER_BIAS = 0, D, 2 * D, 3 * D
    OUTER_BIAS, GAIN_TWO, SHIFT_TWO = 3 * D + FF, 4 * D + FF, 5 * D + FF

    slot_at = {"z": 0, "x": Z - 1, "y": Z + X - 2, "c": Z + X + Y - 3}

    def own_params():
        count = small_in.shape[0]
        start = ((k.z * X + k.x) * 2 * Y + k.y * 2 + k.c) * count
        row = small_in[...].astype(F32).reshape(1, count)
        row = jnp.concatenate([row, jnp.zeros((1, 256 - count), F32)], axis=1)
        row = pltpu.roll(jnp.broadcast_to(row, (8, 256)), start % 128, 1)
        params_sum[0] = jnp.zeros((GRAD_ROWS, 128), F32)
        params_sum[0, pl.ds(start // 128, 1), :] = row[0:1, :128]
        params_sum[0, pl.ds(start // 128 + 1, 1), :] = row[0:1, 128:]

    def share(source, got, axis):
        return [k.send(source, got.at[slot_at[axis] + s - 1], axis, s) for s in k.steps(axis)]

    def take(copies, source, got, axis):
        for copy in copies:
            copy.wait_recv()
        value = source[...]
        for s in k.steps(axis):
            value = value + got[slot_at[axis] + s - 1]
        return value

    def block_rows(block):
        return pl.ds(block * BLOCK, BLOCK)

    def conv_taps(first):
        last = {piece[0]: piece[1] for piece in CONV_GATHER}[first]

        @pl.loop(0, steps)
        def _(step):
            value = None
            for tap in range(first, last):
                term = dot(step_rows(padded, padded_by8, step, tap), side_by_side(conv_w, tap))
                value = term if value is None else value + term
            if first != TAP_ORDER[0]:
                value = value + conv_sum[at_step(step), :]
            conv_sum[at_step(step), :] = value

    def conv_end(block):
        rows = block_rows(block)
        value = conv_sum[rows, :] + param(CONV_BIAS, D)
        conv_sum[rows, :] = value
        hat, _ = normalize(gelu_pair(value)[0])
        start = window_rows(padded, padded_by8, block, REACH // 8).astype(F32)
        value = start + hat * param(GAIN_ONE, D) + param(SHIFT_ONE, D)
        resid[rows, :] = value
        resid_low[rows, :] = value.astype(BF)

    width = inner_w.shape[-1]
    groups = Y * 2

    def inner_piece(piece):
        step, group = piece // groups, piece % groups
        rows, first = pl.ds(step * STEP_ROWS, STEP_ROWS), group * width
        value = dot(resid_low[rows, :], inner_w[0, group // 2, group % 2].reshape(D, width))
        bent, tilt = gelu_pair(value + param(INNER_BIAS + first, width))
        active[rows, first : first + width] = bent.astype(BF)
        slope[rows, first : first + width] = tilt.astype(BF)

    def outer_block(block):
        rows = block_rows(block)
        value = dot(active[rows, :], side_by_side(outer_w, 0)) + param(OUTER_BIAS, D)
        hat, factor = normalize(value)
        gain = param(GAIN_TWO, D)
        result = resid[rows, :] + hat * gain + param(SHIFT_TWO, D)
        rows_buf[rows, :] = (result * live(block)).astype(BF)
        upstream = cot_buf[rows, :].astype(F32) * live(block)
        back = normalize_back(upstream * gain, hat, factor)
        outer_low[rows, :] = back.astype(BF)
        add_grad(OUTER_BIAS, back)
        add_grad(GAIN_TWO, upstream * hat)
        add_grad(SHIFT_TWO, upstream)

    outer_rows = outer_w.shape[5]

    def outer_grad(piece):
        half, y = piece // Y, piece % Y
        size = outer_rows // 2
        left = jnp.concatenate(
            [active[:, i * outer_rows + half * size : i * outer_rows + (half + 1) * size] for i in range(Z * X)],
            axis=1,
        )
        value = dot(left, outer_low[:, y * 256 : (y + 1) * 256], OVER_ROWS).astype(BF)
        for c in range(2):
            outer_partial[c, half, y] = value[:, c * 128 : (c + 1) * 128].reshape(Z, X, size, 128)

    def hidden_piece(piece):
        step, group = piece // groups, piece % groups
        rows, first = pl.ds(step * STEP_ROWS, STEP_ROWS), group * width
        right = jnp.concatenate(
            [outer_w[0, y, c, group].reshape(width, 128) for y in range(Y) for c in range(2)], axis=1
        )
        value = dot(outer_low[rows, :], right, OVER_LANES) * slope[rows, first : first + width].astype(F32)
        add_grad(INNER_BIAS + first, value)
        slope[rows, first : first + width] = value.astype(BF)

    def inner_grad(piece):
        right = jnp.concatenate(
            [slope[:, g * width + piece * 128 : g * width + (piece + 1) * 128] for g in range(groups)], axis=1
        )
        value = dot(resid_low[...], right, OVER_ROWS).astype(BF)
        for g in range(groups):
            part = value[:, g * 128 : (g + 1) * 128]
            inner_partial[g % 2, piece, g // 2] = part.reshape(Z, X, D // (Z * X), 128)

    def resid_block(block):
        rows = block_rows(block)
        value = cot_buf[rows, :].astype(F32) * live(block)
        for g in range(groups):
            right = inner_w[0, g // 2, g % 2].reshape(D, width)
            value = value + dot(slope[rows, g * width : (g + 1) * width], right, OVER_LANES)
        resid[rows, :] = value
        bent, tilt = gelu_pair(conv_sum[rows, :])
        hat, factor = normalize(bent)
        add_grad(GAIN_ONE, value * hat)
        add_grad(SHIFT_ONE, value)
        back = normalize_back(value * param(GAIN_ONE, D), hat, factor) * tilt
        add_grad(CONV_BIAS, back)
        conv_sum[rows, :] = back

    conv_rows = conv_w.shape[5]

    def conv_grad(tap):
        left = all_rows(padded, None, REACH // 8)
        right = all_rows(padded_back, padded_by8, KERNEL_TAPS - 1 - tap)
        value = dot(left, right, OVER_ROWS).astype(BF)
        size = conv_rows // 2
        for g in range(groups):
            part = value[:, g * 128 : (g + 1) * 128].reshape(Z, X, conv_rows, 128)
            for half in range(2):
                conv_partial[g % 2, half * KERNEL_TAPS + tap, g // 2] = part[:, :, half * size : (half + 1) * size]

    def token_piece(piece):
        step, part = piece // 3, piece % 3
        rows = pl.ds(step * STEP_ROWS, STEP_ROWS)
        value = resid[rows, :]
        for tap in range(part * KERNEL_TAPS // 3, (part + 1) * KERNEL_TAPS // 3):
            value = value + dot(
                step_rows(padded_back, padded_by8, step, KERNEL_TAPS - 1 - tap),
                side_by_side(conv_w, tap),
                OVER_LANES,
            )
        if part == 2:
            value = live_rows(value, step)
        resid[rows, :] = value

    def conv_finish(value, first):
        half, tap = first // KERNEL_TAPS, first % KERNEL_TAPS
        size = conv_rows // 2
        conv_out[pl.ds(tap, value.shape[0]), pl.ds(half * size, size), :] = value

    def inner_finish(value, first):
        for i in range(value.shape[0]):
            inner_out[:, (first + i) * 128 : (first + i + 1) * 128] = value[i]

    def outer_finish(value, first):
        size = outer_rows // 2
        outer_out[first * size : first * size + value.shape[0] * size, :] = value.reshape(-1, 128)

    params_sharing = Sharing(share, take, params_sum, params_got, "zxyc")
    grads_sharing = Sharing(share, take, grads, grads_got, "cxyz")

    moves = {}
    for half in range(2):
        for first, last, axes in CONV_GATHER:
            size = conv_w.shape[5] // 2
            rows = (half * size, (half + 1) * size)
            piece = Gather(k, conv_in, conv_w, own[0], (first, last), rows, axes[half])
            moves["c" + str(first) + "ab"[half]] = piece
        for name, shard, whole, copied, kinds in (
            ("fi", inner_in, inner_w, own[1], INNER_GATHER),
            ("fo", outer_in, outer_w, own[2], OUTER_GATHER),
        ):
            size = whole.shape[5] // (2 * len(kinds))
            for i, axes in enumerate(kinds):
                at = (half * len(kinds) + i) * size
                moves[name + str(i) + "ab"[half]] = Gather(k, shard, whole, copied, (0, 1), (at, at + size), axes[half])
    for i, (name, first, last, axes) in enumerate(SCATTER):
        partial, pair, finish = {
            "C": (conv_partial, conv_pair, conv_finish),
            "FI": (inner_partial, inner_pair, inner_finish),
            "FO": (outer_partial, outer_pair, outer_finish),
        }[name.rstrip("0123456789ab")]
        moves[name] = Scatter(k, partial, pair, inboxes[3 * i : 3 * i + 3], (first, last), axes, finish)
    moves["P"] = params_sharing
    moves["G"] = grads_sharing

    def pad_tokens(_):
        rows_in.wait()
        grads[0] = jnp.zeros((GRAD_ROWS, 128), F32)
        pad(rows_buf, padded, padded_by8)

    def pad_back(_):
        pad(conv_sum, padded_back, padded_by8)

    work = {
        "pad": pad_tokens,
        "conv": conv_taps,
        "epi": conv_end,
        "inner": inner_piece,
        "outer": outer_block,
        "og": outer_grad,
        "hid": hidden_piece,
        "ig": inner_grad,
        "res": resid_block,
        "padb": pad_back,
        "cg": conv_grad,
        "tok": token_piece,
    }
    out_copies = []
    own_params()
    params_sharing.send()
    for name in ORDER:
        if name == "outer0":
            cot_in.wait()
        if "." in name:
            moves[name.split(".")[0]].step()
        else:
            kind = name.rstrip("0123456789")
            work[kind](int(name[len(kind) :] or 0))
        if name == "res5":
            grads_sharing.send()
        if name == "outer5":
            out_copies.append(local(0, rows_buf, block_out))
        if name in ("tok2", "tok5", "tok8"):
            rows = pl.ds((int(name[3:]) // 3) * STEP_ROWS, STEP_ROWS)
            out_copies.append(local(5 + int(name[3:]) // 3, resid.at[rows], grad_tokens.at[rows]))
    params_out[...] = grads[4]
    for copy in out_copies:
        copy.wait()
    k.finish()


def run_kernel(sizes, lengths, small, tokens, cotangent, conv_shard, inner_shard, outer_shard):
    Z, X, Y = sizes
    taps, conv_rows, lanes = conv_shard.shape
    inner_rows, width = inner_shard.shape
    outer_rows = outer_shard.shape[0]
    rows = tokens.shape[0]
    blocks = rows // BLOCK
    inner_shard, outer_shard = inner_shard[None], outer_shard[None]

    def whole(shard):
        return pltpu.VMEM((shard.shape[0], Y, 2, Z, X) + shard.shape[1:], BF)

    def pair(count, r):
        return pltpu.VMEM((count, Y, Z, X, r, 128), BF)

    def partial(count, r):
        return pltpu.VMEM((2, count, Y, Z, X, r, 128), BF)

    rows_of = {"C": conv_rows // 2, "FI": inner_rows, "FO": outer_rows // 2}
    parts_of = {"C": 2 * taps, "FI": width // 128, "FO": 2}
    inboxes = []
    for name, first, last, axes in SCATTER:
        r = rows_of[name.rstrip("0123456789ab")]
        inboxes += [pltpu.VMEM(shape, BF) for shape in inbox_shapes(sizes, last - first, r, axes)]
    partners = Z - 1 + X - 1 + Y - 1 + 1
    copies = 40 * (partners + 1)
    padded = BLOCK + 2 * REACH
    scratch = [whole(conv_shard), whole(inner_shard), whole(outer_shard)]
    scratch += [pltpu.VMEM((partners, GRAD_ROWS, 128), F32), pltpu.VMEM((5, GRAD_ROWS, 128), F32)]
    scratch += [
        pltpu.VMEM((rows, D), BF),
        pltpu.VMEM((rows, D), BF),
        pltpu.VMEM((blocks, padded, D), BF),
        pltpu.VMEM((blocks, padded - 16, D), BF),
        pltpu.VMEM((blocks, padded, D), BF),
        pltpu.VMEM((padded, D), F32),
        pltpu.VMEM((rows, D), F32),
        pltpu.VMEM((rows, D), F32),
        pltpu.VMEM((rows, D), BF),
        pltpu.VMEM((rows, FF), BF),
        pltpu.VMEM((rows, FF), BF),
        pltpu.VMEM((rows, D), BF),
    ]
    scratch += [partial(parts_of[name], rows_of[name]) for name in ("C", "FI", "FO")]
    scratch += [pair(parts_of[name], rows_of[name]) for name in ("C", "FI", "FO")]
    scratch += [pltpu.VMEM((5, GRAD_ROWS, 128), F32), pltpu.VMEM((partners, GRAD_ROWS, 128), F32)]
    scratch += [pltpu.SemaphoreType.DMA((copies,)), pltpu.SemaphoreType.DMA((copies,)), pltpu.SemaphoreType.DMA((8,))]
    scratch += inboxes
    far = pl.BlockSpec(memory_space=pl.ANY)
    near = pl.BlockSpec(memory_space=pltpu.VMEM)
    return pl.pallas_call(
        functools.partial(kernel, sizes),
        out_shape=[
            jax.ShapeDtypeStruct((rows, D), BF),
            jax.ShapeDtypeStruct((rows, D), F32),
            jax.ShapeDtypeStruct(conv_shard.shape, F32),
            jax.ShapeDtypeStruct(inner_shard.shape[1:], F32),
            jax.ShapeDtypeStruct(outer_shard.shape[1:], F32),
            jax.ShapeDtypeStruct((GRAD_ROWS, 128), F32),
        ],
        in_specs=[pl.BlockSpec(memory_space=pltpu.SMEM), near] + [far] * 5,
        out_specs=[far, far, near, near, near, near],
        scratch_shapes=scratch,
        compiler_params=pltpu.CompilerParams(
            collective_id=0, has_side_effects=True, vmem_limit_bytes=VMEM_LIMIT
        ),
    )(lengths, small, tokens, cotangent, conv_shard, inner_shard, outer_shard)


def hand_over(parts, grads, *refs):
    count = len(parts)
    sources, targets, small = refs[:count], refs[count : 2 * count], refs[2 * count]
    held, grads_held, sems = refs[2 * count + 1 : 3 * count + 1], refs[-2], refs[-1]
    first = pltpu.make_async_copy(grads, grads_held, sems.at[0, sum(parts)])
    pieces = []
    for source, target, middle, count in zip(sources, targets, held, parts):
        size = source.shape[0] // count
        pieces += [tuple(ref.at[pl.ds(i * size, size)] for ref in (source, middle, target)) for i in range(count)]
    ins = [pltpu.make_async_copy(s, m, sems.at[0, i]) for i, (s, m, _) in enumerate(pieces)]
    outs = [pltpu.make_async_copy(m, t, sems.at[1, i]) for i, (_, m, t) in enumerate(pieces)]
    for copy in ins:
        copy.start()
    first.start()
    for come, go in zip(ins, outs):
        come.wait()
        go.start()
    first.wait()
    size = small.shape[0]
    start = (lax.axis_index("wide") * lax.axis_size("narrow") + lax.axis_index("narrow")) * size
    row = jnp.concatenate([grads_held[pl.ds(start // 128, 1), :], grads_held[pl.ds(start // 128 + 1, 1), :]], axis=1)
    row = pltpu.roll(jnp.broadcast_to(row, (8, 256)), 256 - start % 128, 1)
    small[...] = row[0:1, :size].reshape(size)
    for copy in outs:
        copy.wait()


def settle(share, params_grad, arrays):
    far = pl.BlockSpec(memory_space=pl.ANY)
    near = pl.BlockSpec(memory_space=pltpu.VMEM)
    parts = [max(1, a.size * a.dtype.itemsize >> 19) for a in arrays]
    return pl.pallas_call(
        functools.partial(hand_over, parts),
        out_shape=[jax.ShapeDtypeStruct(a.shape, a.dtype) for a in arrays] + [jax.ShapeDtypeStruct((share,), F32)],
        in_specs=[far] * (len(arrays) + 1),
        out_specs=[far] * len(arrays) + [near],
        scratch_shapes=[pltpu.VMEM(a.shape, a.dtype) for a in arrays]
        + [pltpu.VMEM(params_grad.shape, F32), pltpu.SemaphoreType.DMA((2, sum(parts) + 1))],
        compiler_params=pltpu.CompilerParams(vmem_limit_bytes=VMEM_LIMIT),
    )(params_grad, *arrays)


def fused(
    sizes, tokens, window_lengths, conv_weight, feedforward_input_weight, ffn_out, small_params, cotangent
):
    block_out, grad_tokens, conv_grad, inner_grad, outer_grad, params_grad = run_kernel(
        sizes, window_lengths, small_params, tokens, cotangent, conv_weight, feedforward_input_weight, ffn_out
    )
    return settle(small_params.shape[0], params_grad, [block_out, grad_tokens, conv_grad, inner_grad, outer_grad])


def solution(mesh):
    wide, narrow = mesh.shape["wide"], mesh.shape["narrow"]
    Y = X = narrow // 2
    sizes = (wide // X, X, Y)

    def step(*arrays):
        rows = arrays[0].shape[0]
        inner, outer = arrays[3].shape, arrays[4].shape
        whole_lanes = all(a.shape[-1] % 128 == 0 for a in arrays[2:5])
        fits = rows == 3 * STEP_ROWS and narrow == 4 and inner[1] == X * outer[0] and whole_lanes
        small = arrays[5].shape[0]
        fits = fits and small % 32 == 0 and small <= 160
        if fits and wide % X == 0:
            return fused(sizes, *arrays)
        return shards(*arrays)

    return jax.shard_map(
        step,
        mesh=mesh,
        in_specs=(
            P(("wide", "narrow"), None),
            P(("wide", "narrow"), None),
            P(None, "wide", "narrow"),
            P("wide", "narrow"),
            P("wide", "narrow"),
            P(("wide", "narrow")),
            P(("wide", "narrow"), None),
        ),
        out_specs=(
            P(("wide", "narrow"), None),
            P(("wide", "narrow"), None),
            P(None, "wide", "narrow"),
            P("wide", "narrow"),
            P("wide", "narrow"),
            P(("wide", "narrow")),
        ),
        check_vma=False,
    )
```

```python
import functools

import jax
import jax.numpy as jnp
from jax import lax
from jax.experimental import pallas as pl
from jax.experimental.pallas import tpu as pltpu
from jax.sharding import PartitionSpec as P

D = 512
FF = 2048
KERNEL_TAPS = 9
DILATION_STEP = 8
EPSILON = 1e-05

def layer_norm(values, norm_gain, norm_shift):
    centre = values - jnp.mean(values, axis=-1, keepdims=True)
    spread = jnp.mean(centre * centre, axis=-1, keepdims=True)
    return centre * lax.rsqrt(spread + EPSILON) * norm_gain + norm_shift


def window_masks(lengths, row_count):
    bounds = jnp.cumsum(lengths)
    places = jnp.arange(row_count, dtype=jnp.int32)
    segment_ids = jnp.sum((places[:, None] >= bounds[None, :]).astype(jnp.int32), axis=1)
    live_rows = (places < bounds[-1]).astype(jnp.float32)
    tap_valid = []
    for index_of_tap in range(KERNEL_TAPS):
        tap_displacement = (index_of_tap - KERNEL_TAPS // 2) * DILATION_STEP
        source = places + tap_displacement
        inside = (source >= 0) & (source < row_count)
        same_window = jnp.roll(segment_ids, -tap_displacement) == segment_ids
        tap_valid.append((inside & same_window).astype(jnp.float32))
    return (live_rows, tap_valid)


def split_params(flat_params):
    return (
        flat_params[0:D],
        flat_params[D : 2 * D],
        flat_params[2 * D : 3 * D],
        flat_params[3 * D : 3 * D + FF],
        flat_params[3 * D + FF : 4 * D + FF],
        flat_params[4 * D + FF : 5 * D + FF],
        flat_params[5 * D + FF : 6 * D + FF],
    )


def branch_one(conv_sum, conv_bias, gain_one, shift_one):
    return layer_norm(jax.nn.gelu(conv_sum + conv_bias), gain_one, shift_one)


def branch_two(outer_sum, outer_bias, gain_two, shift_two):
    return layer_norm(outer_sum + outer_bias, gain_two, shift_two)


def fetch_forward(conv_weight, feedforward_input_weight, ffn_out, small_params):
    narrow_set = (
        lax.all_gather(conv_weight, "narrow", axis=2, tiled=True),
        lax.all_gather(feedforward_input_weight, "narrow", axis=1, tiled=True),
        lax.all_gather(ffn_out, "narrow", axis=1, tiled=True),
        lax.all_gather(small_params, "narrow", axis=0, tiled=True),
    )
    return (
        lax.all_gather(narrow_set[0], "wide", axis=1, tiled=True),
        lax.all_gather(narrow_set[1], "wide", axis=0, tiled=True),
        lax.all_gather(narrow_set[2], "wide", axis=0, tiled=True),
        lax.all_gather(narrow_set[3], "wide", axis=0, tiled=True),
    )


def shards(
    tokens, window_lengths, conv_weight, feedforward_input_weight, ffn_out, small_params, cotangent
):
    row_count = tokens.shape[0]
    block_size = min(512, row_count)
    live_rows, tap_valid = window_masks(window_lengths[0], row_count)
    weights = fetch_forward(conv_weight, feedforward_input_weight, ffn_out, small_params)
    conv_full, inner_full, outer_full = (weights[0], weights[1], weights[2])
    pieces = split_params(weights[3].astype(jnp.float32))
    start_rows = tokens * live_rows[:, None].astype(jnp.bfloat16)
    conv_sum = jnp.zeros((row_count, D), jnp.float32)
    for index_of_tap in range(KERNEL_TAPS):
        tap_displacement = (index_of_tap - KERNEL_TAPS // 2) * DILATION_STEP
        shifted = jnp.roll(start_rows, -tap_displacement, axis=0) * tap_valid[index_of_tap][
            :, None
        ].astype(jnp.bfloat16)
        conv_sum = conv_sum + jnp.dot(
            shifted, conv_full[index_of_tap], preferred_element_type=jnp.float32
        )
    branch_out, pull_one = jax.vjp(branch_one, conv_sum, pieces[0], pieces[1], pieces[2])
    residual_one = start_rows.astype(jnp.float32) + branch_out
    residual_low = residual_one.astype(jnp.bfloat16)
    outer_parts = []
    for first_row in range(0, row_count, block_size):
        inner_sum = (
            jnp.dot(
                residual_low[first_row : first_row + block_size],
                inner_full,
                preferred_element_type=jnp.float32,
            )
            + pieces[3]
        )
        active = jax.nn.gelu(inner_sum).astype(jnp.bfloat16)
        outer_parts.append(jnp.dot(active, outer_full, preferred_element_type=jnp.float32))
    outer_sum = jnp.concatenate(outer_parts, axis=0)
    normed, pull_two = jax.vjp(branch_two, outer_sum, pieces[4], pieces[5], pieces[6])
    block_out = (live_rows[:, None] * (residual_one + normed)).astype(jnp.bfloat16)
    upstream = cotangent.astype(jnp.float32) * live_rows[:, None]
    d_outer, d_outer_bias, d_gain_two, d_shift_two = pull_two(upstream)
    outer_low = d_outer.astype(jnp.bfloat16)
    grad_in = jnp.zeros((D, FF), jnp.float32)
    grad_out = jnp.zeros((FF, D), jnp.float32)
    inner_bias_grad = jnp.zeros((FF,), jnp.float32)
    resid_parts = []
    for first_row in range(0, row_count, block_size):
        rows_low = residual_low[first_row : first_row + block_size]
        outer_rows = outer_low[first_row : first_row + block_size]
        inner_sum = jnp.dot(rows_low, inner_full, preferred_element_type=jnp.float32) + pieces[3]
        active_full, pull_gelu = jax.vjp(jax.nn.gelu, inner_sum)
        active = active_full.astype(jnp.bfloat16)
        d_active = jnp.einsum(
            "rd,fd->rf", outer_rows, outer_full, preferred_element_type=jnp.float32
        )
        d_inner = pull_gelu(d_active)[0]
        inner_bias_grad = inner_bias_grad + jnp.sum(d_inner, axis=0)
        inner_low = d_inner.astype(jnp.bfloat16)
        grad_in = grad_in + jnp.einsum(
            "rd,rf->df", rows_low, inner_low, preferred_element_type=jnp.float32
        )
        grad_out = grad_out + jnp.einsum(
            "rf,rd->fd", active, outer_rows, preferred_element_type=jnp.float32
        )
        resid_parts.append(
            jnp.einsum("rf,df->rd", inner_low, inner_full, preferred_element_type=jnp.float32)
        )
    d_resid = upstream + jnp.concatenate(resid_parts, axis=0)
    d_conv, d_conv_bias, d_gain_one, d_shift_one = pull_one(d_resid)
    convolution_reduced = d_conv.astype(jnp.bfloat16)
    conv_grads = []
    d_start = d_resid
    for index_of_tap in range(KERNEL_TAPS):
        tap_displacement = (index_of_tap - KERNEL_TAPS // 2) * DILATION_STEP
        tap_mask = tap_valid[index_of_tap][:, None]
        shifted = jnp.roll(start_rows, -tap_displacement, axis=0) * tap_mask.astype(jnp.bfloat16)
        conv_grads.append(
            jnp.einsum(
                "ri,ro->io", shifted, convolution_reduced, preferred_element_type=jnp.float32
            )
        )
        back_rows = jnp.einsum(
            "ro,io->ri",
            convolution_reduced,
            conv_full[index_of_tap],
            preferred_element_type=jnp.float32,
        )
        d_start = d_start + jnp.roll(back_rows * tap_mask, tap_displacement, axis=0)
    grad_tokens = d_start * live_rows[:, None]
    convolution_weight_gradient = jnp.stack(conv_grads, axis=0)
    grad_flat = jnp.concatenate(
        [
            d_conv_bias,
            d_gain_one,
            d_shift_one,
            inner_bias_grad,
            d_outer_bias,
            d_gain_two,
            d_shift_two,
        ],
        axis=0,
    )
    wide_sums = (
        lax.psum_scatter(convolution_weight_gradient, "wide", scatter_dimension=1, tiled=True),
        lax.psum_scatter(grad_in, "wide", scatter_dimension=0, tiled=True),
        lax.psum_scatter(grad_out, "wide", scatter_dimension=0, tiled=True),
        lax.psum_scatter(grad_flat, "wide", scatter_dimension=0, tiled=True),
    )
    owned = (
        lax.psum_scatter(wide_sums[0], "narrow", scatter_dimension=2, tiled=True),
        lax.psum_scatter(wide_sums[1], "narrow", scatter_dimension=1, tiled=True),
        lax.psum_scatter(wide_sums[2], "narrow", scatter_dimension=1, tiled=True),
        lax.psum_scatter(wide_sums[3], "narrow", scatter_dimension=0, tiled=True),
    )
    owned_flat = owned[3]
    return (block_out, grad_tokens, owned[0], owned[1], owned[2], owned_flat)

MESH = pl.DeviceIdType.MESH
BF = jnp.bfloat16
F32 = jnp.float32
BLOCK = 256
REACH = KERNEL_TAPS // 2 * DILATION_STEP
STEP_ROWS = 512
GRAD_ROWS = 40
VMEM_LIMIT = 63 << 20
SEND_SLOTS = 40
GELU_A = 0.7978845608028654
GELU_B = 0.044715
CONV_GATHER = (
    (0, 1, ('hxly', 'hylx')),
    (1, 3, ('hlxy', 'hlyx')),
    (3, 6, ('hxly', 'hylx')),
    (6, 9, ('hxly', 'hylx')),
)
INNER_GATHER = (('hylx', 'hxly'), ('hxly', 'hylx'))
OUTER_GATHER = (('hxly', 'hylx'), ('lxhy', 'lyhx'))
SCATTER = (
    ('FO0', 0, 1, 'ylhx'),
    ('FO1', 1, 2, 'xlyh'),
    ('FI0', 0, 1, 'xylh'),
    ('FI1', 1, 2, 'yxlh'),
    ('FI2', 2, 3, 'yxlh'),
    ('FI3', 3, 4, 'xlhy'),
    ('C0a', 0, 2, 'ylxh'),
    ('C0b', 9, 11, 'xlyh'),
    ('C2a', 2, 4, 'ylxh'),
    ('C2b', 11, 13, 'xlyh'),
    ('C4a', 4, 6, 'ylxh'),
    ('C4b', 13, 15, 'xlyh'),
    ('C6a', 6, 8, 'xylh'),
    ('C6b', 15, 17, 'yxlh'),
    ('C8a', 8, 9, 'xyhl'),
    ('C8b', 17, 18, 'yxhl'),
)
TAP_ORDER = (0,)
ORDER = (
    "c0a.0", "c1b.0", "fo1a.0", "c1a.0", "c0b.0", "c3a.0", "pad", "c0a.1", "c3b.0", "P.0", "fo1a.1", "fo1b.0",
    "c6b.0", "ups0", "c1a.1", "fi0b.0", "c1b.1", "c6a.0", "c0b.1", "c3a.1", "P.1", "c0a.2", "ups1", "c3b.1",
    "fi0a.0", "c0b.2", "c6b.1", "c1a.2", "fi1b.0", "c3a.2", "c1b.2", "fi1a.0", "fi0b.1", "c6a.1", "P.2",
    "c0a.3", "c3b.2", "c0b.3", "c1a.3", "ups2", "fo0b.0", "c6b.2", "fi0a.1", "c1b.3", "fi1b.1", "c3a.3",
    "c6a.2", "c0b.4", "fi1a.1", "fo0a.0", "c3b.3", "ups3", "c0b.5", "fo1b.1", "fo0b.1", "fi0b.2", "c1a.4",
    "fi1b.2", "c0a.4", "c1b.4", "fi0a.2", "fi1a.2", "P.3", "c0a.5", "fo1a.2", "c6a.3", "ups4", "ups5",
    "c1a.5", "c6b.3", "conv0", "fi0b.3", "c1b.5", "c3a.4", "c3b.4", "conv1", "c3a.5", "c3b.5", "fo0b.2",
    "fo1b.2", "fo0a.1", "fi1b.3", "conv3", "c6a.4", "fi1a.3", "c6b.4", "fi0a.3", "c6a.5", "fo0a.2", "c6b.5",
    "fo1a.3", "fo0b.3", "P.4", "conv6", "epi0", "fi0b.4", "fi1b.4", "fo0a.3", "fi1a.4", "fo1b.3", "fi0a.4",
    "epi1", "epi2", "epi3", "epi4", "epi5", "fi0b.5", "fo0b.4", "fo1a.4", "fi1b.5", "fi0a.5", "fi1a.5",
    "inner0", "inner1", "fo1a.5", "fo0a.4", "fo1b.4", "fo0b.5", "inner2", "fo0a.5", "fo1b.5", "op0", "outer0",
    "outer1", "outer2", "outer3", "outer4", "outer5", "og0", "og1", "og2", "og3", "FO1.0", "FO0.0", "hid0",
    "hid1", "hid2", "hid3", "hid4", "hid5", "hid6", "hid7", "FO1.1", "FO0.1", "hid8", "hid9", "hid10",
    "hid11", "ig0", "ig1", "ig2", "FI0.0", "ig3", "res0", "FI2.0", "FI0.1", "FI3.0", "res1", "res2", "FI1.0",
    "FI2.1", "FO1.2", "FI3.1", "res3", "res4", "res5", "FO0.2", "FI1.1", "padb", "cg0", "cg1", "C0a.0",
    "C0b.0", "G.0", "FO1.3", "FI2.2", "cg2", "FI3.2", "C0b.1", "C0a.1", "cg3", "C2b.0", "FO0.3", "cg4", "cg5",
    "FI2.3", "C4a.0", "FI0.2", "FI1.2", "FO1.4", "C2b.1", "cg6", "C4a.1", "cg7", "C0a.2", "C4b.0", "cg8",
    "C6b.0", "C8b.0", "G.1", "FI0.3", "C4b.1", "C0b.2", "C8a.0", "FO0.4", "C2a.0", "C6a.0", "C8b.1", "FI3.3",
    "tok0", "C6b.1", "C8a.1", "C2a.1", "FI1.3", "tok1", "G.2", "FI0.4", "C2b.2", "FI2.4", "C4a.2", "C6a.1",
    "tok2", "tok3", "C8b.2", "tok4", "C4b.2", "C6b.2", "C8a.2", "C0b.3", "C2b.3", "G.3", "FO0.5", "FI1.4",
    "tok5", "C0a.3", "C2a.2", "C4a.3", "C6a.2", "C8a.3", "C2b.4", "C6b.3", "FI0.5", "C8b.3", "C0b.4", "C4b.3",
    "C6a.3", "C0a.4", "C2a.3", "C4a.4", "C8a.4", "tok6", "FI3.4", "G.4", "C6b.4", "C4b.4", "C8b.4", "FO1.5",
    "C0b.5", "C6a.4", "C2a.4", "tok7", "FI1.5", "tok8", "FI3.5", "C4b.5", "C4a.5", "C8b.5", "C8a.5", "C2b.5",
    "FI2.5", "C6a.5", "C6b.5", "C0a.5", "C2a.5",
)


OUTER_PARTS = min(len(OUTER_GATHER), 2)


def inbox_shapes(sizes, count, rows, axes):
    left = dict(sizes)
    shapes = []
    for axis in axes:
        senders = left.pop(axis) - 1
        rest = tuple(left[name] for name in "yhlx" if name in left)
        shapes.append((senders, count) + rest + (rows, 128))
    return shapes


class Links:
    def __init__(self, sizes, send_sems, recv_sems):
        self.sizes = dict(sizes, c=2)
        wide, narrow = lax.axis_index("wide"), lax.axis_index("narrow")
        z = wide // sizes["x"]
        self.at = {
            "h": z // sizes["l"], "l": z % sizes["l"], "x": wide % sizes["x"], "y": narrow // 2, "c": narrow % 2
        }
        self.send_sems, self.recv_sems = send_sems, recv_sems
        self.used = 0
        self.sent = [None] * SEND_SLOTS

    def device(self, axis, step):
        at = dict(self.at)
        at[axis] = lax.rem(at[axis] + step, self.sizes[axis])
        return ((at["h"] * self.sizes["l"] + at["l"]) * self.sizes["x"] + at["x"], at["y"] * 2 + at["c"])

    def steps(self, axis):
        return range(1, self.sizes[axis])

    def send(self, axis, pairs, total):
        index, slot = self.used, self.used % SEND_SLOTS
        self.used += 1
        if self.sent[slot] is not None:
            self.sent[slot].wait_send()

        def copy(source, target, step):
            return pltpu.make_async_remote_copy(
                src_ref=source,
                dst_ref=target,
                send_sem=self.send_sems.at[slot],
                recv_sem=self.recv_sems.at[index],
                device_id=self.device(axis, step),
                device_id_type=MESH,
            )

        for step, (source, target) in zip(self.steps(axis), pairs):
            copy(source, target, step).start()
        self.sent[slot] = copy(total, total, 1)
        return self.sent[slot]

    def barrier(self):
        semaphore = pltpu.get_barrier_semaphore()
        partners = [self.device(axis, s) for axis in "hlxyc" for s in self.steps(axis)]
        for partner in partners:
            pl.semaphore_signal(semaphore, inc=1, device_id=partner, device_id_type=MESH)
        pl.semaphore_wait(semaphore, len(partners))

    def finish(self):
        for copies in self.sent:
            if copies is not None:
                copies.wait_send()


class Once:
    def __init__(self, copy):
        self.copy = copy

    def wait(self):
        if self.copy is not None:
            self.copy.wait()
        self.copy = None


class Gather:
    def __init__(self, links, shard, whole, own, taps, rows, axes):
        self.links, self.shard, self.whole, self.own = links, shard, whole, own
        self.taps, self.rows = pl.ds(taps[0], taps[1] - taps[0]), pl.ds(rows[0], rows[1] - rows[0])
        self.axes = axes + "c"
        self.stage = 0

    def region(self, axis=None):
        k, done = self.links, self.axes[: self.stage]
        places = {}
        for name in "yhlx":
            places[name] = k.at[name]
            if name in done:
                places[name] = slice(None)
            elif name == axis:
                places[name] = pl.ds(0, len(k.steps(axis)))
        return self.whole.at[
            self.taps, places["y"], k.at["c"], places["h"], places["l"], places["x"], self.rows
        ]

    def step(self):
        k = self.links
        if self.stage > 0:
            self.wait.wait_recv()
        if self.stage == len(self.axes):
            return
        target = self.region()
        source = target
        if self.stage == 0:
            source = self.shard.at[self.taps, self.rows]
        else:
            self.own.wait()
        axis = self.axes[self.stage]
        self.wait = k.send(axis, [(source, target) for _ in k.steps(axis)], self.region(axis))
        self.stage += 1


class Scatter:
    def __init__(self, links, partial, pair, inboxes, parts, axes, finish):
        self.links, self.partial, self.pair, self.inboxes = links, partial, pair, inboxes
        self.parts = pl.ds(parts[0], parts[1] - parts[0])
        self.first, self.axes, self.finish = parts[0], axes, finish
        self.stage = 0

    def region(self, done, axis=None, at=None):
        places = []
        for name in "yhlx":
            own = self.links.at[name] if name in done else slice(None)
            places.append(at if name == axis else own)
        return (self.parts, *places)

    def step(self):
        k, stage, pair = self.links, self.stage, self.pair
        self.stage += 1
        if stage == 0:
            whole = pair.at[self.parts]
            self.wait = k.send("c", [(self.partial.at[1 - k.at["c"], self.parts], whole)], whole)
            return
        self.wait.wait_recv()
        held = self.region(self.axes[: stage - 1])
        if stage == 1:
            came = [self.partial[k.at["c"], self.parts]]
        else:
            inbox = self.inboxes[stage - 2]
            came = [inbox[i] for i in range(inbox.shape[0])]
        if stage > len(self.axes):
            total = pair[held].astype(F32)
            for part in came:
                total = total + part.astype(F32)
            self.finish(total, self.first)
            return
        value = pair[held]
        for part in came:
            value = value + part
        pair[held] = value
        axis = self.axes[stage - 1]
        done = self.axes[: stage - 1]
        inbox = self.inboxes[stage - 1]
        self.wait = k.send(
            axis,
            [
                (pair.at[self.region(done, axis, lax.rem(k.at[axis] + s, k.sizes[axis]))], inbox.at[s - 1])
                for s in k.steps(axis)
            ],
            inbox,
        )


class Sharing:
    def __init__(self, share, take, held, got, axes):
        self.share, self.take, self.held, self.got, self.axes = share, take, held, got, axes
        self.stage = 0

    def send(self):
        self.wait = self.share(self.held.at[self.stage], self.got, self.axes[self.stage])

    def step(self):
        value = self.take(self.wait, self.held.at[self.stage], self.got, self.axes[self.stage])
        self.stage += 1
        self.held[self.stage] = value
        if self.stage < len(self.axes):
            self.send()


def gelu_pair(value):
    square = value * value
    bend = jnp.tanh(value * (GELU_A + (GELU_A * GELU_B) * square))
    share = 0.5 + 0.5 * bend
    slope = share + (0.5 * value) * ((1.0 - bend * bend) * (GELU_A + (3 * GELU_A * GELU_B) * square))
    return value * share, slope


def normalize(value):
    centre = value - jnp.mean(value, axis=-1, keepdims=True)
    factor = lax.rsqrt(jnp.mean(centre * centre, axis=-1, keepdims=True) + EPSILON)
    return centre * factor, factor


def normalize_back(grad, hat, factor):
    return factor * (
        grad
        - jnp.mean(grad, axis=-1, keepdims=True)
        - hat * jnp.mean(grad * hat, axis=-1, keepdims=True)
    )


def side_by_side(whole, tap):
    lanes = whole.shape[-1]
    return jnp.concatenate(
        [whole[tap, y, c].reshape(-1, lanes) for y in range(whole.shape[1]) for c in range(2)], axis=1
    )


def dot(left, right, over=((1,), (0,))):
    return lax.dot_general(left, right, (over, ((), ())), preferred_element_type=F32)


OVER_ROWS = ((0,), (0,))
OVER_LANES = ((1,), (1,))


def kernel(
    sizes, lengths, small_in, tokens, cotangent, conv_in, inner_in, outer_in,
    block_out, grad_tokens, conv_out, inner_out, outer_out, params_out,
    conv_w, inner_w, outer_w, params_got, params_sum,
    rows_buf, cot_buf, padded, padded_by8, padded_back, stage, conv_sum, held, outer_sum, resid_low, active, slope, outer_low,
    conv_partial, inner_partial, outer_partial, conv_pair, inner_pair, outer_pair,
    grads, grads_got, send_sems, recv_sems, local_sems, *inboxes,
):
    k = Links(sizes, send_sems, recv_sems)
    H, L, X, Y = (sizes[axis] for axis in "hlxy")
    row_count = tokens.shape[0]
    blocks = row_count // BLOCK
    steps = row_count // STEP_ROWS
    per_step = STEP_ROWS // BLOCK

    def local(index, source, target):
        copy = pltpu.make_async_copy(source, target, local_sems.at[index])
        copy.start()
        return copy

    rows_in = local(0, tokens, rows_buf)
    own = [
        Once(local(1 + i, shard, whole.at[:, k.at["y"], k.at["c"], k.at["h"], k.at["l"], k.at["x"]]))
        for i, (shard, whole) in enumerate(((conv_in, conv_w), (inner_in, inner_w), (outer_in, outer_w)))
    ]
    cot_in = local(4, cotangent, cot_buf)
    k.barrier()

    bounds = []
    total = 0
    for slot in range(lengths.shape[1]):
        total = total + lengths[0, slot]
        bounds.append(total)

    def window(block):
        number = 0
        for bound in bounds:
            number = number + jnp.where(block * BLOCK >= bound, 1, 0)
        return number

    def live(block):
        return jnp.where(block * BLOCK < total, 1.0, 0.0).astype(F32)

    def joined(block):
        return jnp.where(window(block) == window(block + 1), 1.0, 0.0).astype(F32) * live(block)

    def pad(source, target, target_by8):
        for b in range(blocks):
            at = b * BLOCK
            if b > 0:
                stage[0:REACH] = source[at - REACH : at].astype(F32) * joined(b - 1)
            else:
                stage[0:REACH] = jnp.zeros((REACH, D), F32)
            stage[REACH : REACH + BLOCK] = source[at : at + BLOCK].astype(F32) * live(b)
            if b < blocks - 1:
                stage[REACH + BLOCK :] = source[at + BLOCK : at + BLOCK + REACH].astype(F32) * joined(b)
            else:
                stage[REACH + BLOCK :] = jnp.zeros((REACH, D), F32)
            target[b] = stage[...].astype(BF)
            target_by8[b] = stage[8 : BLOCK + 2 * REACH - 8].astype(BF)

    def window_rows(source, source_by8, block, place):
        if place % 2 == 0:
            return source[block, pl.ds(8 * place, BLOCK), :]
        return source_by8[block, pl.ds(8 * (place - 1), BLOCK), :]

    def step_rows(source, source_by8, step, place):
        return jnp.concatenate(
            [window_rows(source, source_by8, step * per_step + j, place) for j in range(per_step)], axis=0
        )

    def all_rows(source, source_by8, place):
        return jnp.concatenate([window_rows(source, source_by8, b, place) for b in range(blocks)], axis=0)

    def at_step(step):
        return pl.ds(pl.multiple_of(step * STEP_ROWS, STEP_ROWS), STEP_ROWS)

    def live_rows(value, step):
        return jnp.concatenate(
            [value[j * BLOCK : (j + 1) * BLOCK] * live(step * per_step + j) for j in range(per_step)], axis=0
        )

    def param(first, width):
        return jnp.concatenate(
            [params_sum[5, pl.ds((first + i) // 128, 1), :] for i in range(0, width, 128)], axis=1
        )

    def add_grad(first, value):
        summed = jnp.sum(value, axis=0, keepdims=True)
        for i in range(0, summed.shape[1], 128):
            row = (first + i) // 128
            grads[0, row : row + 1, :] = grads[0, row : row + 1, :] + summed[:, i : i + 128]

    CONV_BIAS, GAIN_ONE, SHIFT_ONE, INNER_BIAS = 0, D, 2 * D, 3 * D
    OUTER_BIAS, GAIN_TWO, SHIFT_TWO = 3 * D + FF, 4 * D + FF, 5 * D + FF

    slot_at, slots = {}, 0
    for axis in "hlxyc":
        slot_at[axis], slots = slots, slots + len(k.steps(axis))

    def own_params():
        count = small_in.shape[0]
        wide, narrow = k.device("c", 0)
        start = (wide * 2 * Y + narrow) * count
        row = small_in[...].astype(F32).reshape(1, count)
        row = jnp.concatenate([row, jnp.zeros((1, 256 - count), F32)], axis=1)
        row = pltpu.roll(jnp.broadcast_to(row, (8, 256)), start % 128, 1)
        params_sum[0] = jnp.zeros((GRAD_ROWS, 128), F32)
        params_sum[0, pl.ds(start // 128, 1), :] = row[0:1, :128]
        params_sum[0, pl.ds(start // 128 + 1, 1), :] = row[0:1, 128:]

    def share(source, got, axis):
        slots = got.at[pl.ds(slot_at[axis], len(k.steps(axis)))]
        return k.send(axis, [(source, slots.at[s - 1]) for s in k.steps(axis)], slots)

    def take(wait, source, got, axis):
        wait.wait_recv()
        value = source[...]
        for s in k.steps(axis):
            value = value + got[slot_at[axis] + s - 1]
        return value

    def block_rows(block):
        return pl.ds(block * BLOCK, BLOCK)

    def conv_taps(first):
        last = {piece[0]: piece[1] for piece in CONV_GATHER}[first]

        @pl.loop(0, steps)
        def _(step):
            value = None
            for tap in range(first, last):
                term = dot(step_rows(padded, padded_by8, step, tap), side_by_side(conv_w, tap))
                value = term if value is None else value + term
            if first != TAP_ORDER[0]:
                value = value + conv_sum[at_step(step), :]
            conv_sum[at_step(step), :] = value

    def first_part(block, hat):
        start = window_rows(padded, padded_by8, block, REACH // 8).astype(F32)
        return start + hat * param(GAIN_ONE, D) + param(SHIFT_ONE, D)

    def conv_end(block):
        rows = block_rows(block)
        bent, tilt = gelu_pair(conv_sum[rows, :] + param(CONV_BIAS, D))
        hat, factor = normalize(bent)
        conv_sum[rows, :] = tilt * factor
        held[rows, :] = hat
        resid_low[rows, :] = first_part(block, hat).astype(BF)

    width = inner_w.shape[-1]
    groups = Y * 2

    def inner_piece(piece):
        rows = pl.ds(piece * STEP_ROWS, STEP_ROWS)
        for group in range(groups):
            first = group * width
            value = dot(resid_low[rows, :], inner_w[0, group // 2, group % 2].reshape(D, width))
            bent, tilt = gelu_pair(value + param(INNER_BIAS + first, width))
            active[rows, first : first + width] = bent.astype(BF)
            slope[rows, first : first + width] = tilt.astype(BF)

    outer_rows = outer_w.shape[6]

    def outer_dot(rows, part):
        size = outer_rows // OUTER_PARTS
        left = jnp.concatenate(
            [active[rows, i * outer_rows + part * size : i * outer_rows + (part + 1) * size] for i in range(H * L * X)],
            axis=1,
        )
        right = jnp.concatenate(
            [
                outer_w[0, g // 2, g % 2, :, :, :, part * size : (part + 1) * size, :].reshape(-1, 128)
                for g in range(groups)
            ],
            axis=1,
        )
        return dot(left, right)

    def outer_part(part):
        for step in range(steps):
            rows = pl.ds(step * STEP_ROWS, STEP_ROWS)
            value = outer_dot(rows, part)
            if part > 0:
                value = value + outer_sum[rows, :]
            outer_sum[rows, :] = value

    def outer_block(block):
        rows = block_rows(block)
        value = outer_dot(rows, OUTER_PARTS - 1) + param(OUTER_BIAS, D)
        if OUTER_PARTS > 1:
            value = value + outer_sum[rows, :]
        hat, factor = normalize(value)
        gain = param(GAIN_TWO, D)
        result = first_part(block, held[rows, :]) + hat * gain + param(SHIFT_TWO, D)
        rows_buf[rows, :] = (result * live(block)).astype(BF)
        upstream = cot_buf[rows, :].astype(F32) * live(block)
        back = normalize_back(upstream * gain, hat, factor)
        outer_low[rows, :] = back.astype(BF)
        add_grad(OUTER_BIAS, back)
        add_grad(GAIN_TWO, upstream * hat)

    def upstream_sum(block):
        add_grad(SHIFT_TWO, cot_buf[block_rows(block), :].astype(F32) * live(block))

    def outer_grad(piece):
        half, y = piece // Y, piece % Y
        size = outer_rows // 2
        left = jnp.concatenate(
            [active[:, i * outer_rows + half * size : i * outer_rows + (half + 1) * size] for i in range(H * L * X)],
            axis=1,
        )
        value = dot(left, outer_low[:, y * 256 : (y + 1) * 256], OVER_ROWS).astype(BF)
        for c in range(2):
            outer_partial[c, half, y] = value[:, c * 128 : (c + 1) * 128].reshape(H, L, X, size, 128)

    def hidden_piece(piece):
        step, group = piece // groups, piece % groups
        rows, first = pl.ds(step * STEP_ROWS, STEP_ROWS), group * width
        right = jnp.concatenate(
            [outer_w[0, y, c, group // L, group % L].reshape(width, 128) for y in range(Y) for c in range(2)], axis=1
        )
        value = dot(outer_low[rows, :], right, OVER_LANES) * slope[rows, first : first + width].astype(F32)
        add_grad(INNER_BIAS + first, value)
        slope[rows, first : first + width] = value.astype(BF)

    def inner_grad(piece):
        right = jnp.concatenate(
            [slope[:, g * width + piece * 128 : g * width + (piece + 1) * 128] for g in range(groups)], axis=1
        )
        value = dot(resid_low[...], right, OVER_ROWS).astype(BF)
        for g in range(groups):
            part = value[:, g * 128 : (g + 1) * 128]
            inner_partial[g % 2, piece, g // 2] = part.reshape(H, L, X, -1, 128)

    def resid_block(block):
        rows = block_rows(block)
        value = cot_buf[rows, :].astype(F32) * live(block)
        for g in range(groups):
            right = inner_w[0, g // 2, g % 2].reshape(D, width)
            value = value + dot(slope[rows, g * width : (g + 1) * width], right, OVER_LANES)
        hat = held[rows, :]
        held[rows, :] = value
        add_grad(GAIN_ONE, value * hat)
        add_grad(SHIFT_ONE, value)
        back = normalize_back(value * param(GAIN_ONE, D), hat, conv_sum[rows, :])
        add_grad(CONV_BIAS, back)
        conv_sum[rows, :] = back

    conv_rows = conv_w.shape[6]

    def conv_grad(tap):
        left = all_rows(padded, None, REACH // 8)
        right = all_rows(padded_back, padded_by8, KERNEL_TAPS - 1 - tap)
        value = dot(left, right, OVER_ROWS).astype(BF)
        size = conv_rows // 2
        for g in range(groups):
            part = value[:, g * 128 : (g + 1) * 128].reshape(H, L, X, conv_rows, 128)
            for half in range(2):
                conv_partial[g % 2, half * KERNEL_TAPS + tap, g // 2] = part[:, :, :, half * size : (half + 1) * size]

    def token_piece(piece):
        step, part = piece // 3, piece % 3
        rows = pl.ds(step * STEP_ROWS, STEP_ROWS)
        value = held[rows, :]
        for tap in range(part * KERNEL_TAPS // 3, (part + 1) * KERNEL_TAPS // 3):
            value = value + dot(
                step_rows(padded_back, padded_by8, step, KERNEL_TAPS - 1 - tap),
                side_by_side(conv_w, tap),
                OVER_LANES,
            )
        if part == 2:
            value = live_rows(value, step)
        held[rows, :] = value

    def conv_finish(value, first):
        half, tap = first // KERNEL_TAPS, first % KERNEL_TAPS
        size = conv_rows // 2
        conv_out[pl.ds(tap, value.shape[0]), pl.ds(half * size, size), :] = value

    def inner_finish(value, first):
        for i in range(value.shape[0]):
            inner_out[:, (first + i) * 128 : (first + i + 1) * 128] = value[i]

    def outer_finish(value, first):
        size = outer_rows // 2
        outer_out[first * size : first * size + value.shape[0] * size, :] = value.reshape(-1, 128)

    params_sharing = Sharing(share, take, params_sum, params_got, "hlxyc")
    grads_sharing = Sharing(share, take, grads, grads_got, "cxylh")

    moves = {}
    for half in range(2):
        for first, last, axes in CONV_GATHER:
            size = conv_w.shape[6] // 2
            rows = (half * size, (half + 1) * size)
            piece = Gather(k, conv_in, conv_w, own[0], (first, last), rows, axes[half])
            moves["c" + str(first) + "ab"[half]] = piece
        for name, shard, whole, copied, kinds in (
            ("fi", inner_in, inner_w, own[1], INNER_GATHER),
            ("fo", outer_in, outer_w, own[2], OUTER_GATHER),
        ):
            size = whole.shape[6] // (2 * len(kinds))
            for i, axes in enumerate(kinds):
                at = (2 * i + half) * size
                moves[name + str(i) + "ab"[half]] = Gather(k, shard, whole, copied, (0, 1), (at, at + size), axes[half])
    for i, (name, first, last, axes) in enumerate(SCATTER):
        partial, pair, finish = {
            "C": (conv_partial, conv_pair, conv_finish),
            "FI": (inner_partial, inner_pair, inner_finish),
            "FO": (outer_partial, outer_pair, outer_finish),
        }[name.rstrip("0123456789ab")]
        moves[name] = Scatter(k, partial, pair, inboxes[4 * i : 4 * i + 4], (first, last), axes, finish)
    moves["P"] = params_sharing
    moves["G"] = grads_sharing

    def pad_tokens(_):
        rows_in.wait()
        grads[0] = jnp.zeros((GRAD_ROWS, 128), F32)
        pad(rows_buf, padded, padded_by8)

    def pad_back(_):
        pad(conv_sum, padded_back, padded_by8)

    work = {
        "pad": pad_tokens,
        "conv": conv_taps,
        "epi": conv_end,
        "inner": inner_piece,
        "ups": upstream_sum,
        "op": outer_part,
        "outer": outer_block,
        "og": outer_grad,
        "hid": hidden_piece,
        "ig": inner_grad,
        "res": resid_block,
        "padb": pad_back,
        "cg": conv_grad,
        "tok": token_piece,
    }
    out_copies = []
    own_params()
    params_sharing.send()
    for name in ORDER:
        if name == "ups0":
            cot_in.wait()
        if "." in name:
            moves[name.split(".")[0]].step()
        else:
            kind = name.rstrip("0123456789")
            work[kind](int(name[len(kind) :] or 0))
        if name == "res5":
            grads_sharing.send()
        if name == "outer5":
            out_copies.append(local(0, rows_buf, block_out))
        if name in ("tok2", "tok5", "tok8"):
            rows = pl.ds((int(name[3:]) // 3) * STEP_ROWS, STEP_ROWS)
            out_copies.append(local(5 + int(name[3:]) // 3, held.at[rows], grad_tokens.at[rows]))
    params_out[...] = grads[5]
    for copy in out_copies:
        copy.wait()
    k.finish()


def run_kernel(sizes, lengths, small, tokens, cotangent, conv_shard, inner_shard, outer_shard):
    H, L, X, Y = (sizes[axis] for axis in "hlxy")
    taps, conv_rows, lanes = conv_shard.shape
    inner_rows, width = inner_shard.shape
    outer_rows = outer_shard.shape[0]
    rows = tokens.shape[0]
    blocks = rows // BLOCK
    inner_shard, outer_shard = inner_shard[None], outer_shard[None]

    def whole(shard):
        return pltpu.VMEM((shard.shape[0], Y, 2, H, L, X) + shard.shape[1:], BF)

    def pair(count, r):
        return pltpu.VMEM((count, Y, H, L, X, r, 128), BF)

    def partial(count, r):
        return pltpu.VMEM((2, count, Y, H, L, X, r, 128), BF)

    rows_of = {"C": conv_rows // 2, "FI": inner_rows, "FO": outer_rows // 2}
    parts_of = {"C": 2 * taps, "FI": width // 128, "FO": 2}
    inboxes = []
    for name, first, last, axes in SCATTER:
        r = rows_of[name.rstrip("0123456789ab")]
        inboxes += [pltpu.VMEM(shape, BF) for shape in inbox_shapes(sizes, last - first, r, axes)]
    partners = H + L + X + Y - 3
    gathers = 2 * (len(CONV_GATHER) + len(INNER_GATHER) + len(OUTER_GATHER))
    copies = 5 * (gathers + len(SCATTER) + 2)
    padded = BLOCK + 2 * REACH
    scratch = [whole(conv_shard), whole(inner_shard), whole(outer_shard)]
    scratch += [pltpu.VMEM((partners, GRAD_ROWS, 128), F32), pltpu.VMEM((6, GRAD_ROWS, 128), F32)]
    scratch += [
        pltpu.VMEM((rows, D), BF),
        pltpu.VMEM((rows, D), BF),
        pltpu.VMEM((blocks, padded, D), BF),
        pltpu.VMEM((blocks, padded - 16, D), BF),
        pltpu.VMEM((blocks, padded, D), BF),
        pltpu.VMEM((padded, D), F32),
        pltpu.VMEM((rows, D), F32),
        pltpu.VMEM((rows, D), F32),
        pltpu.VMEM((rows, D), F32) if OUTER_PARTS > 1 else pltpu.VMEM((8, 128), F32),
        pltpu.VMEM((rows, D), BF),
        pltpu.VMEM((rows, FF), BF),
        pltpu.VMEM((rows, FF), BF),
        pltpu.VMEM((rows, D), BF),
    ]
    scratch += [partial(parts_of[name], rows_of[name]) for name in ("C", "FI", "FO")]
    scratch += [pair(parts_of[name], rows_of[name]) for name in ("C", "FI", "FO")]
    scratch += [pltpu.VMEM((6, GRAD_ROWS, 128), F32), pltpu.VMEM((partners, GRAD_ROWS, 128), F32)]
    scratch += [pltpu.SemaphoreType.DMA((SEND_SLOTS,)), pltpu.SemaphoreType.DMA((copies,)), pltpu.SemaphoreType.DMA((8,))]
    scratch += inboxes
    far = pl.BlockSpec(memory_space=pl.ANY)
    near = pl.BlockSpec(memory_space=pltpu.VMEM)
    return pl.pallas_call(
        functools.partial(kernel, sizes),
        out_shape=[
            jax.ShapeDtypeStruct((rows, D), BF),
            jax.ShapeDtypeStruct((rows, D), F32),
            jax.ShapeDtypeStruct(conv_shard.shape, F32),
            jax.ShapeDtypeStruct(inner_shard.shape[1:], F32),
            jax.ShapeDtypeStruct(outer_shard.shape[1:], F32),
            jax.ShapeDtypeStruct((GRAD_ROWS, 128), F32),
        ],
        in_specs=[pl.BlockSpec(memory_space=pltpu.SMEM), near] + [far] * 5,
        out_specs=[far, far, near, near, near, near],
        scratch_shapes=scratch,
        compiler_params=pltpu.CompilerParams(
            collective_id=0, has_side_effects=True, vmem_limit_bytes=VMEM_LIMIT
        ),
    )(lengths, small, tokens, cotangent, conv_shard, inner_shard, outer_shard)


def hand_over(parts, grads, *refs):
    count = len(parts)
    sources, targets, small = refs[:count], refs[count : 2 * count], refs[2 * count]
    held, grads_held, sems = refs[2 * count + 1 : 3 * count + 1], refs[-2], refs[-1]
    first = pltpu.make_async_copy(grads, grads_held, sems.at[0, sum(parts)])
    pieces = []
    for source, target, middle, count in zip(sources, targets, held, parts):
        size = source.shape[0] // count
        pieces += [tuple(ref.at[pl.ds(i * size, size)] for ref in (source, middle, target)) for i in range(count)]
    ins = [pltpu.make_async_copy(s, m, sems.at[0, i]) for i, (s, m, _) in enumerate(pieces)]
    outs = [pltpu.make_async_copy(m, t, sems.at[1, i]) for i, (_, m, t) in enumerate(pieces)]
    for copy in ins:
        copy.start()
    first.start()
    for come, go in zip(ins, outs):
        come.wait()
        go.start()
    first.wait()
    size = small.shape[0]
    start = (lax.axis_index("wide") * lax.axis_size("narrow") + lax.axis_index("narrow")) * size
    row = jnp.concatenate([grads_held[pl.ds(start // 128, 1), :], grads_held[pl.ds(start // 128 + 1, 1), :]], axis=1)
    row = pltpu.roll(jnp.broadcast_to(row, (8, 256)), 256 - start % 128, 1)
    small[...] = row[0:1, :size].reshape(size)
    for copy in outs:
        copy.wait()


def settle(share, params_grad, arrays):
    far = pl.BlockSpec(memory_space=pl.ANY)
    near = pl.BlockSpec(memory_space=pltpu.VMEM)
    parts = [max(1, a.size * a.dtype.itemsize >> 20) for a in arrays]
    return pl.pallas_call(
        functools.partial(hand_over, parts),
        out_shape=[jax.ShapeDtypeStruct(a.shape, a.dtype) for a in arrays] + [jax.ShapeDtypeStruct((share,), F32)],
        in_specs=[far] * (len(arrays) + 1),
        out_specs=[far] * len(arrays) + [near],
        scratch_shapes=[pltpu.VMEM(a.shape, a.dtype) for a in arrays]
        + [pltpu.VMEM(params_grad.shape, F32), pltpu.SemaphoreType.DMA((2, sum(parts) + 1))],
        compiler_params=pltpu.CompilerParams(vmem_limit_bytes=VMEM_LIMIT),
    )(params_grad, *arrays)


def fused(
    sizes, tokens, window_lengths, conv_weight, feedforward_input_weight, ffn_out, small_params, cotangent
):
    block_out, grad_tokens, conv_grad, inner_grad, outer_grad, params_grad = run_kernel(
        sizes, window_lengths, small_params, tokens, cotangent, conv_weight, feedforward_input_weight, ffn_out
    )
    return settle(small_params.shape[0], params_grad, [block_out, grad_tokens, conv_grad, inner_grad, outer_grad])


def solution(mesh):
    wide, narrow = mesh.shape["wide"], mesh.shape["narrow"]
    X = max(narrow // 2, 1)
    sizes = {"h": wide // X // 2, "l": 2, "x": X, "y": X}

    def step(*arrays):
        rows = arrays[0].shape[0]
        inner, outer = arrays[3].shape, arrays[4].shape
        whole_lanes = all(a.shape[-1] % 128 == 0 for a in arrays[2:5])
        fits = rows == 3 * STEP_ROWS and narrow == 4 and wide == 8 and inner[1] == X * outer[0] and whole_lanes
        small = arrays[5].shape[0]
        fits = fits and small % 32 == 0 and small <= 160
        if fits:
            return fused(sizes, *arrays)
        return shards(*arrays)

    return jax.shard_map(
        step,
        mesh=mesh,
        in_specs=(
            P(("wide", "narrow"), None),
            P(("wide", "narrow"), None),
            P(None, "wide", "narrow"),
            P("wide", "narrow"),
            P("wide", "narrow"),
            P(("wide", "narrow")),
            P(("wide", "narrow"), None),
        ),
        out_specs=(
            P(("wide", "narrow"), None),
            P(("wide", "narrow"), None),
            P(None, "wide", "narrow"),
            P("wide", "narrow"),
            P("wide", "narrow"),
            P(("wide", "narrow")),
        ),
        check_vma=False,
    )
```

```python
import functools

import jax
import jax.numpy as jnp
from jax import lax
from jax.experimental import pallas as pl
from jax.experimental.pallas import tpu as pltpu
from jax.sharding import PartitionSpec as P

D = 512
FF = 2048
KERNEL_TAPS = 9
DILATION_STEP = 8
EPSILON = 1e-05

def layer_norm(values, norm_gain, norm_shift):
    centre = values - jnp.mean(values, axis=-1, keepdims=True)
    spread = jnp.mean(centre * centre, axis=-1, keepdims=True)
    return centre * lax.rsqrt(spread + EPSILON) * norm_gain + norm_shift


def window_masks(lengths, row_count):
    bounds = jnp.cumsum(lengths)
    places = jnp.arange(row_count, dtype=jnp.int32)
    segment_ids = jnp.sum((places[:, None] >= bounds[None, :]).astype(jnp.int32), axis=1)
    live_rows = (places < bounds[-1]).astype(jnp.float32)
    tap_valid = []
    for index_of_tap in range(KERNEL_TAPS):
        tap_displacement = (index_of_tap - KERNEL_TAPS // 2) * DILATION_STEP
        source = places + tap_displacement
        inside = (source >= 0) & (source < row_count)
        same_window = jnp.roll(segment_ids, -tap_displacement) == segment_ids
        tap_valid.append((inside & same_window).astype(jnp.float32))
    return (live_rows, tap_valid)


def split_params(flat_params):
    return (
        flat_params[0:D],
        flat_params[D : 2 * D],
        flat_params[2 * D : 3 * D],
        flat_params[3 * D : 3 * D + FF],
        flat_params[3 * D + FF : 4 * D + FF],
        flat_params[4 * D + FF : 5 * D + FF],
        flat_params[5 * D + FF : 6 * D + FF],
    )


def branch_one(conv_sum, conv_bias, gain_one, shift_one):
    return layer_norm(jax.nn.gelu(conv_sum + conv_bias), gain_one, shift_one)


def branch_two(outer_sum, outer_bias, gain_two, shift_two):
    return layer_norm(outer_sum + outer_bias, gain_two, shift_two)


def fetch_forward(conv_weight, feedforward_input_weight, ffn_out, small_params):
    narrow_set = (
        lax.all_gather(conv_weight, "narrow", axis=2, tiled=True),
        lax.all_gather(feedforward_input_weight, "narrow", axis=1, tiled=True),
        lax.all_gather(ffn_out, "narrow", axis=1, tiled=True),
        lax.all_gather(small_params, "narrow", axis=0, tiled=True),
    )
    return (
        lax.all_gather(narrow_set[0], "wide", axis=1, tiled=True),
        lax.all_gather(narrow_set[1], "wide", axis=0, tiled=True),
        lax.all_gather(narrow_set[2], "wide", axis=0, tiled=True),
        lax.all_gather(narrow_set[3], "wide", axis=0, tiled=True),
    )


def shards(
    tokens, window_lengths, conv_weight, feedforward_input_weight, ffn_out, small_params, cotangent
):
    row_count = tokens.shape[0]
    block_size = min(512, row_count)
    live_rows, tap_valid = window_masks(window_lengths[0], row_count)
    weights = fetch_forward(conv_weight, feedforward_input_weight, ffn_out, small_params)
    conv_full, inner_full, outer_full = (weights[0], weights[1], weights[2])
    pieces = split_params(weights[3].astype(jnp.float32))
    start_rows = tokens * live_rows[:, None].astype(jnp.bfloat16)
    conv_sum = jnp.zeros((row_count, D), jnp.float32)
    for index_of_tap in range(KERNEL_TAPS):
        tap_displacement = (index_of_tap - KERNEL_TAPS // 2) * DILATION_STEP
        shifted = jnp.roll(start_rows, -tap_displacement, axis=0) * tap_valid[index_of_tap][
            :, None
        ].astype(jnp.bfloat16)
        conv_sum = conv_sum + jnp.dot(
            shifted, conv_full[index_of_tap], preferred_element_type=jnp.float32
        )
    branch_out, pull_one = jax.vjp(branch_one, conv_sum, pieces[0], pieces[1], pieces[2])
    residual_one = start_rows.astype(jnp.float32) + branch_out
    residual_low = residual_one.astype(jnp.bfloat16)
    outer_parts = []
    for first_row in range(0, row_count, block_size):
        inner_sum = (
            jnp.dot(
                residual_low[first_row : first_row + block_size],
                inner_full,
                preferred_element_type=jnp.float32,
            )
            + pieces[3]
        )
        active = jax.nn.gelu(inner_sum).astype(jnp.bfloat16)
        outer_parts.append(jnp.dot(active, outer_full, preferred_element_type=jnp.float32))
    outer_sum = jnp.concatenate(outer_parts, axis=0)
    normed, pull_two = jax.vjp(branch_two, outer_sum, pieces[4], pieces[5], pieces[6])
    block_out = (live_rows[:, None] * (residual_one + normed)).astype(jnp.bfloat16)
    upstream = cotangent.astype(jnp.float32) * live_rows[:, None]
    d_outer, d_outer_bias, d_gain_two, d_shift_two = pull_two(upstream)
    outer_low = d_outer.astype(jnp.bfloat16)
    grad_in = jnp.zeros((D, FF), jnp.float32)
    grad_out = jnp.zeros((FF, D), jnp.float32)
    inner_bias_grad = jnp.zeros((FF,), jnp.float32)
    resid_parts = []
    for first_row in range(0, row_count, block_size):
        rows_low = residual_low[first_row : first_row + block_size]
        outer_rows = outer_low[first_row : first_row + block_size]
        inner_sum = jnp.dot(rows_low, inner_full, preferred_element_type=jnp.float32) + pieces[3]
        active_full, pull_gelu = jax.vjp(jax.nn.gelu, inner_sum)
        active = active_full.astype(jnp.bfloat16)
        d_active = jnp.einsum(
            "rd,fd->rf", outer_rows, outer_full, preferred_element_type=jnp.float32
        )
        d_inner = pull_gelu(d_active)[0]
        inner_bias_grad = inner_bias_grad + jnp.sum(d_inner, axis=0)
        inner_low = d_inner.astype(jnp.bfloat16)
        grad_in = grad_in + jnp.einsum(
            "rd,rf->df", rows_low, inner_low, preferred_element_type=jnp.float32
        )
        grad_out = grad_out + jnp.einsum(
            "rf,rd->fd", active, outer_rows, preferred_element_type=jnp.float32
        )
        resid_parts.append(
            jnp.einsum("rf,df->rd", inner_low, inner_full, preferred_element_type=jnp.float32)
        )
    d_resid = upstream + jnp.concatenate(resid_parts, axis=0)
    d_conv, d_conv_bias, d_gain_one, d_shift_one = pull_one(d_resid)
    convolution_reduced = d_conv.astype(jnp.bfloat16)
    conv_grads = []
    d_start = d_resid
    for index_of_tap in range(KERNEL_TAPS):
        tap_displacement = (index_of_tap - KERNEL_TAPS // 2) * DILATION_STEP
        tap_mask = tap_valid[index_of_tap][:, None]
        shifted = jnp.roll(start_rows, -tap_displacement, axis=0) * tap_mask.astype(jnp.bfloat16)
        conv_grads.append(
            jnp.einsum(
                "ri,ro->io", shifted, convolution_reduced, preferred_element_type=jnp.float32
            )
        )
        back_rows = jnp.einsum(
            "ro,io->ri",
            convolution_reduced,
            conv_full[index_of_tap],
            preferred_element_type=jnp.float32,
        )
        d_start = d_start + jnp.roll(back_rows * tap_mask, tap_displacement, axis=0)
    grad_tokens = d_start * live_rows[:, None]
    convolution_weight_gradient = jnp.stack(conv_grads, axis=0)
    grad_flat = jnp.concatenate(
        [
            d_conv_bias,
            d_gain_one,
            d_shift_one,
            inner_bias_grad,
            d_outer_bias,
            d_gain_two,
            d_shift_two,
        ],
        axis=0,
    )
    wide_sums = (
        lax.psum_scatter(convolution_weight_gradient, "wide", scatter_dimension=1, tiled=True),
        lax.psum_scatter(grad_in, "wide", scatter_dimension=0, tiled=True),
        lax.psum_scatter(grad_out, "wide", scatter_dimension=0, tiled=True),
        lax.psum_scatter(grad_flat, "wide", scatter_dimension=0, tiled=True),
    )
    owned = (
        lax.psum_scatter(wide_sums[0], "narrow", scatter_dimension=2, tiled=True),
        lax.psum_scatter(wide_sums[1], "narrow", scatter_dimension=1, tiled=True),
        lax.psum_scatter(wide_sums[2], "narrow", scatter_dimension=1, tiled=True),
        lax.psum_scatter(wide_sums[3], "narrow", scatter_dimension=0, tiled=True),
    )
    owned_flat = owned[3]
    return (block_out, grad_tokens, owned[0], owned[1], owned[2], owned_flat)

MESH = pl.DeviceIdType.MESH
BF = jnp.bfloat16
F32 = jnp.float32
BLOCK = 256
REACH = KERNEL_TAPS // 2 * DILATION_STEP
STEP_ROWS = 512
GRAD_ROWS = 40
VMEM_LIMIT = 63 << 20
SEND_SLOTS = 20
GELU_A = 0.7978845608028654
GELU_B = 0.044715
CONV_GATHER = (
    (0, 2, ('hlxy', 'hlyx')),
    (2, 3, ('zxy', 'zyx')),
    (3, 4, ('zyx', 'zxy')),
    (4, 6, ('hxly', 'hylx')),
    (6, 8, ('hxly', 'hylx')),
    (8, 9, ('hxly', 'hylx')),
)
INNER_GATHER = (('hxly', 'hylx'), ('hylx', 'hxly'))
OUTER_GATHER = (('hxly', 'hylx'), ('hyxl', 'hxyl'))
SCATTER = (
    ('FO0', 0, 1, 'zxy'),
    ('FO1', 1, 2, 'qlh'),
    ('FI0', 0, 2, 'ylhx'),
    ('FI1', 2, 4, 'xlyh'),
    ('C0a', 0, 2, 'ylhx'),
    ('C0b', 9, 11, 'xlhy'),
    ('C2a', 2, 4, 'ylxh'),
    ('C2b', 11, 13, 'xlyh'),
    ('C4a', 4, 6, 'ylxh'),
    ('C4b', 13, 15, 'xlyh'),
    ('C6a', 6, 8, 'xylh'),
    ('C6b', 15, 17, 'yxlh'),
    ('C8a', 8, 9, 'xyhl'),
    ('C8b', 17, 18, 'yxhl'),
)
TAP_ORDER = (0,)
ORDER = (
    "c0a.0", "c0b.0", "c2a.0", "pad", "c2b.0", "ups0", "ups1", "ups2", "c3a.0", "ups3", "ups4", "ups5",
    "c3b.0", "c4a.0", "P.0", "c4b.0", "c0a.1", "c6a.0", "c2a.1", "c0b.1", "c2b.1", "c6b.0", "c3a.1", "c8a.0",
    "c8b.0", "fi0a.0", "c3b.1", "fi0b.0", "P.1", "c2a.2", "c4a.1", "fi1a.0", "c2b.2", "c4b.1", "c0a.2",
    "fi1b.0", "c3a.2", "fo0a.0", "c3b.2", "c0b.2", "fo0b.0", "P.2", "c4a.2", "c6a.1", "c6b.1", "c2a.3",
    "c8a.1", "c8b.1", "fi0a.1", "fo1a.0", "c2b.3", "c2a.4", "c4b.2", "fi0b.1", "fi1a.1", "c2b.4", "c3b.3",
    "c0a.3", "fo1b.0", "fi1b.1", "c3b.4", "fo0a.1", "c0b.3", "c3a.3", "P.3", "c6a.2", "c6b.2", "P.4",
    "fo0b.1", "c3a.4", "c4a.3", "c8a.2", "c8b.2", "c4b.3", "fi0a.2", "fo1a.1", "fo1b.1", "fi0b.2", "c6a.3",
    "c0a.4", "c0b.4", "c6b.3", "fi1a.2", "c0a.5", "c0b.5", "conv0", "c4a.4", "c4b.4", "c8a.3", "c8b.3",
    "fi0a.3", "fi1b.2", "fo0a.2", "fo1a.2", "conv2", "c4a.5", "c4b.5", "fi0b.3", "fo0b.2", "conv3", "c6a.4",
    "c6b.4", "fo1b.2", "conv4", "c6a.5", "c6b.5", "c8a.4", "c8b.4", "fi1a.3", "fi1b.3", "fo1a.3", "conv6",
    "c8a.5", "c8b.5", "fi0a.4", "fo0a.3", "fo0b.3", "fi0b.4", "fo1b.3", "conv8", "fi0a.5", "epi0", "fi0b.5",
    "epi1", "epi2", "fi1a.4", "fi1b.4", "fo1a.4", "epi3", "epi4", "epi5", "fi1a.5", "fi1b.5", "fo1a.5",
    "inner0", "fo0a.4", "fo0b.4", "fo1b.4", "inner1", "fo0a.5", "fo0b.5", "fo1b.5", "inner2", "op0", "outer0",
    "outer1", "outer2", "outer3", "outer4", "outer5", "og0", "og1", "FO0.0", "og2", "og3", "FO0.1", "FO1.0",
    "hid0", "hid1", "hid2", "hid3", "hid4", "hid5", "FO1.1", "hid6", "hid7", "hid8", "hid9", "hid10", "hid11",
    "ig0", "ig1", "FI0.0", "ig2", "ig3", "FI0.1", "FI1.0", "res0", "res1", "res2", "FI1.1", "res3", "res4",
    "res5", "FO1.2", "padb", "cg0", "cg1", "C0a.0", "C0b.0", "cg2", "FI0.2", "FO0.2", "C0a.1", "C0b.1", "cg3",
    "FO1.3", "C2a.0", "C2b.0", "cg4", "FI1.2", "cg5", "C2a.1", "C2b.1", "C4a.0", "C4b.0", "cg6", "FO0.3",
    "cg7", "FI0.3", "C4a.1", "C4b.1", "C6a.0", "C6b.0", "cg8", "C0a.2", "C8a.0", "C8b.0", "sums", "C0b.2",
    "C6a.1", "C6b.1", "bo0", "bo1", "C2a.2", "bo2", "bo3", "bo4", "FI1.3", "C8a.1", "bo5", "tok0", "FI0.4",
    "C2b.2", "C8b.1", "tok1", "C0a.3", "C4a.2", "G.0", "tok2", "C0b.3", "C6a.2", "C6b.2", "tok3", "C2a.3",
    "C4b.2", "C8a.2", "tok4", "FI1.4", "C2b.3", "G.1", "C8b.2", "tok5", "C0a.4", "C4a.3", "C6b.3", "C6a.3",
    "tok6", "C0b.4", "C2a.4", "C8a.3", "tok7", "C2b.4", "C4b.3", "C8b.3", "G.2", "tok8", "C4a.4", "C6a.4",
    "C6b.4", "FO0.4", "FO1.4", "FI0.5", "FI1.5", "C0a.5", "C0b.5", "C2a.5", "C8a.4", "C4b.4", "C2b.5", "G.3",
    "C8b.4", "C4a.5", "C6a.5", "C8a.5", "C6b.5", "C4b.5", "C8b.5", "G.4",
)


OUTER_PARTS = min(len(OUTER_GATHER), 2)


TOGETHER = {"z": "hl", "q": "xy"}


def spread(axes):
    return "".join(TOGETHER.get(axis, axis) for axis in axes)


def inbox_shapes(sizes, count, rows, axes):
    left = dict(sizes)
    shapes = []
    for axis in axes:
        senders = 1
        for name in spread(axis):
            senders *= left.pop(name)
        senders -= 1
        rest = tuple(left[name] for name in "yhlx" if name in left)
        shapes.append((senders, count) + rest + (rows, 128))
    return shapes


class Links:
    def __init__(self, sizes, send_sems, recv_sems):
        self.sizes = dict(sizes, c=2)
        wide, narrow = lax.axis_index("wide"), lax.axis_index("narrow")
        z = wide // sizes["x"]
        self.at = {
            "h": z // sizes["l"], "l": z % sizes["l"], "x": wide % sizes["x"], "y": narrow // 2, "c": narrow % 2
        }
        self.send_sems, self.recv_sems = send_sems, recv_sems
        self.used = 0
        self.sent = [None] * SEND_SLOTS

    def there(self, axis, step):
        names = TOGETHER.get(axis, axis)
        index, count = 0, 1
        for name in names:
            index, count = index * self.sizes[name] + self.at[name], count * self.sizes[name]
        index = lax.rem(index + step, count)
        at = dict(self.at)
        for name in reversed(names):
            at[name], index = index % self.sizes[name], index // self.sizes[name]
        return at

    def device(self, axis, step):
        at = self.there(axis, step)
        return ((at["h"] * self.sizes["l"] + at["l"]) * self.sizes["x"] + at["x"], at["y"] * 2 + at["c"])

    def steps(self, axis):
        count = 1
        for name in TOGETHER.get(axis, axis):
            count *= self.sizes[name]
        return range(1, count)

    def send(self, axis, pairs, total, only=None):
        if total is None:
            steps = list(zip(self.steps(axis), pairs))
            return Each([self.send(axis, [pair], pair[1], step) for step, pair in steps])
        index, slot = self.used, self.used % SEND_SLOTS
        self.used += 1
        if self.sent[slot] is not None:
            self.sent[slot].wait_send()

        def copy(source, target, step):
            return pltpu.make_async_remote_copy(
                src_ref=source,
                dst_ref=target,
                send_sem=self.send_sems.at[slot],
                recv_sem=self.recv_sems.at[index],
                device_id=self.device(axis, step),
                device_id_type=MESH,
            )

        for step, (source, target) in zip(self.steps(axis) if only is None else [only], pairs):
            copy(source, target, step).start()
        self.sent[slot] = copy(total, total, 1)
        return self.sent[slot]

    def barrier(self):
        semaphore = pltpu.get_barrier_semaphore()
        partners = [self.device(axis, s) for axis in "zqc" for s in self.steps(axis)]
        for partner in partners:
            pl.semaphore_signal(semaphore, inc=1, device_id=partner, device_id_type=MESH)
        pl.semaphore_wait(semaphore, len(partners))

    def finish(self):
        for copies in self.sent:
            if copies is not None:
                copies.wait_send()


class Each:
    def __init__(self, copies):
        self.copies = copies

    def wait_recv(self):
        for copy in self.copies:
            copy.wait_recv()


class Once:
    def __init__(self, copy):
        self.copy = copy

    def wait(self):
        if self.copy is not None:
            self.copy.wait()
        self.copy = None


class Gather:
    def __init__(self, links, shard, whole, own, taps, rows, axes):
        self.links, self.shard, self.whole, self.own = links, shard, whole, own
        self.taps, self.rows = pl.ds(taps[0], taps[1] - taps[0]), pl.ds(rows[0], rows[1] - rows[0])
        self.axes = axes + "c"
        self.stage = 0

    def region(self, axis=None):
        k, done = self.links, spread(self.axes[: self.stage])
        places = {}
        for name in "yhlx":
            places[name] = k.at[name]
            if name in done:
                places[name] = slice(None)
            elif name == axis:
                places[name] = pl.ds(0, len(k.steps(axis)))
        return self.whole.at[
            self.taps, places["y"], k.at["c"], places["h"], places["l"], places["x"], self.rows
        ]

    def step(self):
        k = self.links
        if self.stage > 0:
            self.wait.wait_recv()
        if self.stage == len(self.axes):
            return
        target = self.region()
        source = target
        if self.stage == 0:
            source = self.shard.at[self.taps, self.rows]
        else:
            self.own.wait()
        axis = self.axes[self.stage]
        total = None if axis in TOGETHER else self.region(axis)
        self.wait = k.send(axis, [(source, target) for _ in k.steps(axis)], total)
        self.stage += 1


class Scatter:
    def __init__(self, links, partial, pair, inboxes, parts, axes, finish):
        self.links, self.partial, self.pair, self.inboxes = links, partial, pair, inboxes
        self.parts = pl.ds(parts[0], parts[1] - parts[0])
        self.first, self.axes, self.finish = parts[0], axes, finish
        self.stage = 0

    def region(self, done, axis="", at=None):
        places = []
        for name in "yhlx":
            own = self.links.at[name] if name in spread(done) else slice(None)
            places.append(at[name] if name in spread(axis) else own)
        return (self.parts, *places)

    def step(self):
        k, stage, pair = self.links, self.stage, self.pair
        self.stage += 1
        if stage == 0:
            whole = pair.at[self.parts]
            self.wait = k.send("c", [(self.partial.at[1 - k.at["c"], self.parts], whole)], whole)
            return
        self.wait.wait_recv()
        held = self.region(self.axes[: stage - 1])
        if stage == 1:
            came = [self.partial[k.at["c"], self.parts]]
        else:
            inbox = self.inboxes[stage - 2]
            came = [inbox[i] for i in range(inbox.shape[0])]
        if stage > len(self.axes):
            total = pair[held].astype(F32)
            for part in came:
                total = total + part.astype(F32)
            self.finish(total, self.first)
            return
        value = pair[held]
        for part in came:
            value = value + part
        pair[held] = value
        axis = self.axes[stage - 1]
        done = self.axes[: stage - 1]
        inbox = self.inboxes[stage - 1]
        self.wait = k.send(
            axis,
            [
                (pair.at[self.region(done, axis, k.there(axis, s))], inbox.at[s - 1])
                for s in k.steps(axis)
            ],
            inbox,
        )


class Sharing:
    def __init__(self, share, take, held, got, axes):
        self.share, self.take, self.held, self.got, self.axes = share, take, held, got, axes
        self.stage = 0

    def send(self):
        self.wait = self.share(self.held.at[self.stage], self.got, self.axes[self.stage])

    def step(self):
        value = self.take(self.wait, self.held.at[self.stage], self.got, self.axes[self.stage])
        self.stage += 1
        self.held[self.stage] = value
        if self.stage < len(self.axes):
            self.send()


def gelu_pair(value):
    square = value * value
    bend = jnp.tanh(value * (GELU_A + (GELU_A * GELU_B) * square))
    share = 0.5 + 0.5 * bend
    slope = share + (0.5 * value) * ((1.0 - bend * bend) * (GELU_A + (3 * GELU_A * GELU_B) * square))
    return value * share, slope


def normalize(value):
    centre = value - jnp.mean(value, axis=-1, keepdims=True)
    factor = lax.rsqrt(jnp.mean(centre * centre, axis=-1, keepdims=True) + EPSILON)
    return centre * factor, factor


def normalize_back(grad, hat, factor):
    return factor * (
        grad
        - jnp.mean(grad, axis=-1, keepdims=True)
        - hat * jnp.mean(grad * hat, axis=-1, keepdims=True)
    )


def side_by_side(whole, tap):
    lanes = whole.shape[-1]
    return jnp.concatenate(
        [whole[tap, y, c].reshape(-1, lanes) for y in range(whole.shape[1]) for c in range(2)], axis=1
    )


def dot(left, right, over=((1,), (0,))):
    return lax.dot_general(left, right, (over, ((), ())), preferred_element_type=F32)


OVER_ROWS = ((0,), (0,))
OVER_LANES = ((1,), (1,))


def kernel(
    sizes, lengths_in, small_in, tokens, cotangent, conv_in, inner_in, outer_in,
    block_out, grad_tokens, conv_out, inner_out, outer_out, params_out,
    conv_w, inner_w, outer_w, params_got, params_sum,
    cot_buf, padded, padded_by8, padded_back, stage, conv_sum, held, outer_sum, resid_low, active, slope, outer_low,
    conv_partial, inner_partial, outer_partial, conv_pair, inner_pair, outer_pair,
    grads, grads_got, lengths, small, send_sems, recv_sems, local_sems, *inboxes,
):
    k = Links(sizes, send_sems, recv_sems)
    H, L, X, Y = (sizes[axis] for axis in "hlxy")
    row_count = tokens.shape[0]
    blocks = row_count // BLOCK
    steps = row_count // STEP_ROWS
    per_step = STEP_ROWS // BLOCK

    def local(index, source, target):
        copy = pltpu.make_async_copy(source, target, local_sems.at[index])
        copy.start()
        return copy

    small_copy = local(8, small_in, small)
    lengths_copy = local(9, lengths_in, lengths)
    rows_in = local(0, tokens, outer_low)
    own = [
        Once(local(1 + i, shard, whole.at[:, k.at["y"], k.at["c"], k.at["h"], k.at["l"], k.at["x"]]))
        for i, (shard, whole) in enumerate(((conv_in, conv_w), (inner_in, inner_w), (outer_in, outer_w)))
    ]
    cot_in = local(4, cotangent, cot_buf)
    k.barrier()

    lengths_copy.wait()

    bounds = []
    total = 0
    for slot in range(lengths.shape[1]):
        total = total + lengths[0, slot]
        bounds.append(total)

    def window(block):
        number = 0
        for bound in bounds:
            number = number + jnp.where(block * BLOCK >= bound, 1, 0)
        return number

    def live(block):
        return jnp.where(block * BLOCK < total, 1.0, 0.0).astype(F32)

    def joined(block):
        return jnp.where(window(block) == window(block + 1), 1.0, 0.0).astype(F32) * live(block)

    def pad(source, target, target_by8):
        for b in range(blocks):
            at = b * BLOCK
            if b > 0:
                stage[0:REACH] = source[at - REACH : at].astype(F32) * joined(b - 1)
            else:
                stage[0:REACH] = jnp.zeros((REACH, D), F32)
            stage[REACH : REACH + BLOCK] = source[at : at + BLOCK].astype(F32) * live(b)
            if b < blocks - 1:
                stage[REACH + BLOCK :] = source[at + BLOCK : at + BLOCK + REACH].astype(F32) * joined(b)
            else:
                stage[REACH + BLOCK :] = jnp.zeros((REACH, D), F32)
            target[b] = stage[...].astype(BF)
            target_by8[b] = stage[8 : BLOCK + 2 * REACH - 8].astype(BF)

    def window_rows(source, source_by8, block, place):
        if place % 2 == 0:
            return source[block, pl.ds(8 * place, BLOCK), :]
        return source_by8[block, pl.ds(8 * (place - 1), BLOCK), :]

    def step_rows(source, source_by8, step, place):
        return jnp.concatenate(
            [window_rows(source, source_by8, step * per_step + j, place) for j in range(per_step)], axis=0
        )

    def all_rows(source, source_by8, place):
        return jnp.concatenate([window_rows(source, source_by8, b, place) for b in range(blocks)], axis=0)

    def at_step(step):
        return pl.ds(pl.multiple_of(step * STEP_ROWS, STEP_ROWS), STEP_ROWS)

    def live_rows(value, step):
        return jnp.concatenate(
            [value[j * BLOCK : (j + 1) * BLOCK] * live(step * per_step + j) for j in range(per_step)], axis=0
        )

    def param(first, width):
        return jnp.concatenate(
            [params_sum[5, pl.ds((first + i) // 128, 1), :] for i in range(0, width, 128)], axis=1
        )

    def add_grad(first, value):
        summed = jnp.sum(value, axis=0, keepdims=True)
        for i in range(0, summed.shape[1], 128):
            row = (first + i) // 128
            grads[0, row : row + 1, :] = grads[0, row : row + 1, :] + summed[:, i : i + 128]

    CONV_BIAS, GAIN_ONE, SHIFT_ONE, INNER_BIAS = 0, D, 2 * D, 3 * D
    OUTER_BIAS, GAIN_TWO, SHIFT_TWO = 3 * D + FF, 4 * D + FF, 5 * D + FF

    slot_at, slots = {}, 0
    for axis in "hlxyc":
        slot_at[axis], slots = slots, slots + len(k.steps(axis))

    def own_params():
        small_copy.wait()
        count = small.shape[0]
        wide, narrow = k.device("c", 0)
        start = (wide * 2 * Y + narrow) * count
        row = small[...].astype(F32).reshape(1, count)
        row = jnp.concatenate([row, jnp.zeros((1, 256 - count), F32)], axis=1)
        row = pltpu.roll(jnp.broadcast_to(row, (8, 256)), start % 128, 1)
        params_sum[0] = jnp.zeros((GRAD_ROWS, 128), F32)
        params_sum[0, pl.ds(start // 128, 1), :] = row[0:1, :128]
        params_sum[0, pl.ds(start // 128 + 1, 1), :] = row[0:1, 128:]

    def share(source, got, axis):
        slots = got.at[pl.ds(slot_at[axis], len(k.steps(axis)))]
        return k.send(axis, [(source, slots.at[s - 1]) for s in k.steps(axis)], slots)

    def take(wait, source, got, axis):
        wait.wait_recv()
        value = source[...]
        for s in k.steps(axis):
            value = value + got[slot_at[axis] + s - 1]
        return value

    def block_rows(block):
        return pl.ds(block * BLOCK, BLOCK)

    def conv_taps(first):
        last = {piece[0]: piece[1] for piece in CONV_GATHER}[first]

        @pl.loop(0, steps)
        def _(step):
            value = None
            for tap in range(first, last):
                term = dot(step_rows(padded, padded_by8, step, tap), side_by_side(conv_w, tap))
                value = term if value is None else value + term
            if first != TAP_ORDER[0]:
                value = value + conv_sum[at_step(step), :]
            conv_sum[at_step(step), :] = value

    def first_part(block, hat):
        start = window_rows(padded, padded_by8, block, REACH // 8).astype(F32)
        return start + hat * param(GAIN_ONE, D) + param(SHIFT_ONE, D)

    def conv_end(block):
        rows = block_rows(block)
        bent, tilt = gelu_pair(conv_sum[rows, :] + param(CONV_BIAS, D))
        hat, factor = normalize(bent)
        conv_sum[rows, :] = tilt * factor
        held[rows, :] = hat
        resid_low[rows, :] = first_part(block, hat).astype(BF)

    width = inner_w.shape[-1]
    groups = Y * 2

    def inner_piece(piece):
        rows = pl.ds(piece * STEP_ROWS, STEP_ROWS)
        for group in range(groups):
            first = group * width
            value = dot(resid_low[rows, :], inner_w[0, group // 2, group % 2].reshape(D, width))
            bent, tilt = gelu_pair(value + param(INNER_BIAS + first, width))
            active[rows, first : first + width] = bent.astype(BF)
            slope[rows, first : first + width] = tilt.astype(BF)

    outer_rows = outer_w.shape[6]

    def outer_dot(rows, part):
        size = outer_rows // OUTER_PARTS
        left = jnp.concatenate(
            [active[rows, i * outer_rows + part * size : i * outer_rows + (part + 1) * size] for i in range(H * L * X)],
            axis=1,
        )
        right = jnp.concatenate(
            [
                outer_w[0, g // 2, g % 2, :, :, :, part * size : (part + 1) * size, :].reshape(-1, 128)
                for g in range(groups)
            ],
            axis=1,
        )
        return dot(left, right)

    def outer_part(part):
        for step in range(steps):
            rows = pl.ds(step * STEP_ROWS, STEP_ROWS)
            value = outer_dot(rows, part)
            if part > 0:
                value = value + outer_sum[rows, :]
            outer_sum[rows, :] = value

    def outer_block(block):
        rows = block_rows(block)
        value = outer_dot(rows, OUTER_PARTS - 1) + param(OUTER_BIAS, D)
        if OUTER_PARTS > 1:
            value = value + outer_sum[rows, :]
        hat, factor = normalize(value)
        outer_sum[rows, :] = hat
        upstream = cot_buf[rows, :].astype(F32) * live(block)
        outer_low[rows, :] = normalize_back(upstream * param(GAIN_TWO, D), hat, factor).astype(BF)

    def block_end(block):
        rows = block_rows(block)
        value = resid_low[rows, :].astype(F32) + outer_sum[rows, :] * param(GAIN_TWO, D) + param(SHIFT_TWO, D)
        resid_low[rows, :] = (value * live(block)).astype(BF)

    def put_sums(first, value):
        for i in range(0, value.shape[1], 128):
            row = (first + i) // 128
            grads[0, row : row + 1, :] = value[0:1, i : i + 128]

    def late_sums(_):
        ones = jnp.ones((16, row_count), BF)
        put_sums(OUTER_BIAS, dot(ones, outer_low[...]))
        put_sums(INNER_BIAS, dot(ones, slope[...]))
        put_sums(CONV_BIAS, dot(ones, all_rows(padded_back, None, REACH // 8)))
        for block in range(blocks):
            rows = block_rows(block)
            add_grad(SHIFT_ONE, held[rows, :])
            add_grad(GAIN_TWO, cot_buf[rows, :].astype(F32) * live(block) * outer_sum[rows, :])

    def upstream_sum(block):
        add_grad(SHIFT_TWO, cot_buf[block_rows(block), :].astype(F32) * live(block))

    def outer_grad(piece):
        half, y = piece // Y, piece % Y
        size = outer_rows // 2
        left = jnp.concatenate(
            [active[:, i * outer_rows + half * size : i * outer_rows + (half + 1) * size] for i in range(H * L * X)],
            axis=1,
        )
        value = dot(left, outer_low[:, y * 256 : (y + 1) * 256], OVER_ROWS).astype(BF)
        for c in range(2):
            outer_partial[c, half, y] = value[:, c * 128 : (c + 1) * 128].reshape(H, L, X, size, 128)

    def hidden_piece(piece):
        step, group = piece // groups, piece % groups
        rows, first = pl.ds(step * STEP_ROWS, STEP_ROWS), group * width
        right = jnp.concatenate(
            [outer_w[0, y, c, group // L, group % L].reshape(width, 128) for y in range(Y) for c in range(2)], axis=1
        )
        value = dot(outer_low[rows, :], right, OVER_LANES) * slope[rows, first : first + width].astype(F32)
        slope[rows, first : first + width] = value.astype(BF)

    def inner_grad(piece):
        right = jnp.concatenate(
            [slope[:, g * width + piece * 128 : g * width + (piece + 1) * 128] for g in range(groups)], axis=1
        )
        value = dot(resid_low[...], right, OVER_ROWS).astype(BF)
        for g in range(groups):
            part = value[:, g * 128 : (g + 1) * 128]
            inner_partial[g % 2, piece, g // 2] = part.reshape(H, L, X, -1, 128)

    def resid_block(block):
        rows = block_rows(block)
        value = cot_buf[rows, :].astype(F32) * live(block)
        for g in range(groups):
            right = inner_w[0, g // 2, g % 2].reshape(D, width)
            value = value + dot(slope[rows, g * width : (g + 1) * width], right, OVER_LANES)
        hat = held[rows, :]
        held[rows, :] = value
        add_grad(GAIN_ONE, value * hat)
        back = normalize_back(value * param(GAIN_ONE, D), hat, conv_sum[rows, :])
        conv_sum[rows, :] = back

    conv_rows = conv_w.shape[6]

    def conv_grad(tap):
        left = all_rows(padded, None, REACH // 8)
        right = all_rows(padded_back, padded_by8, KERNEL_TAPS - 1 - tap)
        value = dot(left, right, OVER_ROWS).astype(BF)
        size = conv_rows // 2
        for g in range(groups):
            part = value[:, g * 128 : (g + 1) * 128].reshape(H, L, X, conv_rows, 128)
            for half in range(2):
                conv_partial[g % 2, half * KERNEL_TAPS + tap, g // 2] = part[:, :, :, half * size : (half + 1) * size]

    def token_piece(piece):
        step, part = piece // 3, piece % 3
        rows = pl.ds(step * STEP_ROWS, STEP_ROWS)
        value = held[rows, :]
        for tap in range(part * KERNEL_TAPS // 3, (part + 1) * KERNEL_TAPS // 3):
            value = value + dot(
                step_rows(padded_back, padded_by8, step, KERNEL_TAPS - 1 - tap),
                side_by_side(conv_w, tap),
                OVER_LANES,
            )
        if part == 2:
            value = live_rows(value, step)
        held[rows, :] = value

    def conv_finish(value, first):
        half, tap = first // KERNEL_TAPS, first % KERNEL_TAPS
        size = conv_rows // 2
        conv_out[pl.ds(tap, value.shape[0]), pl.ds(half * size, size), :] = value

    def inner_finish(value, first):
        for i in range(value.shape[0]):
            inner_out[:, (first + i) * 128 : (first + i + 1) * 128] = value[i]

    def outer_finish(value, first):
        size = outer_rows // 2
        outer_out[first * size : first * size + value.shape[0] * size, :] = value.reshape(-1, 128)

    params_sharing = Sharing(share, take, params_sum, params_got, "hlxyc")
    grads_sharing = Sharing(share, take, grads, grads_got, "cxylh")

    moves = {}
    for half in range(2):
        for first, last, axes in CONV_GATHER:
            size = conv_w.shape[6] // 2
            rows = (half * size, (half + 1) * size)
            piece = Gather(k, conv_in, conv_w, own[0], (first, last), rows, axes[half])
            moves["c" + str(first) + "ab"[half]] = piece
        for name, shard, whole, copied, kinds in (
            ("fi", inner_in, inner_w, own[1], INNER_GATHER),
            ("fo", outer_in, outer_w, own[2], OUTER_GATHER),
        ):
            size = whole.shape[6] // (2 * len(kinds))
            for i, axes in enumerate(kinds):
                at = (2 * i + half) * size
                moves[name + str(i) + "ab"[half]] = Gather(k, shard, whole, copied, (0, 1), (at, at + size), axes[half])
    for i, (name, first, last, axes) in enumerate(SCATTER):
        partial, pair, finish = {
            "C": (conv_partial, conv_pair, conv_finish),
            "FI": (inner_partial, inner_pair, inner_finish),
            "FO": (outer_partial, outer_pair, outer_finish),
        }[name.rstrip("0123456789ab")]
        held_at = sum(len(piece[3]) for piece in SCATTER[:i])
        moves[name] = Scatter(
            k, partial, pair, inboxes[held_at : held_at + len(axes)], (first, last), axes, finish
        )
    moves["P"] = params_sharing
    moves["G"] = grads_sharing

    def pad_tokens(_):
        rows_in.wait()
        grads[0] = jnp.zeros((GRAD_ROWS, 128), F32)
        pad(outer_low, padded, padded_by8)

    def pad_back(_):
        pad(conv_sum, padded_back, padded_by8)

    work = {
        "pad": pad_tokens,
        "conv": conv_taps,
        "epi": conv_end,
        "inner": inner_piece,
        "ups": upstream_sum,
        "op": outer_part,
        "outer": outer_block,
        "og": outer_grad,
        "hid": hidden_piece,
        "ig": inner_grad,
        "res": resid_block,
        "padb": pad_back,
        "sums": late_sums,
        "bo": block_end,
        "cg": conv_grad,
        "tok": token_piece,
    }
    out_copies = []
    own_params()
    params_sharing.send()
    for name in ORDER:
        if name == "ups0":
            cot_in.wait()
        if "." in name:
            moves[name.split(".")[0]].step()
        else:
            kind = name.rstrip("0123456789")
            work[kind](int(name[len(kind) :] or 0))
        if name == "sums":
            grads_sharing.send()
        if name == "bo5":
            out_copies.append(local(0, resid_low, block_out))
        if name in ("tok2", "tok5", "tok8"):
            rows = pl.ds((int(name[3:]) // 3) * STEP_ROWS, STEP_ROWS)
            out_copies.append(local(5 + int(name[3:]) // 3, held.at[rows], grad_tokens.at[rows]))
    params_out[...] = grads[5]
    for copy in out_copies:
        copy.wait()
    k.finish()


def run_kernel(sizes, lengths, small, tokens, cotangent, conv_shard, inner_shard, outer_shard):
    H, L, X, Y = (sizes[axis] for axis in "hlxy")
    taps, conv_rows, lanes = conv_shard.shape
    inner_rows, width = inner_shard.shape
    outer_rows = outer_shard.shape[0]
    rows = tokens.shape[0]
    blocks = rows // BLOCK
    inner_shard, outer_shard = inner_shard[None], outer_shard[None]

    def whole(shard):
        return pltpu.VMEM((shard.shape[0], Y, 2, H, L, X) + shard.shape[1:], BF)

    def pair(count, r):
        return pltpu.VMEM((count, Y, H, L, X, r, 128), BF)

    def partial(count, r):
        return pltpu.VMEM((2, count, Y, H, L, X, r, 128), BF)

    rows_of = {"C": conv_rows // 2, "FI": inner_rows, "FO": outer_rows // 2}
    parts_of = {"C": 2 * taps, "FI": width // 128, "FO": 2}
    inboxes = []
    for name, first, last, axes in SCATTER:
        r = rows_of[name.rstrip("0123456789ab")]
        inboxes += [pltpu.VMEM(shape, BF) for shape in inbox_shapes(sizes, last - first, r, axes)]
    partners = H + L + X + Y - 3
    orders = [piece[2] for piece in CONV_GATHER] + list(INNER_GATHER) + list(OUTER_GATHER)
    copies = sum(1 + sum(3 if axis in TOGETHER else 1 for axis in axes) for order in orders for axes in order)
    copies += sum(1 + len(piece[3]) for piece in SCATTER) + 10
    padded = BLOCK + 2 * REACH
    scratch = [whole(conv_shard), whole(inner_shard), whole(outer_shard)]
    scratch += [pltpu.VMEM((partners, GRAD_ROWS, 128), F32), pltpu.VMEM((6, GRAD_ROWS, 128), F32)]
    scratch += [
        pltpu.VMEM((rows, D), BF),
        pltpu.VMEM((blocks, padded, D), BF),
        pltpu.VMEM((blocks, padded - 16, D), BF),
        pltpu.VMEM((blocks, padded, D), BF),
        pltpu.VMEM((padded, D), F32),
        pltpu.VMEM((rows, D), F32),
        pltpu.VMEM((rows, D), F32),
        pltpu.VMEM((rows, D), F32),
        pltpu.VMEM((rows, D), BF),
        pltpu.VMEM((rows, FF), BF),
        pltpu.VMEM((rows, FF), BF),
        pltpu.VMEM((rows, D), BF),
    ]
    scratch += [partial(parts_of[name], rows_of[name]) for name in ("C", "FI", "FO")]
    scratch += [pair(parts_of[name], rows_of[name]) for name in ("C", "FI", "FO")]
    scratch += [pltpu.VMEM((6, GRAD_ROWS, 128), F32), pltpu.VMEM((partners, GRAD_ROWS, 128), F32)]
    scratch += [pltpu.SMEM(lengths.shape, jnp.int32), pltpu.VMEM(small.shape, BF)]
    scratch += [pltpu.SemaphoreType.DMA((SEND_SLOTS,)), pltpu.SemaphoreType.DMA((copies,)), pltpu.SemaphoreType.DMA((10,))]
    scratch += inboxes
    far = pl.BlockSpec(memory_space=pl.ANY)
    near = pl.BlockSpec(memory_space=pltpu.VMEM)
    return pl.pallas_call(
        functools.partial(kernel, sizes),
        out_shape=[
            jax.ShapeDtypeStruct((rows, D), BF),
            jax.ShapeDtypeStruct((rows, D), F32),
            jax.ShapeDtypeStruct(conv_shard.shape, F32),
            jax.ShapeDtypeStruct(inner_shard.shape[1:], F32),
            jax.ShapeDtypeStruct(outer_shard.shape[1:], F32),
            jax.ShapeDtypeStruct((GRAD_ROWS, 128), F32),
        ],
        in_specs=[far] * 7,
        out_specs=[far, far, near, near, near, near],
        scratch_shapes=scratch,
        compiler_params=pltpu.CompilerParams(
            collective_id=0, has_side_effects=True, vmem_limit_bytes=VMEM_LIMIT
        ),
    )(lengths, small, tokens, cotangent, conv_shard, inner_shard, outer_shard)


def hand_over(parts, grads, *refs):
    count = len(parts)
    sources, targets, small = refs[:count], refs[count : 2 * count], refs[2 * count]
    held, grads_held, sems = refs[2 * count + 1 : 3 * count + 1], refs[-2], refs[-1]
    first = pltpu.make_async_copy(grads, grads_held, sems.at[0, sum(parts)])
    pieces = []
    for source, target, middle, count in zip(sources, targets, held, parts):
        size = source.shape[0] // count
        pieces += [tuple(ref.at[pl.ds(i * size, size)] for ref in (source, middle, target)) for i in range(count)]
    ins = [pltpu.make_async_copy(s, m, sems.at[0, i]) for i, (s, m, _) in enumerate(pieces)]
    outs = [pltpu.make_async_copy(m, t, sems.at[1, i]) for i, (_, m, t) in enumerate(pieces)]
    for copy in ins:
        copy.start()
    first.start()
    for come, go in zip(ins, outs):
        come.wait()
        go.start()
    first.wait()
    size = small.shape[0]
    start = (lax.axis_index("wide") * lax.axis_size("narrow") + lax.axis_index("narrow")) * size
    row = jnp.concatenate([grads_held[pl.ds(start // 128, 1), :], grads_held[pl.ds(start // 128 + 1, 1), :]], axis=1)
    row = pltpu.roll(jnp.broadcast_to(row, (8, 256)), 256 - start % 128, 1)
    small[...] = row[0:1, :size].reshape(size)
    for copy in outs:
        copy.wait()


def settle(share, params_grad, arrays):
    far = pl.BlockSpec(memory_space=pl.ANY)
    near = pl.BlockSpec(memory_space=pltpu.VMEM)
    parts = [max(1, a.size * a.dtype.itemsize >> 20) for a in arrays]
    return pl.pallas_call(
        functools.partial(hand_over, parts),
        out_shape=[jax.ShapeDtypeStruct(a.shape, a.dtype) for a in arrays] + [jax.ShapeDtypeStruct((share,), F32)],
        in_specs=[far] * (len(arrays) + 1),
        out_specs=[far] * len(arrays) + [near],
        scratch_shapes=[pltpu.VMEM(a.shape, a.dtype) for a in arrays]
        + [pltpu.VMEM(params_grad.shape, F32), pltpu.SemaphoreType.DMA((2, sum(parts) + 1))],
        compiler_params=pltpu.CompilerParams(vmem_limit_bytes=VMEM_LIMIT),
    )(params_grad, *arrays)


def fused(
    sizes, tokens, window_lengths, conv_weight, feedforward_input_weight, ffn_out, small_params, cotangent
):
    block_out, grad_tokens, conv_grad, inner_grad, outer_grad, params_grad = run_kernel(
        sizes, window_lengths, small_params, tokens, cotangent, conv_weight, feedforward_input_weight, ffn_out
    )
    return settle(small_params.shape[0], params_grad, [block_out, grad_tokens, conv_grad, inner_grad, outer_grad])


def solution(mesh):
    wide, narrow = mesh.shape["wide"], mesh.shape["narrow"]
    X = max(narrow // 2, 1)
    sizes = {"h": wide // X // 2, "l": 2, "x": X, "y": X}

    def step(*arrays):
        rows = arrays[0].shape[0]
        inner, outer = arrays[3].shape, arrays[4].shape
        whole_lanes = all(a.shape[-1] % 128 == 0 for a in arrays[2:5])
        fits = rows == 3 * STEP_ROWS and narrow == 4 and wide == 8 and inner[1] == X * outer[0] and whole_lanes
        small = arrays[5].shape[0]
        fits = fits and small % 32 == 0 and small <= 160
        if fits:
            return fused(sizes, *arrays)
        return shards(*arrays)

    return jax.shard_map(
        step,
        mesh=mesh,
        in_specs=(
            P(("wide", "narrow"), None),
            P(("wide", "narrow"), None),
            P(None, "wide", "narrow"),
            P("wide", "narrow"),
            P("wide", "narrow"),
            P(("wide", "narrow")),
            P(("wide", "narrow"), None),
        ),
        out_specs=(
            P(("wide", "narrow"), None),
            P(("wide", "narrow"), None),
            P(None, "wide", "narrow"),
            P("wide", "narrow"),
            P("wide", "narrow"),
            P(("wide", "narrow")),
        ),
        check_vma=False,
    )
```

```python
import functools

import jax
import jax.numpy as jnp
from jax import lax
from jax.experimental import pallas as pl
from jax.experimental.pallas import tpu as pltpu
from jax.sharding import PartitionSpec as P

D = 512
FF = 2048
KERNEL_TAPS = 9
DILATION_STEP = 8
EPSILON = 1e-05

def layer_norm(values, norm_gain, norm_shift):
    centre = values - jnp.mean(values, axis=-1, keepdims=True)
    spread = jnp.mean(centre * centre, axis=-1, keepdims=True)
    return centre * lax.rsqrt(spread + EPSILON) * norm_gain + norm_shift


def window_masks(lengths, row_count):
    bounds = jnp.cumsum(lengths)
    places = jnp.arange(row_count, dtype=jnp.int32)
    segment_ids = jnp.sum((places[:, None] >= bounds[None, :]).astype(jnp.int32), axis=1)
    live_rows = (places < bounds[-1]).astype(jnp.float32)
    tap_valid = []
    for index_of_tap in range(KERNEL_TAPS):
        tap_displacement = (index_of_tap - KERNEL_TAPS // 2) * DILATION_STEP
        source = places + tap_displacement
        inside = (source >= 0) & (source < row_count)
        same_window = jnp.roll(segment_ids, -tap_displacement) == segment_ids
        tap_valid.append((inside & same_window).astype(jnp.float32))
    return (live_rows, tap_valid)


def split_params(flat_params):
    return (
        flat_params[0:D],
        flat_params[D : 2 * D],
        flat_params[2 * D : 3 * D],
        flat_params[3 * D : 3 * D + FF],
        flat_params[3 * D + FF : 4 * D + FF],
        flat_params[4 * D + FF : 5 * D + FF],
        flat_params[5 * D + FF : 6 * D + FF],
    )


def branch_one(conv_sum, conv_bias, gain_one, shift_one):
    return layer_norm(jax.nn.gelu(conv_sum + conv_bias), gain_one, shift_one)


def branch_two(outer_sum, outer_bias, gain_two, shift_two):
    return layer_norm(outer_sum + outer_bias, gain_two, shift_two)


def fetch_forward(conv_weight, feedforward_input_weight, ffn_out, small_params):
    narrow_set = (
        lax.all_gather(conv_weight, "narrow", axis=2, tiled=True),
        lax.all_gather(feedforward_input_weight, "narrow", axis=1, tiled=True),
        lax.all_gather(ffn_out, "narrow", axis=1, tiled=True),
        lax.all_gather(small_params, "narrow", axis=0, tiled=True),
    )
    return (
        lax.all_gather(narrow_set[0], "wide", axis=1, tiled=True),
        lax.all_gather(narrow_set[1], "wide", axis=0, tiled=True),
        lax.all_gather(narrow_set[2], "wide", axis=0, tiled=True),
        lax.all_gather(narrow_set[3], "wide", axis=0, tiled=True),
    )


def shards(
    tokens, window_lengths, conv_weight, feedforward_input_weight, ffn_out, small_params, cotangent
):
    row_count = tokens.shape[0]
    block_size = min(512, row_count)
    live_rows, tap_valid = window_masks(window_lengths[0], row_count)
    weights = fetch_forward(conv_weight, feedforward_input_weight, ffn_out, small_params)
    conv_full, inner_full, outer_full = (weights[0], weights[1], weights[2])
    pieces = split_params(weights[3].astype(jnp.float32))
    start_rows = tokens * live_rows[:, None].astype(jnp.bfloat16)
    conv_sum = jnp.zeros((row_count, D), jnp.float32)
    for index_of_tap in range(KERNEL_TAPS):
        tap_displacement = (index_of_tap - KERNEL_TAPS // 2) * DILATION_STEP
        shifted = jnp.roll(start_rows, -tap_displacement, axis=0) * tap_valid[index_of_tap][
            :, None
        ].astype(jnp.bfloat16)
        conv_sum = conv_sum + jnp.dot(
            shifted, conv_full[index_of_tap], preferred_element_type=jnp.float32
        )
    branch_out, pull_one = jax.vjp(branch_one, conv_sum, pieces[0], pieces[1], pieces[2])
    residual_one = start_rows.astype(jnp.float32) + branch_out
    residual_low = residual_one.astype(jnp.bfloat16)
    outer_parts = []
    for first_row in range(0, row_count, block_size):
        inner_sum = (
            jnp.dot(
                residual_low[first_row : first_row + block_size],
                inner_full,
                preferred_element_type=jnp.float32,
            )
            + pieces[3]
        )
        active = jax.nn.gelu(inner_sum).astype(jnp.bfloat16)
        outer_parts.append(jnp.dot(active, outer_full, preferred_element_type=jnp.float32))
    outer_sum = jnp.concatenate(outer_parts, axis=0)
    normed, pull_two = jax.vjp(branch_two, outer_sum, pieces[4], pieces[5], pieces[6])
    block_out = (live_rows[:, None] * (residual_one + normed)).astype(jnp.bfloat16)
    upstream = cotangent.astype(jnp.float32) * live_rows[:, None]
    d_outer, d_outer_bias, d_gain_two, d_shift_two = pull_two(upstream)
    outer_low = d_outer.astype(jnp.bfloat16)
    grad_in = jnp.zeros((D, FF), jnp.float32)
    grad_out = jnp.zeros((FF, D), jnp.float32)
    inner_bias_grad = jnp.zeros((FF,), jnp.float32)
    resid_parts = []
    for first_row in range(0, row_count, block_size):
        rows_low = residual_low[first_row : first_row + block_size]
        outer_rows = outer_low[first_row : first_row + block_size]
        inner_sum = jnp.dot(rows_low, inner_full, preferred_element_type=jnp.float32) + pieces[3]
        active_full, pull_gelu = jax.vjp(jax.nn.gelu, inner_sum)
        active = active_full.astype(jnp.bfloat16)
        d_active = jnp.einsum(
            "rd,fd->rf", outer_rows, outer_full, preferred_element_type=jnp.float32
        )
        d_inner = pull_gelu(d_active)[0]
        inner_bias_grad = inner_bias_grad + jnp.sum(d_inner, axis=0)
        inner_low = d_inner.astype(jnp.bfloat16)
        grad_in = grad_in + jnp.einsum(
            "rd,rf->df", rows_low, inner_low, preferred_element_type=jnp.float32
        )
        grad_out = grad_out + jnp.einsum(
            "rf,rd->fd", active, outer_rows, preferred_element_type=jnp.float32
        )
        resid_parts.append(
            jnp.einsum("rf,df->rd", inner_low, inner_full, preferred_element_type=jnp.float32)
        )
    d_resid = upstream + jnp.concatenate(resid_parts, axis=0)
    d_conv, d_conv_bias, d_gain_one, d_shift_one = pull_one(d_resid)
    convolution_reduced = d_conv.astype(jnp.bfloat16)
    conv_grads = []
    d_start = d_resid
    for index_of_tap in range(KERNEL_TAPS):
        tap_displacement = (index_of_tap - KERNEL_TAPS // 2) * DILATION_STEP
        tap_mask = tap_valid[index_of_tap][:, None]
        shifted = jnp.roll(start_rows, -tap_displacement, axis=0) * tap_mask.astype(jnp.bfloat16)
        conv_grads.append(
            jnp.einsum(
                "ri,ro->io", shifted, convolution_reduced, preferred_element_type=jnp.float32
            )
        )
        back_rows = jnp.einsum(
            "ro,io->ri",
            convolution_reduced,
            conv_full[index_of_tap],
            preferred_element_type=jnp.float32,
        )
        d_start = d_start + jnp.roll(back_rows * tap_mask, tap_displacement, axis=0)
    grad_tokens = d_start * live_rows[:, None]
    convolution_weight_gradient = jnp.stack(conv_grads, axis=0)
    grad_flat = jnp.concatenate(
        [
            d_conv_bias,
            d_gain_one,
            d_shift_one,
            inner_bias_grad,
            d_outer_bias,
            d_gain_two,
            d_shift_two,
        ],
        axis=0,
    )
    wide_sums = (
        lax.psum_scatter(convolution_weight_gradient, "wide", scatter_dimension=1, tiled=True),
        lax.psum_scatter(grad_in, "wide", scatter_dimension=0, tiled=True),
        lax.psum_scatter(grad_out, "wide", scatter_dimension=0, tiled=True),
        lax.psum_scatter(grad_flat, "wide", scatter_dimension=0, tiled=True),
    )
    owned = (
        lax.psum_scatter(wide_sums[0], "narrow", scatter_dimension=2, tiled=True),
        lax.psum_scatter(wide_sums[1], "narrow", scatter_dimension=1, tiled=True),
        lax.psum_scatter(wide_sums[2], "narrow", scatter_dimension=1, tiled=True),
        lax.psum_scatter(wide_sums[3], "narrow", scatter_dimension=0, tiled=True),
    )
    owned_flat = owned[3]
    return (block_out, grad_tokens, owned[0], owned[1], owned[2], owned_flat)

MESH = pl.DeviceIdType.MESH
BF = jnp.bfloat16
F32 = jnp.float32
BLOCK = 256
REACH = KERNEL_TAPS // 2 * DILATION_STEP
STEP_ROWS = 512
GRAD_ROWS = 40
VMEM_LIMIT = 63 << 20
SEND_SLOTS = 20
GELU_A = 0.7978845608028654
GELU_B = 0.044715
CONV_GATHER = (
    (0, 2, ('hlxy', 'hlyx')),
    (2, 3, ('zxy', 'zyx')),
    (3, 4, ('zyx', 'zxy')),
    (4, 6, ('hxly', 'hylx')),
    (6, 8, ('hxly', 'hylx')),
    (8, 9, ('hxly', 'hylx')),
)
INNER_GATHER = (('hxly', 'hylx'), ('hylx', 'hxly'))
OUTER_GATHER = (('hxly', 'hylx'), ('hyxl', 'hxyl'))
SCATTER = (
    ('FO0', 0, 1, 'zxy'),
    ('FO1', 1, 2, 'qlh'),
    ('FI0', 0, 2, 'ylhx'),
    ('FI1', 2, 4, 'xlyh'),
    ('C0a', 0, 2, 'ylhx'),
    ('C0b', 9, 11, 'xlhy'),
    ('C2a', 2, 4, 'ylxh'),
    ('C2b', 11, 13, 'xlyh'),
    ('C4a', 4, 6, 'ylxh'),
    ('C4b', 13, 15, 'xlyh'),
    ('C6a', 6, 8, 'xylh'),
    ('C6b', 15, 17, 'yxlh'),
    ('C8a', 8, 9, 'xyhl'),
    ('C8b', 17, 18, 'yxhl'),
)
TAP_ORDER = (0,)
KINDS = ("pad", "ups", "conv", "epi", "inner", "op", "outer", "og", "hid", "ig", "res", "padb", "cg", "sums", "bo", "tok")
ORDER = (
    16, 26, 17, 0, 27, 1, 1, 1, 18, 1, 1, 1, 28, 19, 50, 29, 16, 20, 17, 26, 27, 30, 18, 21, 31, 22, 28, 32,
    50, 17, 19, 23, 27, 29, 16, 33, 18, 24, 28, 26, 34, 50, 19, 20, 30, 17, 21, 31, 22, 25, 27, 17, 29, 32,
    23, 27, 28, 16, 35, 33, 28, 24, 26, 18, 50, 20, 30, 50, 34, 18, 19, 21, 31, 29, 22, 25, 35, 32, 20, 16,
    26, 30, 23, 16, 26, 2, 19, 29, 21, 31, 22, 33, 24, 25, 2, 19, 29, 32, 34, 2, 20, 30, 35, 2, 20, 30, 21,
    31, 23, 33, 25, 2, 21, 31, 22, 24, 34, 32, 35, 2, 22, 3, 32, 3, 3, 23, 33, 25, 3, 3, 3, 23, 33, 25, 4, 24,
    34, 35, 4, 24, 34, 35, 4, 5, 6, 6, 6, 6, 6, 6, 7, 7, 36, 7, 7, 36, 37, 8, 8, 8, 8, 8, 8, 37, 8, 8, 8, 8,
    8, 8, 9, 9, 38, 9, 9, 38, 39, 10, 10, 10, 39, 10, 10, 10, 37, 11, 12, 12, 40, 41, 12, 38, 36, 40, 41, 12,
    37, 42, 43, 12, 39, 12, 42, 43, 44, 45, 12, 36, 12, 38, 44, 45, 46, 47, 12, 40, 48, 49, 13, 41, 46, 47,
    14, 14, 42, 14, 14, 14, 39, 48, 14, 15, 38, 43, 49, 15, 40, 44, 51, 15, 41, 46, 47, 15, 42, 45, 48, 15,
    39, 43, 51, 49, 15, 40, 44, 47, 46, 15, 41, 42, 48, 15, 43, 45, 49, 51, 15, 44, 46, 47, 36, 37, 38, 39,
    40, 41, 42, 48, 45, 43, 51, 49, 44, 46, 48, 47, 45, 49, 51,
)


OUTER_PARTS = min(len(OUTER_GATHER), 2)


TOGETHER = {"z": "hl", "q": "xy"}


def spread(axes):
    return "".join(TOGETHER.get(axis, axis) for axis in axes)


def inbox_shapes(sizes, count, rows, axes):
    left = dict(sizes)
    shapes = []
    for axis in axes:
        senders = 1
        for name in spread(axis):
            senders *= left.pop(name)
        senders -= 1
        rest = tuple(left[name] for name in "yhlx" if name in left)
        shapes.append((senders, count) + rest + (rows, 128))
    return shapes


class Links:
    def __init__(self, sizes, send_sems, recv_sems):
        self.sizes = dict(sizes, c=2)
        wide, narrow = lax.axis_index("wide"), lax.axis_index("narrow")
        z = wide // sizes["x"]
        self.at = {
            "h": z // sizes["l"], "l": z % sizes["l"], "x": wide % sizes["x"], "y": narrow // 2, "c": narrow % 2
        }
        self.send_sems, self.recv_sems = send_sems, recv_sems
        self.used = 0
        self.sent = [None] * SEND_SLOTS

    def there(self, axis, step):
        names = TOGETHER.get(axis, axis)
        index, count = 0, 1
        for name in names:
            index, count = index * self.sizes[name] + self.at[name], count * self.sizes[name]
        index = lax.rem(index + step, count)
        at = dict(self.at)
        for name in reversed(names):
            at[name], index = index % self.sizes[name], index // self.sizes[name]
        return at

    def device(self, axis, step):
        at = self.there(axis, step)
        return ((at["h"] * self.sizes["l"] + at["l"]) * self.sizes["x"] + at["x"], at["y"] * 2 + at["c"])

    def steps(self, axis):
        count = 1
        for name in TOGETHER.get(axis, axis):
            count *= self.sizes[name]
        return range(1, count)

    def send(self, axis, pairs, total, only=None):
        if total is None:
            steps = list(zip(self.steps(axis), pairs))
            return Each([self.send(axis, [pair], pair[1], step) for step, pair in steps])
        index, slot = self.used, self.used % SEND_SLOTS
        self.used += 1
        if self.sent[slot] is not None:
            self.sent[slot].wait_send()

        def copy(source, target, step):
            return pltpu.make_async_remote_copy(
                src_ref=source,
                dst_ref=target,
                send_sem=self.send_sems.at[slot],
                recv_sem=self.recv_sems.at[index],
                device_id=self.device(axis, step),
                device_id_type=MESH,
            )

        for step, (source, target) in zip(self.steps(axis) if only is None else [only], pairs):
            copy(source, target, step).start()
        self.sent[slot] = copy(total, total, 1)
        return self.sent[slot]

    def barrier(self):
        semaphore = pltpu.get_barrier_semaphore()
        partners = [self.device(axis, s) for axis in "zqc" for s in self.steps(axis)]
        for partner in partners:
            pl.semaphore_signal(semaphore, inc=1, device_id=partner, device_id_type=MESH)
        pl.semaphore_wait(semaphore, len(partners))

    def finish(self):
        for copies in self.sent:
            if copies is not None:
                copies.wait_send()


class Each:
    def __init__(self, copies):
        self.copies = copies

    def wait_recv(self):
        for copy in self.copies:
            copy.wait_recv()


class Once:
    def __init__(self, copy):
        self.copy = copy

    def wait(self):
        if self.copy is not None:
            self.copy.wait()
        self.copy = None


class Gather:
    def __init__(self, links, shard, whole, own, taps, rows, axes):
        self.links, self.shard, self.whole, self.own = links, shard, whole, own
        self.taps, self.rows = pl.ds(taps[0], taps[1] - taps[0]), pl.ds(rows[0], rows[1] - rows[0])
        self.axes = axes + "c"
        self.stage = 0

    def region(self, axis=None):
        k, done = self.links, spread(self.axes[: self.stage])
        places = {}
        for name in "yhlx":
            places[name] = k.at[name]
            if name in done:
                places[name] = slice(None)
            elif name == axis:
                places[name] = pl.ds(0, len(k.steps(axis)))
        return self.whole.at[
            self.taps, places["y"], k.at["c"], places["h"], places["l"], places["x"], self.rows
        ]

    def step(self):
        k = self.links
        if self.stage > 0:
            self.wait.wait_recv()
        if self.stage == len(self.axes):
            return
        target = self.region()
        source = target
        if self.stage == 0:
            source = self.shard.at[self.taps, self.rows]
        else:
            self.own.wait()
        axis = self.axes[self.stage]
        total = None if axis in TOGETHER else self.region(axis)
        self.wait = k.send(axis, [(source, target) for _ in k.steps(axis)], total)
        self.stage += 1


class Scatter:
    def __init__(self, links, partial, pair, inboxes, parts, axes, finish):
        self.links, self.partial, self.pair, self.inboxes = links, partial, pair, inboxes
        self.parts = pl.ds(parts[0], parts[1] - parts[0])
        self.first, self.axes, self.finish = parts[0], axes, finish
        self.stage = 0

    def region(self, done, axis="", at=None):
        places = []
        for name in "yhlx":
            own = self.links.at[name] if name in spread(done) else slice(None)
            places.append(at[name] if name in spread(axis) else own)
        return (self.parts, *places)

    def step(self):
        k, stage, pair = self.links, self.stage, self.pair
        self.stage += 1
        if stage == 0:
            whole = pair.at[self.parts]
            self.wait = k.send("c", [(self.partial.at[1 - k.at["c"], self.parts], whole)], whole)
            return
        self.wait.wait_recv()
        held = self.region(self.axes[: stage - 1])
        if stage == 1:
            came = [self.partial[k.at["c"], self.parts]]
        else:
            inbox = self.inboxes[stage - 2]
            came = [inbox[i] for i in range(inbox.shape[0])]
        if stage > len(self.axes):
            total = pair[held].astype(F32)
            for part in came:
                total = total + part.astype(F32)
            self.finish(total, self.first)
            return
        value = pair[held]
        for part in came:
            value = value + part
        pair[held] = value
        axis = self.axes[stage - 1]
        done = self.axes[: stage - 1]
        inbox = self.inboxes[stage - 1]
        self.wait = k.send(
            axis,
            [
                (pair.at[self.region(done, axis, k.there(axis, s))], inbox.at[s - 1])
                for s in k.steps(axis)
            ],
            inbox,
        )


class Sharing:
    def __init__(self, share, take, held, got, axes):
        self.share, self.take, self.held, self.got, self.axes = share, take, held, got, axes
        self.stage = 0

    def send(self):
        self.wait = self.share(self.held.at[self.stage], self.got, self.axes[self.stage])

    def step(self):
        value = self.take(self.wait, self.held.at[self.stage], self.got, self.axes[self.stage])
        self.stage += 1
        self.held[self.stage] = value
        if self.stage < len(self.axes):
            self.send()


def gelu_pair(value):
    square = value * value
    bend = jnp.tanh(value * (GELU_A + (GELU_A * GELU_B) * square))
    share = 0.5 + 0.5 * bend
    slope = share + (0.5 * value) * ((1.0 - bend * bend) * (GELU_A + (3 * GELU_A * GELU_B) * square))
    return value * share, slope


def normalize(value):
    centre = value - jnp.mean(value, axis=-1, keepdims=True)
    factor = lax.rsqrt(jnp.mean(centre * centre, axis=-1, keepdims=True) + EPSILON)
    return centre * factor, factor


def normalize_back(grad, hat, factor):
    return factor * (
        grad
        - jnp.mean(grad, axis=-1, keepdims=True)
        - hat * jnp.mean(grad * hat, axis=-1, keepdims=True)
    )


def side_by_side(whole, tap):
    lanes = whole.shape[-1]
    return jnp.concatenate(
        [whole[tap, y, c].reshape(-1, lanes) for y in range(whole.shape[1]) for c in range(2)], axis=1
    )


def dot(left, right, over=((1,), (0,))):
    return lax.dot_general(left, right, (over, ((), ())), preferred_element_type=F32)


OVER_ROWS = ((0,), (0,))
OVER_LANES = ((1,), (1,))


def kernel(
    sizes, lengths_in, small_in, tokens, cotangent, conv_in, inner_in, outer_in,
    block_out, grad_tokens, conv_out, inner_out, outer_out, params_out,
    conv_w, inner_w, outer_w, params_got, params_sum,
    cot_buf, padded, padded_by8, padded_back, stage, conv_sum, held, outer_sum, resid_low, active, slope, outer_low,
    conv_partial, inner_partial, outer_partial, conv_pair, inner_pair, outer_pair,
    grads, grads_got, lengths, small, send_sems, recv_sems, local_sems, *inboxes,
):
    k = Links(sizes, send_sems, recv_sems)
    H, L, X, Y = (sizes[axis] for axis in "hlxy")
    row_count = tokens.shape[0]
    blocks = row_count // BLOCK
    steps = row_count // STEP_ROWS
    per_step = STEP_ROWS // BLOCK

    def local(index, source, target):
        copy = pltpu.make_async_copy(source, target, local_sems.at[index])
        copy.start()
        return copy

    small_copy = local(8, small_in, small)
    lengths_copy = local(9, lengths_in, lengths)
    rows_in = local(0, tokens, outer_low)
    own = [
        Once(local(1 + i, shard, whole.at[:, k.at["y"], k.at["c"], k.at["h"], k.at["l"], k.at["x"]]))
        for i, (shard, whole) in enumerate(((conv_in, conv_w), (inner_in, inner_w), (outer_in, outer_w)))
    ]
    cot_in = local(4, cotangent, cot_buf)
    k.barrier()

    lengths_copy.wait()

    bounds = []
    total = 0
    for slot in range(lengths.shape[1]):
        total = total + lengths[0, slot]
        bounds.append(total)

    def window(block):
        number = 0
        for bound in bounds:
            number = number + jnp.where(block * BLOCK >= bound, 1, 0)
        return number

    def live(block):
        return jnp.where(block * BLOCK < total, 1.0, 0.0).astype(F32)

    def joined(block):
        return jnp.where(window(block) == window(block + 1), 1.0, 0.0).astype(F32) * live(block)

    def pad(source, target, target_by8):
        for b in range(blocks):
            at = b * BLOCK
            if b > 0:
                stage[0:REACH] = source[at - REACH : at].astype(F32) * joined(b - 1)
            else:
                stage[0:REACH] = jnp.zeros((REACH, D), F32)
            stage[REACH : REACH + BLOCK] = source[at : at + BLOCK].astype(F32) * live(b)
            if b < blocks - 1:
                stage[REACH + BLOCK :] = source[at + BLOCK : at + BLOCK + REACH].astype(F32) * joined(b)
            else:
                stage[REACH + BLOCK :] = jnp.zeros((REACH, D), F32)
            target[b] = stage[...].astype(BF)
            target_by8[b] = stage[8 : BLOCK + 2 * REACH - 8].astype(BF)

    def window_rows(source, source_by8, block, place):
        if place % 2 == 0:
            return source[block, pl.ds(8 * place, BLOCK), :]
        return source_by8[block, pl.ds(8 * (place - 1), BLOCK), :]

    def step_rows(source, source_by8, step, place):
        return jnp.concatenate(
            [window_rows(source, source_by8, step * per_step + j, place) for j in range(per_step)], axis=0
        )

    def all_rows(source, source_by8, place):
        return jnp.concatenate([window_rows(source, source_by8, b, place) for b in range(blocks)], axis=0)

    def at_step(step):
        return pl.ds(pl.multiple_of(step * STEP_ROWS, STEP_ROWS), STEP_ROWS)

    def live_rows(value, step):
        return jnp.concatenate(
            [value[j * BLOCK : (j + 1) * BLOCK] * live(step * per_step + j) for j in range(per_step)], axis=0
        )

    def param(first, width):
        return jnp.concatenate(
            [params_sum[5, pl.ds((first + i) // 128, 1), :] for i in range(0, width, 128)], axis=1
        )

    def add_grad(first, value):
        summed = jnp.sum(value, axis=0, keepdims=True)
        for i in range(0, summed.shape[1], 128):
            row = (first + i) // 128
            grads[0, row : row + 1, :] = grads[0, row : row + 1, :] + summed[:, i : i + 128]

    CONV_BIAS, GAIN_ONE, SHIFT_ONE, INNER_BIAS = 0, D, 2 * D, 3 * D
    OUTER_BIAS, GAIN_TWO, SHIFT_TWO = 3 * D + FF, 4 * D + FF, 5 * D + FF

    slot_at, slots = {}, 0
    for axis in "hlxyc":
        slot_at[axis], slots = slots, slots + len(k.steps(axis))

    def own_params():
        small_copy.wait()
        count = small.shape[0]
        wide, narrow = k.device("c", 0)
        start = (wide * 2 * Y + narrow) * count
        row = small[...].astype(F32).reshape(1, count)
        row = jnp.concatenate([row, jnp.zeros((1, 256 - count), F32)], axis=1)
        row = pltpu.roll(jnp.broadcast_to(row, (8, 256)), start % 128, 1)
        params_sum[0] = jnp.zeros((GRAD_ROWS, 128), F32)
        params_sum[0, pl.ds(start // 128, 1), :] = row[0:1, :128]
        params_sum[0, pl.ds(start // 128 + 1, 1), :] = row[0:1, 128:]

    def share(source, got, axis):
        slots = got.at[pl.ds(slot_at[axis], len(k.steps(axis)))]
        return k.send(axis, [(source, slots.at[s - 1]) for s in k.steps(axis)], slots)

    def take(wait, source, got, axis):
        wait.wait_recv()
        value = source[...]
        for s in k.steps(axis):
            value = value + got[slot_at[axis] + s - 1]
        return value

    def block_rows(block):
        return pl.ds(block * BLOCK, BLOCK)

    def conv_taps(first):
        last = {piece[0]: piece[1] for piece in CONV_GATHER}[first]

        @pl.loop(0, steps)
        def _(step):
            value = None
            for tap in range(first, last):
                term = dot(step_rows(padded, padded_by8, step, tap), side_by_side(conv_w, tap))
                value = term if value is None else value + term
            if first != TAP_ORDER[0]:
                value = value + conv_sum[at_step(step), :]
            conv_sum[at_step(step), :] = value

    def first_part(block, hat):
        start = window_rows(padded, padded_by8, block, REACH // 8).astype(F32)
        return start + hat * param(GAIN_ONE, D) + param(SHIFT_ONE, D)

    def conv_end(block):
        rows = block_rows(block)
        bent, tilt = gelu_pair(conv_sum[rows, :] + param(CONV_BIAS, D))
        hat, factor = normalize(bent)
        conv_sum[rows, :] = tilt * factor
        held[rows, :] = hat
        resid_low[rows, :] = first_part(block, hat).astype(BF)

    width = inner_w.shape[-1]
    groups = Y * 2

    def inner_piece(piece):
        rows = pl.ds(piece * STEP_ROWS, STEP_ROWS)
        for group in range(groups):
            first = group * width
            value = dot(resid_low[rows, :], inner_w[0, group // 2, group % 2].reshape(D, width))
            bent, tilt = gelu_pair(value + param(INNER_BIAS + first, width))
            active[rows, first : first + width] = bent.astype(BF)
            slope[rows, first : first + width] = tilt.astype(BF)

    outer_rows = outer_w.shape[6]

    def outer_dot(rows, part):
        size = outer_rows // OUTER_PARTS
        left = jnp.concatenate(
            [active[rows, i * outer_rows + part * size : i * outer_rows + (part + 1) * size] for i in range(H * L * X)],
            axis=1,
        )
        right = jnp.concatenate(
            [
                outer_w[0, g // 2, g % 2, :, :, :, part * size : (part + 1) * size, :].reshape(-1, 128)
                for g in range(groups)
            ],
            axis=1,
        )
        return dot(left, right)

    def outer_part(part):
        for step in range(steps):
            rows = pl.ds(step * STEP_ROWS, STEP_ROWS)
            value = outer_dot(rows, part)
            if part > 0:
                value = value + outer_sum[rows, :]
            outer_sum[rows, :] = value

    def outer_block(block):
        rows = block_rows(block)
        value = outer_dot(rows, OUTER_PARTS - 1) + param(OUTER_BIAS, D)
        if OUTER_PARTS > 1:
            value = value + outer_sum[rows, :]
        hat, factor = normalize(value)
        outer_sum[rows, :] = hat
        upstream = cot_buf[rows, :].astype(F32) * live(block)
        outer_low[rows, :] = normalize_back(upstream * param(GAIN_TWO, D), hat, factor).astype(BF)

    def block_end(block):
        rows = block_rows(block)
        value = resid_low[rows, :].astype(F32) + outer_sum[rows, :] * param(GAIN_TWO, D) + param(SHIFT_TWO, D)
        resid_low[rows, :] = (value * live(block)).astype(BF)

    def put_sums(first, value):
        for i in range(0, value.shape[1], 128):
            row = (first + i) // 128
            grads[0, row : row + 1, :] = value[0:1, i : i + 128]

    def late_sums(_):
        ones = jnp.ones((16, row_count), BF)
        put_sums(OUTER_BIAS, dot(ones, outer_low[...]))
        put_sums(INNER_BIAS, dot(ones, slope[...]))
        put_sums(CONV_BIAS, dot(ones, all_rows(padded_back, None, REACH // 8)))
        for block in range(blocks):
            rows = block_rows(block)
            add_grad(SHIFT_ONE, held[rows, :])
            add_grad(GAIN_TWO, cot_buf[rows, :].astype(F32) * live(block) * outer_sum[rows, :])

    def upstream_sum(block):
        add_grad(SHIFT_TWO, cot_buf[block_rows(block), :].astype(F32) * live(block))

    def outer_grad(piece):
        half, y = piece // Y, piece % Y
        size = outer_rows // 2
        left = jnp.concatenate(
            [active[:, i * outer_rows + half * size : i * outer_rows + (half + 1) * size] for i in range(H * L * X)],
            axis=1,
        )
        value = dot(left, outer_low[:, y * 256 : (y + 1) * 256], OVER_ROWS).astype(BF)
        for c in range(2):
            outer_partial[c, half, y] = value[:, c * 128 : (c + 1) * 128].reshape(H, L, X, size, 128)

    def hidden_piece(piece):
        step, group = piece // groups, piece % groups
        rows, first = pl.ds(step * STEP_ROWS, STEP_ROWS), group * width
        right = jnp.concatenate(
            [outer_w[0, y, c, group // L, group % L].reshape(width, 128) for y in range(Y) for c in range(2)], axis=1
        )
        value = dot(outer_low[rows, :], right, OVER_LANES) * slope[rows, first : first + width].astype(F32)
        slope[rows, first : first + width] = value.astype(BF)

    def inner_grad(piece):
        right = jnp.concatenate(
            [slope[:, g * width + piece * 128 : g * width + (piece + 1) * 128] for g in range(groups)], axis=1
        )
        value = dot(resid_low[...], right, OVER_ROWS).astype(BF)
        for g in range(groups):
            part = value[:, g * 128 : (g + 1) * 128]
            inner_partial[g % 2, piece, g // 2] = part.reshape(H, L, X, -1, 128)

    def resid_block(block):
        rows = block_rows(block)
        value = cot_buf[rows, :].astype(F32) * live(block)
        for g in range(groups):
            right = inner_w[0, g // 2, g % 2].reshape(D, width)
            value = value + dot(slope[rows, g * width : (g + 1) * width], right, OVER_LANES)
        hat = held[rows, :]
        held[rows, :] = value
        add_grad(GAIN_ONE, value * hat)
        back = normalize_back(value * param(GAIN_ONE, D), hat, conv_sum[rows, :])
        conv_sum[rows, :] = back

    conv_rows = conv_w.shape[6]

    def conv_grad(tap):
        left = all_rows(padded, None, REACH // 8)
        right = all_rows(padded_back, padded_by8, KERNEL_TAPS - 1 - tap)
        value = dot(left, right, OVER_ROWS).astype(BF)
        size = conv_rows // 2
        for g in range(groups):
            part = value[:, g * 128 : (g + 1) * 128].reshape(H, L, X, conv_rows, 128)
            for half in range(2):
                conv_partial[g % 2, half * KERNEL_TAPS + tap, g // 2] = part[:, :, :, half * size : (half + 1) * size]

    def token_piece(piece):
        step, part = piece // 3, piece % 3
        rows = pl.ds(step * STEP_ROWS, STEP_ROWS)
        value = held[rows, :]
        for tap in range(part * KERNEL_TAPS // 3, (part + 1) * KERNEL_TAPS // 3):
            value = value + dot(
                step_rows(padded_back, padded_by8, step, KERNEL_TAPS - 1 - tap),
                side_by_side(conv_w, tap),
                OVER_LANES,
            )
        if part == 2:
            value = live_rows(value, step)
        held[rows, :] = value

    def conv_finish(value, first):
        half, tap = first // KERNEL_TAPS, first % KERNEL_TAPS
        size = conv_rows // 2
        conv_out[pl.ds(tap, value.shape[0]), pl.ds(half * size, size), :] = value

    def inner_finish(value, first):
        for i in range(value.shape[0]):
            inner_out[:, (first + i) * 128 : (first + i + 1) * 128] = value[i]

    def outer_finish(value, first):
        size = outer_rows // 2
        outer_out[first * size : first * size + value.shape[0] * size, :] = value.reshape(-1, 128)

    params_sharing = Sharing(share, take, params_sum, params_got, "hlxyc")
    grads_sharing = Sharing(share, take, grads, grads_got, "cxylh")

    moves = {}
    for half in range(2):
        for first, last, axes in CONV_GATHER:
            size = conv_w.shape[6] // 2
            rows = (half * size, (half + 1) * size)
            piece = Gather(k, conv_in, conv_w, own[0], (first, last), rows, axes[half])
            moves["c" + str(first) + "ab"[half]] = piece
        for name, shard, whole, copied, kinds in (
            ("fi", inner_in, inner_w, own[1], INNER_GATHER),
            ("fo", outer_in, outer_w, own[2], OUTER_GATHER),
        ):
            size = whole.shape[6] // (2 * len(kinds))
            for i, axes in enumerate(kinds):
                at = (2 * i + half) * size
                moves[name + str(i) + "ab"[half]] = Gather(k, shard, whole, copied, (0, 1), (at, at + size), axes[half])
    for i, (name, first, last, axes) in enumerate(SCATTER):
        partial, pair, finish = {
            "C": (conv_partial, conv_pair, conv_finish),
            "FI": (inner_partial, inner_pair, inner_finish),
            "FO": (outer_partial, outer_pair, outer_finish),
        }[name.rstrip("0123456789ab")]
        held_at = sum(len(piece[3]) for piece in SCATTER[:i])
        moves[name] = Scatter(
            k, partial, pair, inboxes[held_at : held_at + len(axes)], (first, last), axes, finish
        )
    moves["P"] = params_sharing
    moves["G"] = grads_sharing

    def pad_tokens(_):
        rows_in.wait()
        grads[0] = jnp.zeros((GRAD_ROWS, 128), F32)
        pad(outer_low, padded, padded_by8)

    def pad_back(_):
        pad(conv_sum, padded_back, padded_by8)

    work = {
        "pad": pad_tokens,
        "conv": conv_taps,
        "epi": conv_end,
        "inner": inner_piece,
        "ups": upstream_sum,
        "op": outer_part,
        "outer": outer_block,
        "og": outer_grad,
        "hid": hidden_piece,
        "ig": inner_grad,
        "res": resid_block,
        "padb": pad_back,
        "sums": late_sums,
        "bo": block_end,
        "cg": conv_grad,
        "tok": token_piece,
    }
    out_copies = []
    own_params()
    params_sharing.send()
    pieces = list(moves.values())
    done = dict.fromkeys(KINDS, 0)
    for code in ORDER:
        if code >= len(KINDS):
            pieces[code - len(KINDS)].step()
            continue
        kind = KINDS[code]
        number = done[kind]
        done[kind] += 1
        if kind == "ups" and number == 0:
            cot_in.wait()
        work[kind](CONV_GATHER[number][0] if kind == "conv" else number)
        if kind == "sums":
            grads_sharing.send()
        if kind == "bo" and number == blocks - 1:
            out_copies.append(local(0, resid_low, block_out))
        if kind == "tok" and number % 3 == 2:
            rows = pl.ds(number // 3 * STEP_ROWS, STEP_ROWS)
            out_copies.append(local(5 + number // 3, held.at[rows], grad_tokens.at[rows]))
    params_out[...] = grads[5]
    for copy in out_copies:
        copy.wait()
    k.finish()


def run_kernel(sizes, lengths, small, tokens, cotangent, conv_shard, inner_shard, outer_shard):
    H, L, X, Y = (sizes[axis] for axis in "hlxy")
    taps, conv_rows, lanes = conv_shard.shape
    inner_rows, width = inner_shard.shape
    outer_rows = outer_shard.shape[0]
    rows = tokens.shape[0]
    blocks = rows // BLOCK
    inner_shard, outer_shard = inner_shard[None], outer_shard[None]

    def whole(shard):
        return pltpu.VMEM((shard.shape[0], Y, 2, H, L, X) + shard.shape[1:], BF)

    def pair(count, r):
        return pltpu.VMEM((count, Y, H, L, X, r, 128), BF)

    def partial(count, r):
        return pltpu.VMEM((2, count, Y, H, L, X, r, 128), BF)

    rows_of = {"C": conv_rows // 2, "FI": inner_rows, "FO": outer_rows // 2}
    parts_of = {"C": 2 * taps, "FI": width // 128, "FO": 2}
    inboxes = []
    for name, first, last, axes in SCATTER:
        r = rows_of[name.rstrip("0123456789ab")]
        inboxes += [pltpu.VMEM(shape, BF) for shape in inbox_shapes(sizes, last - first, r, axes)]
    partners = H + L + X + Y - 3
    orders = [piece[2] for piece in CONV_GATHER] + list(INNER_GATHER) + list(OUTER_GATHER)
    copies = sum(1 + sum(3 if axis in TOGETHER else 1 for axis in axes) for order in orders for axes in order)
    copies += sum(1 + len(piece[3]) for piece in SCATTER) + 10
    padded = BLOCK + 2 * REACH
    scratch = [whole(conv_shard), whole(inner_shard), whole(outer_shard)]
    scratch += [pltpu.VMEM((partners, GRAD_ROWS, 128), F32), pltpu.VMEM((6, GRAD_ROWS, 128), F32)]
    scratch += [
        pltpu.VMEM((rows, D), BF),
        pltpu.VMEM((blocks, padded, D), BF),
        pltpu.VMEM((blocks, padded - 16, D), BF),
        pltpu.VMEM((blocks, padded, D), BF),
        pltpu.VMEM((padded, D), F32),
        pltpu.VMEM((rows, D), F32),
        pltpu.VMEM((rows, D), F32),
        pltpu.VMEM((rows, D), F32),
        pltpu.VMEM((rows, D), BF),
        pltpu.VMEM((rows, FF), BF),
        pltpu.VMEM((rows, FF), BF),
        pltpu.VMEM((rows, D), BF),
    ]
    scratch += [partial(parts_of[name], rows_of[name]) for name in ("C", "FI", "FO")]
    scratch += [pair(parts_of[name], rows_of[name]) for name in ("C", "FI", "FO")]
    scratch += [pltpu.VMEM((6, GRAD_ROWS, 128), F32), pltpu.VMEM((partners, GRAD_ROWS, 128), F32)]
    scratch += [pltpu.SMEM(lengths.shape, jnp.int32), pltpu.VMEM(small.shape, BF)]
    scratch += [pltpu.SemaphoreType.DMA((SEND_SLOTS,)), pltpu.SemaphoreType.DMA((copies,)), pltpu.SemaphoreType.DMA((10,))]
    scratch += inboxes
    far = pl.BlockSpec(memory_space=pl.ANY)
    near = pl.BlockSpec(memory_space=pltpu.VMEM)
    return pl.pallas_call(
        functools.partial(kernel, sizes),
        out_shape=[
            jax.ShapeDtypeStruct((rows, D), BF),
            jax.ShapeDtypeStruct((rows, D), F32),
            jax.ShapeDtypeStruct(conv_shard.shape, F32),
            jax.ShapeDtypeStruct(inner_shard.shape[1:], F32),
            jax.ShapeDtypeStruct(outer_shard.shape[1:], F32),
            jax.ShapeDtypeStruct((GRAD_ROWS, 128), F32),
        ],
        in_specs=[far] * 7,
        out_specs=[far, far, near, near, near, near],
        scratch_shapes=scratch,
        compiler_params=pltpu.CompilerParams(
            collective_id=0, has_side_effects=True, vmem_limit_bytes=VMEM_LIMIT
        ),
    )(lengths, small, tokens, cotangent, conv_shard, inner_shard, outer_shard)


def hand_over(parts, grads, *refs):
    count = len(parts)
    sources, targets, small = refs[:count], refs[count : 2 * count], refs[2 * count]
    held, grads_held, sems = refs[2 * count + 1 : 3 * count + 1], refs[-2], refs[-1]
    first = pltpu.make_async_copy(grads, grads_held, sems.at[0, sum(parts)])
    pieces = []
    for source, target, middle, count in zip(sources, targets, held, parts):
        size = source.shape[0] // count
        pieces += [tuple(ref.at[pl.ds(i * size, size)] for ref in (source, middle, target)) for i in range(count)]
    ins = [pltpu.make_async_copy(s, m, sems.at[0, i]) for i, (s, m, _) in enumerate(pieces)]
    outs = [pltpu.make_async_copy(m, t, sems.at[1, i]) for i, (_, m, t) in enumerate(pieces)]
    for copy in ins:
        copy.start()
    first.start()
    for come, go in zip(ins, outs):
        come.wait()
        go.start()
    first.wait()
    size = small.shape[0]
    start = (lax.axis_index("wide") * lax.axis_size("narrow") + lax.axis_index("narrow")) * size
    row = jnp.concatenate([grads_held[pl.ds(start // 128, 1), :], grads_held[pl.ds(start // 128 + 1, 1), :]], axis=1)
    row = pltpu.roll(jnp.broadcast_to(row, (8, 256)), 256 - start % 128, 1)
    small[...] = row[0:1, :size].reshape(size)
    for copy in outs:
        copy.wait()


def settle(share, params_grad, arrays):
    far = pl.BlockSpec(memory_space=pl.ANY)
    near = pl.BlockSpec(memory_space=pltpu.VMEM)
    parts = [max(1, a.size * a.dtype.itemsize >> 20) for a in arrays]
    return pl.pallas_call(
        functools.partial(hand_over, parts),
        out_shape=[jax.ShapeDtypeStruct(a.shape, a.dtype) for a in arrays] + [jax.ShapeDtypeStruct((share,), F32)],
        in_specs=[far] * (len(arrays) + 1),
        out_specs=[far] * len(arrays) + [near],
        scratch_shapes=[pltpu.VMEM(a.shape, a.dtype) for a in arrays]
        + [pltpu.VMEM(params_grad.shape, F32), pltpu.SemaphoreType.DMA((2, sum(parts) + 1))],
        compiler_params=pltpu.CompilerParams(vmem_limit_bytes=VMEM_LIMIT),
    )(params_grad, *arrays)


def fused(
    sizes, tokens, window_lengths, conv_weight, feedforward_input_weight, ffn_out, small_params, cotangent
):
    block_out, grad_tokens, conv_grad, inner_grad, outer_grad, params_grad = run_kernel(
        sizes, window_lengths, small_params, tokens, cotangent, conv_weight, feedforward_input_weight, ffn_out
    )
    return settle(small_params.shape[0], params_grad, [block_out, grad_tokens, conv_grad, inner_grad, outer_grad])


def solution(mesh):
    wide, narrow = mesh.shape["wide"], mesh.shape["narrow"]
    X = max(narrow // 2, 1)
    sizes = {"h": wide // X // 2, "l": 2, "x": X, "y": X}

    def step(*arrays):
        rows = arrays[0].shape[0]
        inner, outer = arrays[3].shape, arrays[4].shape
        whole_lanes = all(a.shape[-1] % 128 == 0 for a in arrays[2:5])
        fits = rows == 3 * STEP_ROWS and narrow == 4 and wide == 8 and inner[1] == X * outer[0] and whole_lanes
        small = arrays[5].shape[0]
        fits = fits and small % 32 == 0 and small <= 160
        if fits:
            return fused(sizes, *arrays)
        return shards(*arrays)

    return jax.shard_map(
        step,
        mesh=mesh,
        in_specs=(
            P(("wide", "narrow"), None),
            P(("wide", "narrow"), None),
            P(None, "wide", "narrow"),
            P("wide", "narrow"),
            P("wide", "narrow"),
            P(("wide", "narrow")),
            P(("wide", "narrow"), None),
        ),
        out_specs=(
            P(("wide", "narrow"), None),
            P(("wide", "narrow"), None),
            P(None, "wide", "narrow"),
            P("wide", "narrow"),
            P("wide", "narrow"),
            P(("wide", "narrow")),
        ),
        check_vma=False,
    )
```
